128 devices in a mesh: seq: 64 (over z_lo, y, x, core), grp: 2 (over z_hi).
Axes of the slice: x: 4, y: 4, z: 4 (z_hi: 2, z_lo: 2; z = z_hi * 2 + z_lo), core: 2. Of those that a mesh axis runs over, the one named last changes fastest.
Arguments:
- inputs: bfloat16 [8192, 2048], P('seq'), may hold values from -16 to 16
- attention_gain: float32 [2048], replicated, may hold values from 0.25 to 1.75
- query_weight: bfloat16 [2048, 2048], P('seq', 'grp'), may hold values from -0.125 to 0.125
- key_matrix: bfloat16 [2048, 1024], P('seq', 'grp'), may hold values from -0.125 to 0.125
- value_matrix: bfloat16 [2048, 1024], P('seq', 'grp'), may hold values from -0.125 to 0.125
- gate_weight: bfloat16 [2048, 16], P('seq', 'grp'), may hold values from -0.125 to 0.125
- query_gain: float32 [128], replicated, may hold values from 0.25 to 1.75
- key_gain: float32 [128], replicated, may hold values from 0.25 to 1.75
- out_weight: bfloat16 [2048, 2048], P('grp', 'seq'), may hold values from -3 to 3
- feed_gain: float32 [2048], replicated, may hold values from 0.25 to 1.75
- feed_gate: bfloat16 [2048, 6144], P('seq', 'grp'), may hold values from -0.125 to 0.125
- feed_up: bfloat16 [2048, 6144], P('seq', 'grp'), may hold values from -0.125 to 0.125
- feed_down: bfloat16 [6144, 2048], P('grp', 'seq'), may hold values from -0.078125 to 0.078125
- cotangent: bfloat16 [8192, 2048], P('seq'), may hold values from -16 to 16
Outputs:
- output: bfloat16 [8192, 2048], P('seq')
- grad_inputs: bfloat16 [8192, 2048], P('seq')
- grad_attention_gain: float32 [2048], P('seq')
- grad_query_weight: float32 [2048, 2048], P('seq', 'grp')
- grad_key_weight: float32 [2048, 1024], P('seq', 'grp')
- grad_value_weight: float32 [2048, 1024], P('seq', 'grp')
- grad_gate_weight: float32 [2048, 16], P('seq', 'grp')
- grad_query_gain: float32 [128], replicated
- grad_key_gain: float32 [128], replicated
- grad_out_weight: float32 [2048, 2048], P('grp', 'seq')
- grad_feed_gain: float32 [2048], P('seq')
- grad_feed_gate: float32 [2048, 6144], P('seq', 'grp')
- grad_feed_up: float32 [2048, 6144], P('seq', 'grp')
- grad_feed_down: float32 [6144, 2048], P('grp', 'seq')
The draws below stay inside these ranges and needn't reach their ends.
All inputs are finite; a program needn't handle non-finite values.
Results may differ from the reference program's by a relative error of at most 0.022.
Values may be sent and summed in bfloat16 or wider, within the bound.
A program may use at most 256 MiB of HBM per device.

```python
import jax
import jax.numpy as jnp
from jax import lax

MODEL_WIDTH = 2048
QUERY_HEAD_COUNT = 16
VALUE_KEY_HEADS = 8
HEAD_WIDTH = 128
FF = 6144
LEN = 8192


def spiked(values, rng, source, target, shards_of, factor):
    owner, partner = [(jnp.arange(values.shape[position]) // (values.shape[position] // shards_of)).reshape([-1 if axis == position else 1 for axis in range(values.ndim)]) for position in (source, target)]
    chosen = jax.random.permutation(rng, shards_of)[partner]
    strong = (owner == chosen) | (owner == (partner + shards_of // 2) % shards_of)
    return jnp.where(strong, factor * values, values)


def level_of(own_key, dims, shards, least, top_value):
    def one(axis_at, parts):
        steps = jax.random.uniform(jax.random.fold_in(jax.random.fold_in(own_key, 6), axis_at), (parts,), jnp.float32, least / len(shards), top_value / len(shards))
        return jnp.repeat(jnp.exp(steps), dims[axis_at] // parts).reshape((-1,) + (1,) * (len(dims) - axis_at - 1))

    gain = one(*shards[0])
    for cut in shards[1:]:
        gain = gain * one(*cut)
    return gain


def bell_draw(key, extent, spread, limit, shards=(), kind=jnp.bfloat16):
    entries = jax.random.normal(key, extent, jnp.float32) * spread
    if len(shards) > 0:
        entries = level_of(key, extent, shards, -0.22, 0.18) * entries
    return jnp.clip(entries, min=-limit, max=limit).astype(kind)


def gaussian_with(rng, extent, spread, reach, split, heavy, kind=jnp.bfloat16):
    drawn = spread * jax.random.normal(rng, extent, jnp.float32)
    if split:
        drawn = drawn * level_of(rng, extent, split, -0.22, 0.18)
    return jnp.clip(spiked(drawn, jax.random.fold_in(rng, 3), *heavy), -reach, reach).astype(kind)


def setup_inputs(seed: int = 0) -> dict:
    streams_of = jax.random.split(jax.random.key(seed), 15)
    inputs = gaussian_with(streams_of[0], (LEN, MODEL_WIDTH), 1.0, 16.0, ((0, 64),), (0, 1, 64, 4.0))
    attention_gain = jnp.clip(1.0 + 0.15 * jax.random.normal(streams_of[1], (MODEL_WIDTH,), jnp.float32), 0.25, 1.75)
    query_weight = bell_draw(streams_of[2], (MODEL_WIDTH, QUERY_HEAD_COUNT * HEAD_WIDTH), MODEL_WIDTH ** -0.5, 0.125, ((0, 64), (1, 2)))
    key_matrix = bell_draw(streams_of[3], (MODEL_WIDTH, VALUE_KEY_HEADS * HEAD_WIDTH), MODEL_WIDTH ** -0.5, 0.125, ((0, 64), (1, 2)))
    value_matrix = bell_draw(streams_of[4], (MODEL_WIDTH, VALUE_KEY_HEADS * HEAD_WIDTH), MODEL_WIDTH ** -0.5, 0.125, ((0, 64), (1, 2)))
    gate_weight = bell_draw(streams_of[5], (MODEL_WIDTH, QUERY_HEAD_COUNT), MODEL_WIDTH ** -0.5, 0.125, ((0, 64), (1, 2)))
    query_gain = jnp.clip(1.0 + 0.15 * jax.random.normal(streams_of[6], (HEAD_WIDTH,), jnp.float32), 0.25, 1.75)
    key_gain = jnp.clip(1.0 + 0.15 * jax.random.normal(streams_of[7], (HEAD_WIDTH,), jnp.float32), 0.25, 1.75)
    out_weight = bell_draw(streams_of[8], (QUERY_HEAD_COUNT * HEAD_WIDTH, MODEL_WIDTH), (max(1, QUERY_HEAD_COUNT * HEAD_WIDTH // 512)) ** -0.5, 3.0, ((0, 2), (1, 64)))
    feed_gain = jnp.clip(1.0 + 0.15 * jax.random.normal(streams_of[9], (MODEL_WIDTH,), jnp.float32), 0.25, 1.75)
    feed_gate = bell_draw(streams_of[10], (MODEL_WIDTH, FF), MODEL_WIDTH ** -0.5, 0.125, ((0, 64), (1, 2)))
    feed_up = bell_draw(streams_of[11], (MODEL_WIDTH, FF), MODEL_WIDTH ** -0.5, 0.125, ((0, 64), (1, 2)))
    feed_down = bell_draw(streams_of[12], (FF, MODEL_WIDTH), FF ** -0.5, 0.078125, ((0, 2), (1, 64)))
    cotangent = gaussian_with(streams_of[13], (LEN, MODEL_WIDTH), 1.0, 16.0, ((0, 64),), (0, 1, 64, 4.0))
    return {"inputs": inputs, "attention_gain": attention_gain, "query_weight": query_weight, "key_matrix": key_matrix, "value_matrix": value_matrix, "gate_weight": gate_weight, "query_gain": query_gain, "key_gain": key_gain, "out_weight": out_weight, "feed_gain": feed_gain, "feed_gate": feed_gate, "feed_up": feed_up, "feed_down": feed_down, "cotangent": cotangent}


EPSILON = 1e-06
ROPE_BASE = 1000000.0
FULL_PRECISION = lax.Precision.HIGHEST

@jax.custom_vjp
def reduced_rows(v):
    return lax.optimization_barrier(v.astype(jnp.bfloat16)).astype(jnp.float32)

@jax.custom_vjp
def reduced_backward(v):
    return v

def low_keep(v):
    return (reduced_rows(v), None)

def low_pass(kept, grad):
    return (grad,)

def back_keep(v):
    return (v, None)

def back_low(kept, grad):
    return (reduced_rows(grad),)
reduced_rows.defvjp(low_keep, low_pass)
reduced_backward.defvjp(back_keep, back_low)

def rms_norm(matrix, norm_gain):
    return matrix * lax.rsqrt(lax.optimization_barrier(jnp.mean(matrix * matrix, axis=-1, keepdims=True)) + EPSILON) * norm_gain

def rotate_half(head_rows, cosine_rows, sine_rows):
    middle = head_rows.shape[-1] // 2
    first_half = head_rows[..., :middle]
    second_half = head_rows[..., middle:]
    return jnp.concatenate([first_half * cosine_rows - second_half * sine_rows, second_half * cosine_rows + first_half * sine_rows], axis=-1)

def rope_tables(positions, head_size):
    middle = head_size // 2
    inverse = ROPE_BASE ** (-(jnp.arange(middle, dtype=jnp.float32) * 2.0) / head_size)
    angles = positions.astype(jnp.float32)[:, None] * inverse[None, :]
    return (jnp.cos(angles)[:, None, :], jnp.sin(angles)[:, None, :])

def head_prepare(projected, norm_gain, cosine_rows, sine_rows):
    return rotate_half(rms_norm(projected, norm_gain), cosine_rows, sine_rows)

def attention(query_matrix, keys_all, values_all):
    sequence_length = query_matrix.shape[0]
    block_length = min(512, sequence_length)
    group_width = QUERY_HEAD_COUNT // VALUE_KEY_HEADS
    scale_factor = HEAD_WIDTH ** (-0.5)
    grouped_rows = query_matrix.reshape(sequence_length // block_length, block_length, VALUE_KEY_HEADS, group_width, HEAD_WIDTH)
    starts = jnp.arange(sequence_length // block_length, dtype=jnp.int32) * block_length
    key_positions = jnp.arange(sequence_length, dtype=jnp.int32)

    @jax.checkpoint
    def one_block(block_pair):
        query_rows, block_start = block_pair
        raw_scores = reduced_backward(jnp.einsum('qgrd,kgd->grqk', query_rows, keys_all, precision=FULL_PRECISION))
        query_positions = block_start + jnp.arange(block_length, dtype=jnp.int32)
        allowed = key_positions[None, :] <= query_positions[:, None]
        scores = jnp.where(allowed, raw_scores * scale_factor, -1e+30)
        softmax_rows = reduced_rows(jax.nn.softmax(scores, axis=-1))
        return jnp.einsum('grqk,kgd->qgrd', softmax_rows, values_all, precision=FULL_PRECISION)
    return lax.map(one_block, (grouped_rows, starts)).reshape(sequence_length, QUERY_HEAD_COUNT, HEAD_WIDTH)

def layer(inputs, attention_gain, query_weight, key_matrix, value_matrix, gate_weight, query_gain, key_gain, out_weight, feed_gain, feed_gate, feed_up, feed_down):
    sequence_length = inputs.shape[0]
    normed_input = reduced_rows(rms_norm(inputs, attention_gain))
    cosine_rows, sine_rows = rope_tables(jnp.arange(sequence_length, dtype=jnp.int32), HEAD_WIDTH)
    query_raw = reduced_backward(jnp.dot(normed_input, query_weight, precision=FULL_PRECISION)).reshape(sequence_length, QUERY_HEAD_COUNT, HEAD_WIDTH)
    unrotated_keys = reduced_backward(jnp.dot(normed_input, key_matrix, precision=FULL_PRECISION)).reshape(sequence_length, VALUE_KEY_HEADS, HEAD_WIDTH)
    value_rows = reduced_rows(reduced_backward(jnp.dot(normed_input, value_matrix, precision=FULL_PRECISION))).reshape(sequence_length, VALUE_KEY_HEADS, HEAD_WIDTH)
    gate_logits = reduced_backward(jnp.dot(normed_input, gate_weight, precision=FULL_PRECISION))
    query_matrix = reduced_rows(head_prepare(query_raw, query_gain, cosine_rows, sine_rows))
    rotated_keys = reduced_rows(head_prepare(unrotated_keys, key_gain, cosine_rows, sine_rows))
    attended = reduced_backward(attention(query_matrix, rotated_keys, value_rows))
    gated_rows = reduced_rows((attended * jax.nn.sigmoid(gate_logits)[:, :, None]).reshape(sequence_length, QUERY_HEAD_COUNT * HEAD_WIDTH))
    hidden = inputs + reduced_backward(jnp.dot(gated_rows, out_weight, precision=FULL_PRECISION))
    normed_mlp = reduced_rows(rms_norm(hidden, feed_gain))
    gate_part = reduced_backward(jnp.dot(normed_mlp, feed_gate, precision=FULL_PRECISION))
    up_part = reduced_backward(jnp.dot(normed_mlp, feed_up, precision=FULL_PRECISION))
    mixed_rows = reduced_rows(jax.nn.silu(gate_part) * up_part)
    return hidden + jnp.dot(mixed_rows, feed_down, precision=FULL_PRECISION)

def reference(inputs, attention_gain, query_weight, key_matrix, value_matrix, gate_weight, query_gain, key_gain, out_weight, feed_gain, feed_gate, feed_up, feed_down, cotangent):
    arrays = [entry.astype(jnp.float32) for entry in (inputs, attention_gain, query_weight, key_matrix, value_matrix, gate_weight, query_gain, key_gain, out_weight, feed_gain, feed_gate, feed_up, feed_down)]
    output, pullback = jax.vjp(layer, *arrays)
    gradients = pullback(cotangent.astype(jnp.float32))
    return (output.astype(jnp.bfloat16), gradients[0].astype(jnp.bfloat16), gradients[1], gradients[2], gradients[3], gradients[4], gradients[5], gradients[6], gradients[7], gradients[8], gradients[9], gradients[10], gradients[11], gradients[12])
```

```python
from types import SimpleNamespace

import jax
import jax.numpy as jnp
from jax import lax
from jax.experimental import pallas as pl
from jax.experimental.pallas import tpu as pltpu
from jax.sharding import PartitionSpec as P

EPSILON = 1e-06
ROPE_BASE = 1000000.0
WIDTH = 2048
HEAD = 128
EIGHTH = 768
ATT = 896
PROJ = 640
SCALE = HEAD**-0.5
LOG2E = 1.4426950408889634
LN2 = 0.6931471805599453
BF, F32 = jnp.bfloat16, jnp.float32
MESH = pl.DeviceIdType.MESH
ALL = slice(None)


def mm(a, b):
    return jnp.dot(a, b, preferred_element_type=F32)


def mm_tb(a, b):
    return lax.dot_general(a, b, (((1,), (1,)), ((), ())), preferred_element_type=F32)


def rms_scale(v):
    return lax.rsqrt(jnp.mean(v * v, axis=-1, keepdims=True) + EPSILON)


def rms_back(v, gain, dy):
    r = rms_scale(v)
    u = gain * dy
    dv = r * (u - v * (r * r * jnp.mean(u * v, axis=-1, keepdims=True)))
    return dv, jnp.sum(dy * v * r, axis=0, keepdims=True)


def rope(v, cos, sin):
    return v * cos + pltpu.roll(v, HEAD // 2, 1) * sin


def rope_back(v, cos, sin):
    return v * cos + pltpu.roll(v * sin, HEAD // 2, 1)


def three_parts(v, lanes):
    hi = v.astype(BF).astype(F32)
    mid = (v - hi).astype(BF).astype(F32)
    low = v - hi - mid
    return jnp.where(
        lanes == 0, hi, jnp.where(lanes == 1, mid, jnp.where(lanes == 2, low, 0.0))
    ).astype(BF)


def select(row_of, shape):
    row = lax.broadcasted_iota(jnp.int32, shape, 0)
    col = lax.broadcasted_iota(jnp.int32, shape, 1)
    return jnp.where(row_of(row, col), 1.0, 0.0).astype(BF)


def body(R):
    s, zh = lax.axis_index("seq"), lax.axis_index("grp")
    c = lax.rem(s, 2)
    x = lax.rem(lax.div(s, 2), 4)
    y = lax.rem(lax.div(s, 8), 4)
    zl = lax.div(s, 32)
    z = zh * 2 + zl
    j = y * 4 + x
    me = zl * 2 + c

    def up(v, k):
        return lax.rem(v + k, 4)

    def dev(zz, yy, xx, cc):
        return (lax.rem(zz, 2) * 32 + yy * 8 + xx * 2 + cc, lax.div(zz, 2))

    sib = dev(z, y, x, 1 - c)
    zs = [up(z, 1), up(z, 3), up(z, 2)]
    zdev = [dev(v, y, x, c) for v in zs]
    part = (zl_dev := (1 - zl) * 32 + y * 8 + x * 2 + c, zh)
    diag = ((1 - zl) * 32 + y * 8 + x * 2 + 1 - c, zh)
    other = (zl_dev, 1 - zh)
    xdev = [dev(z, y, up(x, k), c) for k in (1, 3, 2)]
    ydev = [dev(z, up(y, k), x, c) for k in (1, 3, 2)]

    barrier = pltpu.get_barrier_semaphore()
    greet = [sib, diag] + zdev + xdev + ydev
    for d in greet:
        pl.semaphore_signal(barrier, inc=1, device_id=d, device_id_type=MESH)

    count = [0]

    def ids(k):
        count[0] += k
        return count[0] - k

    class Group:
        def __init__(self, k):
            self.base, self.sent = ids(k), []

        def copy(self, src, dst, d, i):
            i += self.base
            return pltpu.make_async_remote_copy(
                src_ref=src, dst_ref=dst, send_sem=R.send.at[i], recv_sem=R.recv.at[i],
                device_id=d, device_id_type=MESH,
            )

        def go(self, src, dst, d, i):
            cp = self.copy(src, dst, d, i)
            cp.start()
            self.sent.append(cp)

        def got(self, ref, i):
            self.copy(ref, ref, sib, i).wait_recv()

        def end(self):
            for cp in self.sent:
                cp.wait_send()

    def exchange(buf, wl):
        g = Group(3)

        def start():
            buf[zl, y, x, c] = wl[me]
            dst = buf.at[zl, y, x, c]
            g.go(wl.at[zl * 2 + 1 - c], dst, sib, 0)
            g.go(wl.at[(1 - zl) * 2 + c], dst, part, 1)
            g.go(wl.at[(1 - zl) * 2 + 1 - c], dst, diag, 2)

        def wait():
            g.got(buf.at[zl, y, x, 1 - c], 0)
            g.got(buf.at[1 - zl, y, x, c], 1)
            g.got(buf.at[1 - zl, y, x, 1 - c], 2)

        return start, wait, g.end

    def give_back(src, dst):
        g = Group(3)

        def start():
            dst[me] = src[zl, y, x, c]
            g.go(src.at[zl, y, x, 1 - c], dst.at[me], sib, 0)
            g.go(src.at[1 - zl, y, x, c], dst.at[me], part, 1)
            g.go(src.at[1 - zl, y, x, 1 - c], dst.at[me], diag, 2)

        def wait():
            g.got(dst.at[zl * 2 + 1 - c], 0)
            g.got(dst.at[(1 - zl) * 2 + c], 1)
            g.got(dst.at[(1 - zl) * 2 + 1 - c], 2)

        return start, wait, g.end

    a_y = SimpleNamespace(
        full=lambda p: (0, p), half=lambda p, h: (0, p, ALL, h), elem=lambda p, k, h: (0, p, k, h),
        k=4, pos=y, dev=ydev,
    )
    a_x = SimpleNamespace(
        full=lambda p: (0, y, p), half=lambda p, h: (0, y, p, h), elem=lambda p, k, h: (0, y, p, h),
        k=1, pos=x, dev=xdev,
    )
    b_x = SimpleNamespace(
        full=lambda p: (1, ALL, p), half=lambda p, h: (1, ALL, p, h), elem=lambda p, k, h: (1, k, p, h),
        k=4, pos=x, dev=xdev,
    )
    b_y = SimpleNamespace(
        full=lambda p: (1, p, x), half=lambda p, h: (1, p, x, h), elem=lambda p, k, h: (1, p, x, h),
        k=1, pos=y, dev=ydev,
    )

    def gather_ring(buf, a):
        g, p = Group(4), a.pos

        def s1():
            mine = buf.at[a.full(p)]
            g.go(mine, mine, a.dev[0], 0)
            g.go(mine, mine, a.dev[1], 1)

        def s2():
            g.got(buf.at[a.full(up(p, 3))], 0)
            low = buf.at[a.half(up(p, 3), 0)]
            g.go(low, low, a.dev[0], 2)
            g.got(buf.at[a.full(up(p, 1))], 1)
            high = buf.at[a.half(up(p, 1), 1)]
            g.go(high, high, a.dev[1], 3)

        def s3():
            g.got(buf.at[a.half(up(p, 2), 0)], 2)
            g.got(buf.at[a.half(up(p, 2), 1)], 3)

        return s1, s2, s3, g.end

    def gather(buf):
        one = [gather_ring(buf, a_x), gather_ring(buf, b_y)]
        two = [gather_ring(buf, a_y), gather_ring(buf, b_x)]

        def t1():
            for r in one:
                r[0]()

        def t2():
            for r in one:
                r[1]()

        def t3():
            for r, q in zip(one, two):
                r[2]()
                q[0]()

        def t4():
            for r in two:
                r[1]()

        def t5():
            for r in two:
                r[2]()
            for r in one + two:
                r[3]()

        return t1, t2, t3, t4, t5

    def reduce_ring(buf, a, r2, r1, cs):
        g, p, k = Group(4), a.pos, a.k

        def slot(ref, i):
            if k == 1:
                return ref.at[(i, 0) + (ALL,) * (len(ref.shape) - 3) + (cs,)]
            return ref.at[(i,) + (ALL,) * (len(ref.shape) - 2) + (cs,)]

        def loop(fn):
            if k == 1:
                fn(0)
            else:
                pl.loop(0, k)(fn)

        def s1():
            g.go(buf.at[a.half(up(p, 2), 0)], slot(r2, 0), a.dev[0], 0)
            g.go(buf.at[a.half(up(p, 2), 1)], slot(r2, 1), a.dev[1], 1)

        def s2():
            for i, step in ((0, 1), (1, 3)):
                g.got(slot(r2, i), i)
                to = up(p, step)

                def add(q, i=i, to=to):
                    at = a.elem(to, q, i)
                    buf[at] = buf[at] + r2[i, q, :, cs]

                loop(add)
                g.go(buf.at[a.full(to)], slot(r1, i), a.dev[i], 2 + i)

        def s3():
            g.got(slot(r1, 0), 2)
            g.got(slot(r1, 1), 3)

            def add(q):
                for h in (0, 1):
                    at = a.elem(p, q, h)
                    total = (
                        buf[at].astype(F32)
                        + r1[0, q, h, :, cs].astype(F32)
                        + r1[1, q, h, :, cs].astype(F32)
                    )
                    buf[at] = total.astype(BF)

            loop(add)

        return s1, s2, s3, g.end

    def scatter(buf, bufs, cs):
        one = [
            reduce_ring(buf, a_y, bufs[0].at[0], bufs[1].at[0], cs),
            reduce_ring(buf, b_x, bufs[0].at[1], bufs[1].at[1], cs),
        ]
        two = [
            reduce_ring(buf, a_x, bufs[2].at[0], bufs[3].at[0], cs),
            reduce_ring(buf, b_y, bufs[2].at[1], bufs[3].at[1], cs),
        ]

        def t1():
            for r in one:
                r[0]()

        def t2():
            for r in one:
                r[1]()

        def t3():
            for r, q in zip(one, two):
                r[2]()
                q[0]()

        def t4():
            for r in two:
                r[1]()

        def t5():
            for r in two:
                r[2]()
            for r in one + two:
                r[3]()

        return t1, t2, t3, t4, t5

    def reduce_rows(pb, rsib, rz):
        g = Group(5)

        def s0():
            for t in (0, 1):
                g.go(pb.at[t * 2 + 1 - c], rsib.at[t], sib, t)

        def s1():
            for t in (0, 1):
                g.got(rsib.at[t], t)

                def add(h, t=t):
                    pb[t * 2 + c, h] = pb[t * 2 + c, h] + rsib[t, h]

                pl.loop(0, 2)(add)
            for i in range(3):
                zz = zs[i]
                src = pb.at[lax.rem(zz, 2) * 2 + c, lax.div(zz, 2)]
                g.go(src, rz.at[i], zdev[i], 2 + i)

        def s2():
            for i in range(3):
                g.got(rz.at[i], 2 + i)

        def total(rows):
            v = pb[me, zh, rows].astype(F32)
            for i in range(3):
                v = v + rz[i, rows].astype(F32)
            return v

        return s0, s1, s2, g.end, total

    def gather_rows(buf):
        g = Group(7)

        def place(zz, cc):
            return buf.at[lax.rem(zz, 2) * 2 + cc, lax.div(zz, 2)]

        def s0():
            mine = buf.at[me, zh]
            for i in range(3):
                g.go(mine, mine, zdev[i], i)
            g.go(mine, mine, sib, 3)

        came = [zs[1], zs[0], zs[2]]

        def s1():
            for i in range(3):
                at = place(came[i], c)
                g.got(at, i)
                g.go(at, at, sib, 4 + i)

        def s2():
            g.got(place(z, 1 - c), 3)
            for i in range(3):
                g.got(place(came[i], 1 - c), 4 + i)

        return s0, s1, s2, g.end

    def gather_blocks(buf):
        g = Group(5)

        def s0():
            g.go(buf.at[me, 0], buf.at[me, 0], part, 0)
            g.go(buf.at[me, 1], buf.at[me, 1], other, 1)
            g.go(buf.at[me], buf.at[me], sib, 2)

        def s1():
            for h in (0, 1):
                at = buf.at[(1 - zl) * 2 + c, h]
                g.got(at, h)
                g.go(at, at, sib, 3 + h)

        def s2():
            g.got(buf.at[zl * 2 + 1 - c], 2)
            for h in (0, 1):
                g.got(buf.at[(1 - zl) * 2 + 1 - c, h], 3 + h)

        return s0, s1, s2, g.end

    def twin(buf):
        g = Group(1)

        def start():
            g.go(buf.at[zh], buf.at[zh], zdev[2], 0)

        def wait():
            g.got(buf.at[1 - zh], 0)
            g.end()

        return start, wait

    for i in range(4):
        R.wla[i, :, 0:256] = R.qw[:, i * 256 : (i + 1) * 256]
        R.wla[i, :, 256:384] = R.kw[:, i * 128 : (i + 1) * 128]
        R.wla[i, :, 384:512] = R.vw[:, i * 128 : (i + 1) * 128]
        pick = select(lambda r, q, i=i: (r == q + 2 * i) & (q < 2), (8, 128))
        R.wla[i, :, 512:640] = mm(R.gw[...], pick).astype(BF)
        R.wla[i, :, 640:896] = R.ow[:, i * 256 : (i + 1) * 256]
    ex_a = exchange(R.wa, R.wla)
    ag_a = gather(R.wa)
    ex_m = exchange(R.wm, R.wlm)
    ag_m = gather(R.wm)
    ag_x = gather_blocks(R.xn)
    ag_c = gather_blocks(R.cot)
    ag_kv = gather(R.kv)

    pl.semaphore_wait(barrier, len(greet))
    ex_a[0]()

    @pl.loop(0, 4)
    def _(t):
        rows = pl.ds(pl.multiple_of(lax.rem(t, 2) * 32, 32), 32)
        v = R.x[pl.ds(pl.multiple_of(t * 32, 32), 32), :].astype(F32)
        R.xn[me, lax.div(t, 2), rows] = (v * rms_scale(v) * R.ag[...]).astype(BF)

    ag_x[0]()
    for i in range(4):
        R.wlm[i, :, 0:768] = R.fg[:, i * 768 : (i + 1) * 768]
        R.wlm[i, :, 768:1536] = R.fu[:, i * 768 : (i + 1) * 768]
        R.wlm[i, :, 1536:2304] = R.fd[:, i * 768 : (i + 1) * 768]
    R.cot[me] = R.ct[...].reshape(2, 64, WIDTH)
    ex_a[1]()
    ag_a[0]()
    ag_x[1]()
    ag_a[1]()
    ex_m[0]()
    ag_c[0]()
    ag_a[2]()
    ag_x[2]()
    ag_a[3]()
    ag_c[1]()
    ex_m[1]()
    ag_a[4]()
    ag_m[0]()

    @pl.loop(0, 4)
    def _(i):
        zi, ci = lax.div(i, 2), lax.rem(i, 2)
        w = R.wa[:, :, :, :, :, 0:PROJ].reshape(WIDTH, PROJ)
        raw = mm(R.xn[i].reshape(128, WIDTH), w)
        cos, sin = R.cos[i], R.sin[i]
        R.qraw[i] = raw[:, 0:256]
        R.kraw[i] = raw[:, 256:384]
        R.gl[i] = raw[:, 512:640]
        for h in (0, 1):
            v = raw[:, h * 128 : (h + 1) * 128]
            q = rope(v * rms_scale(v) * R.qg[...], cos, sin) * (SCALE * LOG2E)
            R.qx[zi, h, ci, :, 0:128] = q.astype(BF)
        v = raw[:, 256:384]
        k = rope(v * rms_scale(v) * R.kg[...], cos, sin)
        R.kv[zi, y, x, ci, :, 0:128] = k.astype(BF)
        R.kv[zi, y, x, ci, :, 128:256] = raw[:, 384:512].astype(BF)

    ag_kv[0]()
    ag_m[1]()
    ag_kv[1]()
    ag_kv[2]()
    ag_kv[3]()
    ag_kv[4]()
    ag_m[2]()

    ones = jnp.ones((256, 128), BF)
    key_i = lax.broadcasted_iota(jnp.int32, (512, 256), 1)
    row_i = lax.broadcasted_iota(jnp.int32, (512, 256), 0)
    seen = key_i <= lax.rem(row_i, 256)

    def tile(t):
        return (lax.div(t, 16), lax.rem(lax.div(t, 4), 4), lax.rem(t, 4))

    R.oacc[...] = jnp.zeros((2, 512, 256), F32)

    def forward(t, groups, diagonal):
        at = tile(t)
        k = R.kv[at + (ALL, ALL, slice(0, 128))].reshape(256, 128)
        v = R.kv[at + (ALL, ALL, slice(128, 256))].reshape(256, 128)
        v = jnp.concatenate([v, ones], axis=1)
        for g in groups:
            p = jnp.exp2(mm_tb(R.qx[g, :, :, :, 0:128].reshape(512, 128), k))
            if g == diagonal:
                p = jnp.where(seen, p, 0.0)
            R.oacc[g] += mm(p.astype(BF), v)

    @pl.loop(0, j)
    def _(t):
        forward(t, (0, 1), None)

    forward(j, (0, 1), 0)

    @pl.loop(j + 1, j + 16)
    def _(t):
        forward(t, (1,), None)

    forward(j + 16, (1,), 1)
    ag_m[3]()

    lanes = lax.broadcasted_iota(jnp.int32, (128, 128), 1)

    @pl.loop(0, 4)
    def _(i):
        zi, ci = lax.div(i, 2), lax.rem(i, 2)
        for h in (0, 1):
            rows = pl.ds(pl.multiple_of(h * 256 + ci * 128, 128), 128)
            total = R.oacc[zi, rows, 128:256]
            a = R.oacc[zi, rows, 0:128] / total
            R.att[i, :, h * 128 : (h + 1) * 128] = a
            R.qx[zi, h, ci, :, 128:256] = three_parts(-jnp.log2(total), lanes)
            gate = jax.nn.sigmoid(R.gl[i][:, h : h + 1])
            R.gated[i, :, h * 128 : (h + 1) * 128] = (a * gate).astype(BF)

    def spread(n, value):
        cols = pl.ds(pl.multiple_of(n * 256, 256), 256)
        return cols, value.reshape(4, 2, 64, 256).astype(BF)

    @pl.loop(0, 8)
    def _(n):
        w = R.wa[lax.div(n, 4), lax.rem(n, 4), :, :, :, PROJ:ATT].reshape(256, 256)
        cols, v = spread(n, mm_tb(R.gated[...].reshape(512, 256), w))
        R.pb[:, :, :, cols] = v

    rs1 = reduce_rows(R.pb, R.rsib, R.rz)
    ag_n = gather_rows(R.nm)
    rs1[0]()
    rs1[1]()
    rs1[2]()

    def owned(t):
        return pl.ds(pl.multiple_of(t * 16, 16), 16)

    @pl.loop(0, 4)
    def _(t):
        rows = owned(t)
        v = R.x[pl.ds(pl.multiple_of(zh * 64 + t * 16, 16), 16), :].astype(F32)
        v = v + rs1[4](rows)
        R.hid[rows] = v
        R.nm[me, zh, rows] = (v * rms_scale(v) * R.fgain[...]).astype(BF)

    rs1[3]()
    ex_a[2]()
    ex_m[2]()
    ag_n[0]()
    ag_c[2]()
    ag_m[4]()
    ag_n[1]()
    ag_n[2]()

    @pl.loop(0, 3)
    def _(n):
        cols = pl.ds(pl.multiple_of(n * 256, 256), 256)

        def weight(k):
            at = pl.ds(pl.multiple_of(k * 768 + n * 256, 256), 256)
            return R.wm[:, :, :, :, :, at].reshape(WIDTH, 256)

        rows = R.nm[...].reshape(512, WIDTH)
        gate = mm(rows, weight(0))
        upper = mm(rows, weight(1))
        grad = mm(R.cot[...].reshape(512, WIDTH), weight(2))
        sg = jax.nn.sigmoid(gate)
        silu = gate * sg
        R.act[0, :, cols] = (grad * upper * (sg * (1.0 + gate * (1.0 - sg)))).astype(BF)
        R.act[1, :, cols] = (grad * silu).astype(BF)
        R.act[2, :, cols] = (silu * upper).astype(BF)

    @pl.loop(0, 8)
    def _(n):
        at = (lax.div(n, 4), lax.rem(n, 4), ALL, ALL, ALL)
        v = mm_tb(R.act[0], R.wm[at + (slice(0, 768),)].reshape(256, 768))
        v = v + mm_tb(R.act[1], R.wm[at + (slice(768, 1536),)].reshape(256, 768))
        cols, v = spread(n, v)
        R.pb[:, :, :, cols] = v

    rs2 = reduce_rows(R.pb, R.rsib, R.rz)
    rs_f = reduce_rows(R.pb2, R.rsib2, R.rz2)
    rs2[0]()

    @pl.loop(0, 8)
    def _(n):
        at = (lax.div(n, 4), lax.rem(n, 4), ALL, ALL, ALL)
        w = R.wm[at + (slice(1536, 2304),)].reshape(256, 768)
        cols, v = spread(n, mm_tb(R.act[2], w))
        R.pb2[:, :, :, cols] = v

    rs2[1]()
    rs_f[0]()

    @pl.loop(0, 8)
    def _(n):
        at = (lax.div(n, 4), lax.rem(n, 4), ALL, ALL, ALL)
        cols = pl.ds(pl.multiple_of(n * 256, 256), 256)
        t = R.nm[:, :, :, cols].reshape(512, 256).T
        R.wm[at + (slice(0, 768),)] = mm(t, R.act[0]).astype(BF).reshape(4, 2, 32, 768)
        R.wm[at + (slice(768, 1536),)] = mm(t, R.act[1]).astype(BF).reshape(4, 2, 32, 768)
        t = R.cot[:, :, :, cols].reshape(512, 256).T
        R.wm[at + (slice(1536, 2304),)] = mm(t, R.act[2]).astype(BF).reshape(4, 2, 32, 768)

    ag_n[3]()
    for d in [sib] + zdev:
        pl.semaphore_signal(R.free, inc=1, device_id=d, device_id_type=MESH)

    big = (R.m_r2, R.m_r1, R.m_q2, R.m_q1)
    rs_m = scatter(R.wm, big, slice(0, 2304))
    ag_h = gather_rows(R.nm)
    rs_m[0]()
    rs_f[1]()
    rs2[2]()
    R.dgs[...] = jnp.zeros((2, WIDTH), F32)
    ag_c[3]()
    pl.semaphore_wait(R.free, 4)

    @pl.loop(0, 4)
    def _(t):
        rows = owned(t)
        dv, dg = rms_back(R.hid[rows], R.fgain[...], rs2[4](rows))
        dh = dv + R.ct[pl.ds(pl.multiple_of(zh * 64 + t * 16, 16), 16), :].astype(F32)
        R.dgs[1:2, :] += dg
        R.gh[rows] = dh
        R.nm[me, zh, rows] = dh.astype(BF)

    rs2[3]()
    ag_h[0]()
    rs_m[1]()
    ag_h[1]()
    rs_f[2]()
    tw_o = twin(R.ob)

    @pl.loop(0, 4)
    def _(t):
        rows = owned(t)
        R.ob[zh, rows] = (R.hid[rows] + rs_f[4](rows)).astype(BF)

    rs_f[3]()
    tw_o[0]()
    ag_h[2]()

    @pl.loop(0, 4)
    def _(i):
        zi, ci = lax.div(i, 2), lax.rem(i, 2)
        w = R.wa[:, :, :, :, :, PROJ:ATT].reshape(WIDTH, 256)
        grad = mm(R.nm[i].reshape(128, WIDTH), w)
        logits = jnp.zeros((128, 128), F32)
        for h in (0, 1):
            gate = jax.nn.sigmoid(R.gl[i][:, h : h + 1])
            gr = grad[:, h * 128 : (h + 1) * 128]
            a = R.att[i, :, h * 128 : (h + 1) * 128]
            low = (gr * gate).astype(BF)
            dl = jnp.sum(gr * a, axis=1, keepdims=True) * (gate * (1.0 - gate))
            logits = jnp.where(lanes == h, dl, logits)
            delta = jnp.sum(low.astype(F32) * a, axis=1, keepdims=True)
            R.dox[zi, h, ci, :, 0:128] = low
            R.dox[zi, h, ci, :, 128:256] = three_parts(-delta, lanes)
        R.gsc[i, :, 512:640] = logits.astype(BF)

    R.oacc[...] = jnp.zeros((2, 512, 256), F32)
    row_t = lax.broadcasted_iota(jnp.int32, (256, 512), 1)
    key_t = lax.broadcasted_iota(jnp.int32, (256, 512), 0)
    seen_t = key_t <= lax.rem(row_t, 256)

    def backward(t, groups, diagonal):
        at = tile(t)
        k = R.kv[at + (ALL, ALL, slice(0, 128))].reshape(256, 128)
        v = R.kv[at + (ALL, ALL, slice(128, 256))].reshape(256, 128)
        kx = jnp.concatenate([k, ones], axis=1)
        vx = jnp.concatenate([v, ones], axis=1)
        kt = k.T
        dk = dv = None
        for g in groups:
            q, d = R.qx[g].reshape(512, 256), R.dox[g].reshape(512, 256)
            p = jnp.exp2(mm_tb(kx, q))
            if g == diagonal:
                p = jnp.where(seen_t, p, 0.0)
            ds = (p * mm_tb(vx, d)).astype(BF)
            dvg = mm(p.astype(BF), d[:, 0:128])
            dkg = mm(ds, q[:, 0:128])
            dk, dv = (dkg, dvg) if dk is None else (dk + dkg, dv + dvg)
            dq = mm(kt, ds)
            R.oacc[g, 0:128] += dq[:, 0:256]
            R.oacc[g, 128:256] += dq[:, 256:512]
        R.kv[at + (ALL, ALL, slice(0, 128))] = dk.astype(BF).reshape(2, 128, 128)
        R.kv[at + (ALL, ALL, slice(128, 256))] = dv.astype(BF).reshape(2, 128, 128)

    @pl.loop(0, j)
    def _(t):
        backward(t, (0, 1), None)

    backward(j, (0, 1), 0)
    rs_m[2]()

    @pl.loop(j + 1, j + 16)
    def _(t):
        backward(t, (1,), None)

    backward(j + 16, (1,), 1)

    @pl.loop(j + 17, 32)
    def _(t):
        R.kv[tile(t)] = jnp.zeros((2, 128, 256), BF)

    rs_m[3]()
    rs_k = scatter(R.kv, (R.k_r2, R.k_r1, R.k_q2, R.k_q1), slice(0, 256))
    rs_k[0]()
    rs_m[4]()
    rs_k[1]()
    gb_m = give_back(R.wm, R.wlm)
    gb_m[0]()

    R.dgh[...] = jnp.zeros((8, 128), F32)

    @pl.loop(0, 4)
    def _(i):
        zi, ci = lax.div(i, 2), lax.rem(i, 2)
        for h in (0, 1):
            cols = pl.ds(pl.multiple_of(ci * 128, 128), 128)
            dq = R.oacc[zi, h * 128 : (h + 1) * 128, cols].T * SCALE
            dq = rope_back(dq, R.cos[i], R.sin[i])
            dv, dg = rms_back(R.qraw[i, :, h * 128 : (h + 1) * 128], R.qg[...], dq)
            R.dgh[0:1, :] += dg
            R.gsc[i, :, h * 128 : (h + 1) * 128] = dv.astype(BF)

    rs_k[2]()

    @pl.loop(0, 8)
    def _(n):
        at = (lax.div(n, 4), lax.rem(n, 4), ALL, ALL, ALL, slice(PROJ, ATT))
        cols = pl.ds(pl.multiple_of(n * 256, 256), 256)
        t = R.nm[:, :, :, cols].reshape(512, 256).T
        g = mm(t, R.gated[...].reshape(512, 256))
        R.wa[at] = g.astype(BF).reshape(4, 2, 32, 256)

    rs_k[3]()
    rs_k[4]()

    @pl.loop(0, 4)
    def _(i):
        zi, ci = lax.div(i, 2), lax.rem(i, 2)
        dk = R.kv[zi, y, x, ci, :, 0:128].astype(F32) * LN2
        dk = rope_back(dk, R.cos[i], R.sin[i])
        dv, dg = rms_back(R.kraw[i], R.kg[...], dk)
        R.dgh[1:2, :] += dg
        R.gsc[i, :, 256:384] = dv.astype(BF)
        R.gsc[i, :, 384:512] = R.kv[zi, y, x, ci, :, 128:256]

    @pl.loop(0, 8)
    def _(n):
        w = R.wa[lax.div(n, 4), lax.rem(n, 4), :, :, :, 0:PROJ].reshape(256, PROJ)
        cols, v = spread(n, mm_tb(R.gsc[...].reshape(512, PROJ), w))
        R.pb[:, :, :, cols] = v

    rs3 = reduce_rows(R.pb, R.rsib, R.rz)
    rs3[0]()

    @pl.loop(0, 8)
    def _(n):
        at = (lax.div(n, 4), lax.rem(n, 4), ALL, ALL, ALL, slice(0, PROJ))
        cols = pl.ds(pl.multiple_of(n * 256, 256), 256)
        t = R.xn[:, :, :, cols].reshape(512, 256).T
        g = mm(t, R.gsc[...].reshape(512, PROJ))
        R.wa[at] = g.astype(BF).reshape(4, 2, 32, PROJ)

    rs_a = scatter(R.wa, big, slice(0, ATT))
    rs_a[0]()
    rs3[1]()
    rs_a[1]()
    rs3[2]()
    tw_i = twin(R.ib)

    @pl.loop(0, 4)
    def _(t):
        rows = owned(t)
        v = R.x[pl.ds(pl.multiple_of(zh * 64 + t * 16, 16), 16), :].astype(F32)
        dv, dg = rms_back(v, R.ag[...], rs3[4](rows))
        R.dgs[0:1, :] += dg
        R.ib[zh, rows] = (R.gh[rows] + dv).astype(BF)

    tw_i[0]()
    rs3[3]()

    for r in range(16):
        R.sums[0, r : r + 1, :] = R.dgs[0:1, r * 128 : (r + 1) * 128]
        R.sums[0, 16 + r : 17 + r, :] = R.dgs[1:2, r * 128 : (r + 1) * 128]
    R.sums[0, 32:40, :] = R.dgh[...]
    g_z, g_x, g_y, g_c = Group(3), Group(3), Group(3), Group(1)

    def add_up(g, stage, first, devices):
        for i, d in enumerate(devices):
            g.go(R.sums.at[stage], R.came.at[first + i], d, i)

        def finish():
            v = R.sums[stage]
            for i in range(len(devices)):
                g.got(R.came.at[first + i], i)
                v = v + R.came[first + i]
            R.sums[stage + 1] = v
            g.end()

        return finish

    fin = add_up(g_z, 0, 0, zdev)
    rs_a[2]()
    fin()
    fin = add_up(g_x, 1, 3, xdev)
    rs_a[3]()
    fin()
    fin = add_up(g_y, 2, 6, ydev)
    rs_a[4]()
    gb_a = give_back(R.wa, R.wla)
    gb_a[0]()
    fin()
    fin = add_up(g_c, 3, 9, [sib])

    gb_m[1]()
    for i in range(4):
        at = slice(i * 768, (i + 1) * 768)
        R.o_fg[:, at] = R.wlm[i, :, 0:768].astype(F32)
        R.o_fu[:, at] = R.wlm[i, :, 768:1536].astype(F32)
        R.o_fd[:, at] = R.wlm[i, :, 1536:2304].astype(F32)
    tw_o[1]()
    R.o_out[...] = R.ob[...].reshape(128, WIDTH)
    fin()
    R.o_gain[...] = R.sums[4]
    tw_i[1]()
    R.o_in[...] = R.ib[...].reshape(128, WIDTH)
    gb_a[1]()
    gates = jnp.zeros((32, 8), F32)
    for i in range(4):
        R.o_q[:, i * 256 : (i + 1) * 256] = R.wla[i, :, 0:256].astype(F32)
        R.o_k[:, i * 128 : (i + 1) * 128] = R.wla[i, :, 256:384].astype(F32)
        R.o_v[:, i * 128 : (i + 1) * 128] = R.wla[i, :, 384:512].astype(F32)
        R.o_o[:, i * 256 : (i + 1) * 256] = R.wla[i, :, 640:896].astype(F32)
        pick = select(lambda r, q, i=i: (q == r + 2 * i) & (r < 2), (128, 8))
        gates = gates + mm(R.wla[i, :, 512:640], pick)
    R.o_g[...] = gates
    for g in (ag_x, ag_h):
        g[3]()
    gb_m[2]()
    gb_a[2]()
    assert count[0] == COPIES, count


INPUTS = [
    *("x", "ct", "ag", "qg", "kg", "fgain"),
    *("qw", "kw", "vw", "gw", "ow", "fg", "fu", "fd"),
    *("cos", "sin"),
]
OUTPUTS = [
    ("o_out", (128, WIDTH), BF),
    ("o_in", (128, WIDTH), BF),
    ("o_gain", (40, 128), F32),
    ("o_q", (32, 1024), F32),
    ("o_k", (32, 512), F32),
    ("o_v", (32, 512), F32),
    ("o_g", (32, 8), F32),
    ("o_o", (32, 1024), F32),
    ("o_fg", (32, 3072), F32),
    ("o_fu", (32, 3072), F32),
    ("o_fd", (32, 3072), F32),
]
SCRATCH = [
    ("wla", (4, 32, ATT), BF),
    ("wlm", (4, 32, 2304), BF),
    ("wa", (2, 4, 4, 2, 32, ATT), BF),
    ("wm", (2, 4, 4, 2, 32, 2304), BF),
    ("kv", (2, 4, 4, 2, 128, 256), BF),
    ("xn", (4, 2, 64, WIDTH), BF),
    ("cot", (4, 2, 64, WIDTH), BF),
    ("nm", (4, 2, 64, WIDTH), BF),
    ("qraw", (4, 128, 256), F32),
    ("kraw", (4, 128, 128), F32),
    ("gl", (4, 128, 128), F32),
    ("qx", (2, 2, 2, 128, 256), BF),
    ("dox", (2, 2, 2, 128, 256), BF),
    ("oacc", (2, 512, 256), F32),
    ("att", (4, 128, 256), F32),
    ("gated", (4, 128, 256), BF),
    ("gsc", (4, 128, PROJ), BF),
    ("act", (3, 512, 768), BF),
    ("hid", (64, WIDTH), F32),
    ("gh", (64, WIDTH), F32),
    ("dgs", (2, WIDTH), F32),
    ("dgh", (8, 128), F32),
    ("pb", (4, 2, 64, WIDTH), BF),
    ("pb2", (4, 2, 64, WIDTH), BF),
    ("rsib", (2, 2, 64, WIDTH), BF),
    ("rsib2", (2, 2, 64, WIDTH), BF),
    ("rz", (3, 64, WIDTH), BF),
    ("rz2", (3, 64, WIDTH), BF),
    ("m_r2", (2, 2, 4, 32, 2304), BF),
    ("m_r1", (2, 2, 4, 2, 32, 2304), BF),
    ("m_q2", (2, 2, 1, 32, 2304), BF),
    ("m_q1", (2, 2, 1, 2, 32, 2304), BF),
    ("k_r2", (2, 2, 4, 128, 256), BF),
    ("k_r1", (2, 2, 4, 2, 128, 256), BF),
    ("k_q2", (2, 2, 1, 128, 256), BF),
    ("k_q1", (2, 2, 1, 2, 128, 256), BF),
    ("ob", (2, 64, WIDTH), BF),
    ("ib", (2, 64, WIDTH), BF),
    ("sums", (5, 40, 128), F32),
    ("came", (10, 40, 128), F32),
]
COPIES = 164


def kernel(*refs):
    names = INPUTS + [o[0] for o in OUTPUTS] + [v[0] for v in SCRATCH] + ["send", "recv", "free"]
    body(SimpleNamespace(**dict(zip(names, refs))))


def per_device(
    inputs,
    attention_gain,
    query_weight,
    key_matrix,
    value_matrix,
    gate_weight,
    query_gain,
    key_gain,
    out_weight,
    feed_gain,
    feed_gate,
    feed_up,
    feed_down,
    cotangent,
):
    place = lax.axis_index("seq")
    run = lax.rem(lax.div(place, 2), 16)
    half = jnp.arange(4, dtype=jnp.int32)[:, None]
    row = jnp.arange(128, dtype=jnp.int32)[None, :]
    positions = (half // 2) * 4096 + run * 256 + (half % 2) * 128 + row
    inverse = ROPE_BASE ** (-(jnp.arange(HEAD // 2, dtype=F32) * 2.0) / HEAD)
    angles = positions.astype(F32)[:, :, None] * inverse
    cos, sin = jnp.cos(angles), jnp.sin(angles)
    cos = jnp.concatenate([cos, cos], axis=-1)
    sin = jnp.concatenate([-sin, sin], axis=-1)
    vmem = pl.BlockSpec(memory_space=pltpu.VMEM)
    out = pl.pallas_call(
        kernel,
        out_shape=[jax.ShapeDtypeStruct(shape, kind) for _, shape, kind in OUTPUTS],
        in_specs=[vmem] * len(INPUTS),
        out_specs=[vmem] * len(OUTPUTS),
        scratch_shapes=[pltpu.VMEM(shape, kind) for _, shape, kind in SCRATCH]
        + [pltpu.SemaphoreType.DMA((COPIES,)), pltpu.SemaphoreType.DMA((COPIES,))]
        + [pltpu.SemaphoreType.REGULAR],
        compiler_params=pltpu.CompilerParams(
            collective_id=0, has_side_effects=True, vmem_limit_bytes=63 * 2**20
        ),
        name="block",
    )(
        inputs,
        cotangent,
        attention_gain.reshape(1, WIDTH),
        query_gain.reshape(1, HEAD),
        key_gain.reshape(1, HEAD),
        feed_gain.reshape(1, WIDTH),
        query_weight,
        key_matrix,
        value_matrix,
        gate_weight,
        out_weight.T,
        feed_gate,
        feed_up,
        feed_down.T,
        cos,
        sin,
    )
    output, grad_inputs, gains, gq, gk, gv, gg, go, gfg, gfu, gfd = out
    own = lax.dynamic_slice_in_dim(gains[:32].reshape(2, WIDTH), place * 32, 32, 1)
    return (
        output,
        grad_inputs,
        own[0],
        gq,
        gk,
        gv,
        gg,
        gains[32],
        gains[33],
        go.T,
        own[1],
        gfg,
        gfu,
        gfd.T,
    )


def solution(mesh):
    seq, both, turned = P("seq", None), P("seq", "grp"), P("grp", "seq")
    in_specs = (seq, P(), both, both, both, both, P(), P(), turned, P(), both, both, turned, seq)
    out_specs = (
        seq, seq, P("seq"), both, both, both, both, P(), P(), turned, P("seq"), both, both, turned,
    )
    return jax.shard_map(
        per_device, mesh=mesh, in_specs=in_specs, out_specs=out_specs, check_vma=False
    )
```

```python
from types import SimpleNamespace

import jax
import jax.numpy as jnp
from jax import lax
from jax.experimental import pallas as pl
from jax.experimental.pallas import tpu as pltpu
from jax.sharding import PartitionSpec as P

EPSILON = 1e-06
ROPE_BASE = 1000000.0
WIDTH = 2048
HEAD = 128
EIGHTH = 768
ATT = 896
PROJ = 640
SCALE = HEAD**-0.5
LOG2E = 1.4426950408889634
LN2 = 0.6931471805599453
BF, F32 = jnp.bfloat16, jnp.float32
MESH = pl.DeviceIdType.MESH
ALL = slice(None)


def mm(a, b):
    return jnp.dot(a, b, preferred_element_type=F32)


def mm_tb(a, b):
    return lax.dot_general(a, b, (((1,), (1,)), ((), ())), preferred_element_type=F32)


def rms_scale(v):
    return lax.rsqrt(jnp.mean(v * v, axis=-1, keepdims=True) + EPSILON)


def rms_back(v, gain, dy):
    r = rms_scale(v)
    u = gain * dy
    dv = r * (u - v * (r * r * jnp.mean(u * v, axis=-1, keepdims=True)))
    return dv, jnp.sum(dy * v * r, axis=0, keepdims=True)


def rope(v, cos, sin):
    return v * cos + pltpu.roll(v, HEAD // 2, 1) * sin


def rope_back(v, cos, sin):
    return v * cos + pltpu.roll(v * sin, HEAD // 2, 1)


def three_parts(v, lanes):
    hi = v.astype(BF).astype(F32)
    mid = (v - hi).astype(BF).astype(F32)
    low = v - hi - mid
    return jnp.where(
        lanes == 0, hi, jnp.where(lanes == 1, mid, jnp.where(lanes == 2, low, 0.0))
    ).astype(BF)


def select(row_of, shape):
    row = lax.broadcasted_iota(jnp.int32, shape, 0)
    col = lax.broadcasted_iota(jnp.int32, shape, 1)
    return jnp.where(row_of(row, col), 1.0, 0.0).astype(BF)


def body(R):
    s, zh = lax.axis_index("seq"), lax.axis_index("grp")
    c = lax.rem(s, 2)
    x = lax.rem(lax.div(s, 2), 4)
    y = lax.rem(lax.div(s, 8), 4)
    zl = lax.div(s, 32)
    z = zh * 2 + zl
    j = y * 4 + x
    me = zl * 2 + c

    def up(v, k):
        return lax.rem(v + k, 4)

    def dev(zz, yy, xx, cc):
        return (lax.rem(zz, 2) * 32 + yy * 8 + xx * 2 + cc, lax.div(zz, 2))

    sib = dev(z, y, x, 1 - c)
    zs = [up(z, 1), up(z, 3), up(z, 2)]
    zdev = [dev(v, y, x, c) for v in zs]
    part = (zl_dev := (1 - zl) * 32 + y * 8 + x * 2 + c, zh)
    diag = ((1 - zl) * 32 + y * 8 + x * 2 + 1 - c, zh)
    other = (zl_dev, 1 - zh)
    xdev = [dev(z, y, up(x, k), c) for k in (1, 3, 2)]
    ydev = [dev(z, up(y, k), x, c) for k in (1, 3, 2)]

    barrier = pltpu.get_barrier_semaphore()
    zsib = [dev(v, y, x, 1 - c) for v in zs]
    greet = [sib] + zdev + zsib + xdev + ydev
    for d in greet:
        pl.semaphore_signal(barrier, inc=1, device_id=d, device_id_type=MESH)

    count = [0]

    def ids(k):
        count[0] += k
        return count[0] - k

    class Group:
        def __init__(self, k):
            self.base, self.sent = ids(k), []

        def copy(self, src, dst, d, i):
            i += self.base
            return pltpu.make_async_remote_copy(
                src_ref=src, dst_ref=dst, send_sem=R.send.at[i], recv_sem=R.recv.at[i],
                device_id=d, device_id_type=MESH,
            )

        def go(self, src, dst, d, i):
            cp = self.copy(src, dst, d, i)
            cp.start()
            self.sent.append(cp)

        def got(self, ref, i):
            self.copy(ref, ref, sib, i).wait_recv()

        def end(self):
            for cp in self.sent:
                cp.wait_send()

    def exchange(buf, wl):
        g = Group(3)

        def start():
            buf[zl, y, x, c] = wl[me]
            dst = buf.at[zl, y, x, c]
            g.go(wl.at[zl * 2 + 1 - c], dst, sib, 0)
            g.go(wl.at[(1 - zl) * 2 + c], dst, part, 1)
            g.go(wl.at[(1 - zl) * 2 + 1 - c], dst, diag, 2)

        def wait():
            g.got(buf.at[zl, y, x, 1 - c], 0)
            g.got(buf.at[1 - zl, y, x, c], 1)
            g.got(buf.at[1 - zl, y, x, 1 - c], 2)

        return start, wait, g.end

    def give_back(src, dst):
        g = Group(3)

        def start():
            dst[me] = src[zl, y, x, c]
            g.go(src.at[zl, y, x, 1 - c], dst.at[me], sib, 0)
            g.go(src.at[1 - zl, y, x, c], dst.at[me], part, 1)
            g.go(src.at[1 - zl, y, x, 1 - c], dst.at[me], diag, 2)

        def wait():
            g.got(dst.at[zl * 2 + 1 - c], 0)
            g.got(dst.at[(1 - zl) * 2 + c], 1)
            g.got(dst.at[(1 - zl) * 2 + 1 - c], 2)

        return start, wait, g.end

    a_y = SimpleNamespace(
        full=lambda p: (0, p), half=lambda p, h: (0, p, ALL, h), elem=lambda p, k, h: (0, p, k, h),
        k=4, pos=y, dev=ydev,
    )
    a_x = SimpleNamespace(
        full=lambda p: (0, y, p), half=lambda p, h: (0, y, p, h), elem=lambda p, k, h: (0, y, p, h),
        k=1, pos=x, dev=xdev,
    )
    b_x = SimpleNamespace(
        full=lambda p: (1, ALL, p), half=lambda p, h: (1, ALL, p, h), elem=lambda p, k, h: (1, k, p, h),
        k=4, pos=x, dev=xdev,
    )
    b_y = SimpleNamespace(
        full=lambda p: (1, p, x), half=lambda p, h: (1, p, x, h), elem=lambda p, k, h: (1, p, x, h),
        k=1, pos=y, dev=ydev,
    )

    def gather_ring(buf, a):
        g, p = Group(6), a.pos
        left, right, across = up(p, 3), up(p, 1), up(p, 2)

        def half(q, h):
            return buf.at[a.half(q, h)]

        def s1():
            for i, (h, d) in enumerate(((0, 0), (1, 1), (1, 0), (0, 1))):
                g.go(half(p, h), half(p, h), a.dev[d], i)

        def s2():
            g.got(half(left, 0), 0)
            g.go(half(left, 0), half(left, 0), a.dev[0], 4)
            g.got(half(right, 1), 1)
            g.go(half(right, 1), half(right, 1), a.dev[1], 5)

        def s3():
            g.got(half(left, 1), 2)
            g.got(half(right, 0), 3)

        def s4():
            g.got(half(across, 0), 4)
            g.got(half(across, 1), 5)

        return s1, s2, s3, s4, g.end

    def gather(buf):
        one = [gather_ring(buf, a_x), gather_ring(buf, b_y)]
        two = [gather_ring(buf, a_y), gather_ring(buf, b_x)]

        def t1():
            for r in one:
                r[0]()

        def t2():
            for r in one:
                r[1]()

        def t3():
            for r, q in zip(one, two):
                r[2]()
                r[3]()
                q[0]()

        def t4():
            for r in two:
                r[1]()

        def t5():
            for r in two:
                r[2]()

        def t6():
            for r in two:
                r[3]()
            for r in one + two:
                r[4]()

        return t1, t2, t3, t4, t5, t6

    def reduce_ring(buf, a, r2, r1, cs, bs):
        g, p, k = Group(6), a.pos, a.k
        first = ALL if k == 4 else 0

        def half(q, h):
            at = a.half(q, h)
            return buf.at[at + (ALL,) * (5 - len(at)) + (cs,)]

        def elem(q, n, h):
            return a.elem(q, n, h) + (ALL, cs)

        def far(i):
            return r2.at[i, first, :, bs]

        def near(i, h):
            return r1.at[i, first, h, :, bs]

        def loop(fn):
            if k == 1:
                fn(0)
            else:
                pl.loop(0, k)(fn)

        def s1():
            for i in (0, 1):
                g.go(half(up(p, 2), i), far(i), a.dev[i], i)

        def direct(i):
            g.go(half(up(p, 1 + 2 * i), 1 - i), near(i, 1 - i), a.dev[i], 2 + i)

        def s2(i):
            g.got(far(i), i)
            to = up(p, 1 + 2 * i)

            def add(n):
                at = elem(to, n, i)
                buf[at] = buf[at] + r2[i, n, :, bs]

            loop(add)
            g.go(half(to, i), near(i, i), a.dev[i], 4 + i)

        def s3():
            for i in (0, 1):
                g.got(near(i, 1 - i), 2 + i)
                g.got(near(i, i), 4 + i)

            def add(n):
                for h in (0, 1):
                    at = elem(p, n, h)
                    total = (
                        buf[at].astype(F32)
                        + r1[0, n, h, :, bs].astype(F32)
                        + r1[1, n, h, :, bs].astype(F32)
                    )
                    buf[at] = total.astype(BF)

            loop(add)

        return s1, direct, s2, s3, g.end

    def scatter(buf, bufs, cs, bs=None):
        bs = cs if bs is None else bs
        one = [
            reduce_ring(buf, a_y, bufs[0].at[0], bufs[1].at[0], cs, bs),
            reduce_ring(buf, b_x, bufs[0].at[1], bufs[1].at[1], cs, bs),
        ]
        two = [
            reduce_ring(buf, a_x, bufs[2].at[0], bufs[3].at[0], cs, bs),
            reduce_ring(buf, b_y, bufs[2].at[1], bufs[3].at[1], cs, bs),
        ]

        def t0():
            for r in one:
                r[0]()

        def t1(i):
            for r in one:
                r[1](i)

        def t2(i):
            for r in one:
                r[2](i)

        def t3():
            for r, q in zip(one, two):
                r[3]()
                q[0]()
                q[1](0)
                q[1](1)

        def t4():
            for i in (0, 1):
                for r in two:
                    r[2](i)

        def t5():
            for r in two:
                r[3]()
            for r in one + two:
                r[4]()

        def start():
            t0()
            t1(0)
            t1(1)

        def onward():
            t2(0)
            t2(1)

        return SimpleNamespace(t0=t0, t1=t1, t2=t2, t3=t3, t4=t4, t5=t5, start=start, onward=onward)

    def place(zz, cc):
        return (lax.rem(zz, 2) * 2 + cc, lax.div(zz, 2))

    half_rows = (slice(0, 32), slice(32, 64))

    def reduce_rows(pb, rsib, rz):
        g = Group(8)

        def mine(zz, h):
            return pb.at[place(zz, c) + (half_rows[h],)]

        def s0():
            for t in (0, 1):
                g.go(pb.at[t * 2 + 1 - c], rsib.at[t], sib, t)

        def s1():
            g.got(rsib.at[0], 0)
            g.got(rsib.at[1], 1)

            def add(zz):
                at = place(zz, c)
                pb[at] = pb[at] + rsib[lax.rem(zz, 2), lax.div(zz, 2)]

            add(zs[2])
            for i in (0, 1):
                g.go(mine(zs[2], i), rz.at[2, half_rows[i]], zdev[i], 2 + i)
            for i in (0, 1):
                add(zs[i])
                g.go(mine(zs[i], 1 - i), rz.at[i, half_rows[1 - i]], zdev[i], 4 + i)
            add(z)

        def s2():
            for i in (0, 1):
                rows = half_rows[i]
                g.got(rz.at[2, rows], 2 + i)
                at = place(zs[i], c) + (rows,)
                pb[at] = pb[at] + rz[2, rows]
                g.go(mine(zs[i], i), rz.at[i, rows], zdev[i], 6 + i)

        def s3():
            for i in (0, 1):
                g.got(rz.at[i, half_rows[1 - i]], 4 + i)
                g.got(rz.at[i, half_rows[i]], 6 + i)

        def total(rows):
            v = pb[me, zh, rows].astype(F32)
            return v + rz[0, rows].astype(F32) + rz[1, rows].astype(F32)

        return SimpleNamespace(s0=s0, s1=s1, s2=s2, s3=s3, end=g.end, total=total)

    def gather_rows(buf):
        g = Group(10)

        def at(zz, h):
            return buf.at[place(zz, c) + (half_rows[h],)]

        def s0():
            for i, (h, d) in enumerate(((0, 0), (1, 1), (1, 0), (0, 1))):
                g.go(at(z, h), at(z, h), zdev[d], i)
            own = buf.at[place(z, c)]
            g.go(own, own, sib, 6)

        def s1():
            g.got(at(zs[1], 0), 0)
            g.go(at(zs[1], 0), at(zs[1], 0), zdev[0], 4)
            g.got(at(zs[0], 1), 1)
            g.go(at(zs[0], 1), at(zs[0], 1), zdev[1], 5)

        def s2():
            def hand_on(zz, i):
                whole = buf.at[place(zz, c)]
                g.go(whole, whole, sib, i)

            g.got(at(zs[1], 1), 2)
            hand_on(zs[1], 7)
            g.got(at(zs[0], 0), 3)
            hand_on(zs[0], 8)
            g.got(at(zs[2], 0), 4)
            g.got(at(zs[2], 1), 5)
            hand_on(zs[2], 9)

        def s3():
            for i, zz in ((6, z), (7, zs[1]), (8, zs[0]), (9, zs[2])):
                g.got(buf.at[place(zz, 1 - c)], i)

        return SimpleNamespace(s0=s0, s1=s1, s2=s2, s3=s3, end=g.end)

    def gather_blocks(buf):
        g = Group(5)

        def s0():
            g.go(buf.at[me, 0], buf.at[me, 0], part, 0)
            g.go(buf.at[me, 1], buf.at[me, 1], other, 1)
            g.go(buf.at[me], buf.at[me], sib, 2)

        def s1():
            for h in (0, 1):
                at = buf.at[(1 - zl) * 2 + c, h]
                g.got(at, h)
                g.go(at, at, sib, 3 + h)

        def s2():
            g.got(buf.at[zl * 2 + 1 - c], 2)
            for h in (0, 1):
                g.got(buf.at[(1 - zl) * 2 + 1 - c, h], 3 + h)

        return s0, s1, s2, g.end

    def twin(buf):
        g = Group(1)

        def start():
            g.go(buf.at[zh], buf.at[zh], zdev[2], 0)

        def wait():
            g.got(buf.at[1 - zh], 0)
            g.end()

        return start, wait

    for i in range(4):
        R.wla[i, :, 0:256] = R.qw[:, i * 256 : (i + 1) * 256]
        R.wla[i, :, 256:384] = R.kw[:, i * 128 : (i + 1) * 128]
        R.wla[i, :, 384:512] = R.vw[:, i * 128 : (i + 1) * 128]
        pick = select(lambda r, q, i=i: (r == q + 2 * i) & (q < 2), (8, 128))
        R.wla[i, :, 512:640] = mm(R.gw[...], pick).astype(BF)
    ex_a, ex_o, ex_m = exchange(R.wa, R.wla), exchange(R.wo, R.wlo), exchange(R.wm, R.wlm)
    ag_a, ag_o, ag_m = gather(R.wa), gather(R.wo), gather(R.wm)
    ag_x = gather_blocks(R.xn)
    ag_c = gather_blocks(R.cot)
    ag_kv = gather(R.kv)

    pl.semaphore_wait(barrier, len(greet))
    ex_a[0]()

    @pl.loop(0, 4)
    def _(t):
        rows = pl.ds(pl.multiple_of(lax.rem(t, 2) * 32, 32), 32)
        v = R.x[pl.ds(pl.multiple_of(t * 32, 32), 32), :].astype(F32)
        R.xn[me, lax.div(t, 2), rows] = (v * rms_scale(v) * R.ag[...]).astype(BF)

    ag_x[0]()
    for i in range(4):
        R.wlo[i] = R.ow[:, i * 256 : (i + 1) * 256]
        R.wlm[i, :, 0:768] = R.fg[:, i * 768 : (i + 1) * 768]
        R.wlm[i, :, 768:1536] = R.fu[:, i * 768 : (i + 1) * 768]
        R.wlm[i, :, 1536:2304] = R.fd[:, i * 768 : (i + 1) * 768]
    R.cot[me] = R.ct[...].reshape(2, 64, WIDTH)
    ex_a[1]()
    ag_a[0]()
    ag_a[1]()
    ag_x[1]()
    ag_a[2]()
    ex_o[0]()
    ex_m[0]()
    ag_x[2]()
    ag_a[3]()
    ex_o[1]()
    ag_o[0]()
    ag_a[4]()
    ex_m[1]()
    ag_m[0]()
    ag_a[5]()

    @pl.loop(0, 4)
    def _(i):
        zi, ci = lax.div(i, 2), lax.rem(i, 2)
        w = R.wa[...].reshape(WIDTH, PROJ)
        raw = mm(R.xn[i].reshape(128, WIDTH), w)
        cos, sin = R.cos[i], R.sin[i]
        R.qraw[i] = raw[:, 0:256]
        R.kraw[i] = raw[:, 256:384]
        R.gl[i] = raw[:, 512:640]
        for h in (0, 1):
            v = raw[:, h * 128 : (h + 1) * 128]
            q = rope(v * rms_scale(v) * R.qg[...], cos, sin) * (SCALE * LOG2E)
            R.qx[zi, h, ci, :, 0:128] = q.astype(BF)
        v = raw[:, 256:384]
        k = rope(v * rms_scale(v) * R.kg[...], cos, sin)
        R.kv[zi, y, x, ci, :, 0:128] = k.astype(BF)
        R.kv[zi, y, x, ci, :, 128:256] = raw[:, 384:512].astype(BF)

    ag_kv[0]()
    ag_c[0]()

    ones = jnp.ones((256, 128), BF)
    key_i = lax.broadcasted_iota(jnp.int32, (512, 256), 1)
    row_i = lax.broadcasted_iota(jnp.int32, (512, 256), 0)
    seen = key_i <= lax.rem(row_i, 256)
    R.oacc[...] = jnp.zeros((2, 512, 256), F32)

    def forward(at, groups, diagonal):
        k = R.kv[at + (ALL, ALL, slice(0, 128))].reshape(256, 128)
        v = R.kv[at + (ALL, ALL, slice(128, 256))].reshape(256, 128)
        v = jnp.concatenate([v, ones], axis=1)
        for g in groups:
            p = jnp.exp2(mm_tb(R.qx[g, :, :, :, 0:128].reshape(512, 128), k))
            if g == diagonal:
                p = jnp.where(seen, p, 0.0)
            R.oacc[g] += mm(p.astype(BF), v)

    def tile_pair(fn, empty, at0, at1):
        t0, t1 = at0[0] * 4 + at0[1], at1[0] * 4 + at1[1]

        @pl.when(t0 < j)
        def _():
            fn((0,) + at0, (0, 1), None)

        @pl.when(t0 > j)
        def _():
            fn((0,) + at0, (1,), None)

        @pl.when(t1 < j)
        def _():
            fn((1,) + at1, (1,), None)

        if empty is not None:

            @pl.when(t1 > j)
            def _():
                empty((1,) + at1)

    def near(fn, empty=None):
        @pl.loop(1, 4)
        def _(k):
            tile_pair(fn, empty, (y, up(x, k)), (up(y, k), x))

    def side(fn, a, empty=None):
        @pl.loop(0, 4)
        def _(k):
            tile_pair(fn, empty, (up(y, a), k), (k, up(x, a)))

    ag_o[1]()
    forward((0, y, x), (0, 1), 0)
    forward((1, y, x), (1,), 1)
    ag_kv[1]()
    ag_m[1]()
    ag_kv[2]()
    ag_o[2]()
    near(forward)
    ag_c[1]()
    ag_kv[3]()
    ag_o[3]()
    ag_kv[4]()
    ag_m[2]()
    @pl.loop(0, 2)
    def _(k):
        side(forward, 1 + 2 * k)

    ag_kv[5]()
    side(forward, 2)
    ag_o[4]()
    ag_o[5]()

    lanes = lax.broadcasted_iota(jnp.int32, (128, 128), 1)

    @pl.loop(0, 4)
    def _(i):
        zi, ci = lax.div(i, 2), lax.rem(i, 2)
        for h in (0, 1):
            rows = pl.ds(pl.multiple_of(h * 256 + ci * 128, 128), 128)
            total = R.oacc[zi, rows, 128:256]
            a = R.oacc[zi, rows, 0:128] / total
            R.att[i, :, h * 128 : (h + 1) * 128] = a
            R.qx[zi, h, ci, :, 128:256] = three_parts(-jnp.log2(total), lanes)
            gate = jax.nn.sigmoid(R.gl[i][:, h : h + 1])
            R.gated[i, :, h * 128 : (h + 1) * 128] = (a * gate).astype(BF)

    def spread(n, value):
        cols = pl.ds(pl.multiple_of(n * 256, 256), 256)
        return cols, value.reshape(4, 2, 64, 256).astype(BF)

    rs1 = reduce_rows(R.pb, R.rsib, R.rz)
    ag_n = gather_rows(R.nm)

    def project(cc):
        rows = jnp.concatenate([R.gated[cc], R.gated[2 + cc]], axis=0)

        @pl.loop(0, 8)
        def _(n):
            w = R.wo[lax.div(n, 4), lax.rem(n, 4)].reshape(256, 256)
            cols = pl.ds(pl.multiple_of(n * 256, 256), 256)
            v = mm_tb(rows, w).astype(BF).reshape(2, 2, 64, 256)
            R.pb[cc, :, :, cols] = v[0]
            R.pb[2 + cc, :, :, cols] = v[1]

    project(1 - c)
    rs1.s0()
    project(c)
    rs1.s1()
    rs1.s2()
    ag_m[3]()
    rs1.s3()

    def owned(t):
        return pl.ds(pl.multiple_of(t * 16, 16), 16)

    @pl.loop(0, 4)
    def _(t):
        rows = owned(t)
        v = R.x[pl.ds(pl.multiple_of(zh * 64 + t * 16, 16), 16), :].astype(F32)
        v = v + rs1.total(rows)
        R.hid[rows] = v
        R.nm[me, zh, rows] = (v * rms_scale(v) * R.fgain[...]).astype(BF)

    rs1.end()
    for g in (ex_a, ex_o, ex_m):
        g[2]()
    ag_n.s0()
    ag_c[2]()
    ag_n.s1()
    ag_n.s2()
    ag_m[4]()
    ag_m[5]()
    ag_n.s3()

    @pl.loop(0, 3)
    def _(n):
        cols = pl.ds(pl.multiple_of(n * 256, 256), 256)

        def weight(k):
            at = pl.ds(pl.multiple_of(k * 768 + n * 256, 256), 256)
            return R.wm[:, :, :, :, :, at].reshape(WIDTH, 256)

        rows = R.nm[...].reshape(512, WIDTH)
        gate = mm(rows, weight(0))
        upper = mm(rows, weight(1))
        grad = mm(R.cot[...].reshape(512, WIDTH), weight(2))
        sg = jax.nn.sigmoid(gate)
        silu = gate * sg
        R.act[0, :, cols] = (grad * upper * (sg * (1.0 + gate * (1.0 - sg)))).astype(BF)
        R.act[1, :, cols] = (grad * silu).astype(BF)
        R.act[2, :, cols] = (silu * upper).astype(BF)

    def block(n):
        return (lax.div(n, 4), lax.rem(n, 4), ALL, ALL, ALL)

    def turned(ref, n):
        cols = pl.ds(pl.multiple_of(n * 256, 256), 256)
        return ref[:, :, :, cols].reshape(512, 256).T

    big = (R.m_r2, R.m_r1, R.m_q2, R.m_q1)
    rs_d = scatter(R.ga, big, slice(0, 768))
    rs_m = scatter(R.wm, big, slice(0, 1536), slice(768, 2304))

    @pl.loop(0, 8)
    def _(n):
        g = mm(turned(R.cot, n), R.act[2])
        R.ga[block(n) + (slice(0, 768),)] = g.astype(BF).reshape(4, 2, 32, 768)

    rs_d.start()

    @pl.loop(0, 8)
    def _(n):
        at = block(n)
        v = mm_tb(R.act[0], R.wm[at + (slice(0, 768),)].reshape(256, 768))
        v = v + mm_tb(R.act[1], R.wm[at + (slice(768, 1536),)].reshape(256, 768))
        cols, v = spread(n, v)
        R.pb[:, :, :, cols] = v

    rs2 = reduce_rows(R.pb, R.rsib, R.rz)
    rs_f = reduce_rows(R.pb2, R.rsib, R.rz)
    rs2.s0()

    def feed_weights(n):
        at = block(n)
        t = turned(R.nm, n)
        R.wm[at + (slice(0, 768),)] = mm(t, R.act[0]).astype(BF).reshape(4, 2, 32, 768)
        R.wm[at + (slice(768, 1536),)] = mm(t, R.act[1]).astype(BF).reshape(4, 2, 32, 768)

    pl.loop(0, 4)(feed_weights)
    rs2.s1()
    rs_d.onward()
    pl.loop(4, 8)(feed_weights)
    rs2.s2()

    def tell(devices, sem):
        for d in devices:
            pl.semaphore_signal(sem, inc=1, device_id=d, device_id_type=MESH)

    group = [sib] + zdev
    ring = xdev[:2] + ydev[:2]
    ag_n.end()
    tell(group, R.free.at[0])
    ag_h = gather_rows(R.nm)
    rs_m.start()

    @pl.loop(0, 8)
    def _(n):
        w = R.wm[block(n) + (slice(1536, 2304),)].reshape(256, 768)
        cols, v = spread(n, mm_tb(R.act[2], w))
        R.pb2[:, :, :, cols] = v

    R.dgs[...] = jnp.zeros((2, WIDTH), F32)
    ag_c[3]()
    rs2.s3()
    pl.semaphore_wait(R.free.at[0], 4)

    @pl.loop(0, 4)
    def _(t):
        rows = owned(t)
        dv, dg = rms_back(R.hid[rows], R.fgain[...], rs2.total(rows))
        dh = dv + R.ct[pl.ds(pl.multiple_of(zh * 64 + t * 16, 16), 16), :].astype(F32)
        R.dgs[1:2, :] += dg
        R.gh[rows] = dh
        R.nm[me, zh, rows] = dh.astype(BF)

    rs2.end()
    ag_h.s0()
    rs_d.t3()
    ag_h.s1()
    rs_m.onward()
    ag_h.s2()
    ag_h.s3()
    rs_f.s0()

    @pl.loop(0, 4)
    def _(i):
        zi, ci = lax.div(i, 2), lax.rem(i, 2)
        grad = mm(R.nm[i].reshape(128, WIDTH), R.wo[...].reshape(WIDTH, 256))
        logits = jnp.zeros((128, 128), F32)
        for h in (0, 1):
            gate = jax.nn.sigmoid(R.gl[i][:, h : h + 1])
            gr = grad[:, h * 128 : (h + 1) * 128]
            a = R.att[i, :, h * 128 : (h + 1) * 128]
            low = (gr * gate).astype(BF)
            dl = jnp.sum(gr * a, axis=1, keepdims=True) * (gate * (1.0 - gate))
            logits = jnp.where(lanes == h, dl, logits)
            delta = jnp.sum(low.astype(F32) * a, axis=1, keepdims=True)
            R.dox[zi, h, ci, :, 0:128] = low
            R.dox[zi, h, ci, :, 128:256] = three_parts(-delta, lanes)
        R.gsc[i, :, 512:640] = logits.astype(BF)

    rs_d.t4()
    rs_f.s1()

    R.oacc[...] = jnp.zeros((2, 512, 256), F32)
    row_t = lax.broadcasted_iota(jnp.int32, (256, 512), 1)
    key_t = lax.broadcasted_iota(jnp.int32, (256, 512), 0)
    seen_t = key_t <= lax.rem(row_t, 256)

    def backward(at, groups, diagonal):
        k = R.kv[at + (ALL, ALL, slice(0, 128))].reshape(256, 128)
        v = R.kv[at + (ALL, ALL, slice(128, 256))].reshape(256, 128)
        kx = jnp.concatenate([k, ones], axis=1)
        vx = jnp.concatenate([v, ones], axis=1)
        kt = k.T
        dk = dv = None
        for g in groups:
            q, d = R.qx[g].reshape(512, 256), R.dox[g].reshape(512, 256)
            p = jnp.exp2(mm_tb(kx, q))
            if g == diagonal:
                p = jnp.where(seen_t, p, 0.0)
            ds = (p * mm_tb(vx, d)).astype(BF)
            dvg = mm(p.astype(BF), d[:, 0:128])
            dkg = mm(ds, q[:, 0:128])
            dk, dv = (dkg, dvg) if dk is None else (dk + dkg, dv + dvg)
            dq = mm(kt, ds)
            R.oacc[g, 0:128] += dq[:, 0:256]
            R.oacc[g, 128:256] += dq[:, 256:512]
        R.kv[at + (ALL, ALL, slice(0, 128))] = dk.astype(BF).reshape(2, 128, 128)
        R.kv[at + (ALL, ALL, slice(128, 256))] = dv.astype(BF).reshape(2, 128, 128)

    def nothing(at):
        R.kv[at] = jnp.zeros((2, 128, 256), BF)

    rs_k = scatter(R.kv, (R.k_r2, R.k_r1, R.k_q2, R.k_q1), slice(0, 256))
    side(backward, 2, nothing)
    rs_k.t0()
    side(backward, 1, nothing)
    rs_k.t1(0)
    rs_m.t3()
    rs_k.t2(0)
    rs_f.s2()
    side(backward, 3, nothing)
    rs_k.t1(1)
    rs_k.t2(1)
    rs_d.t5()
    R.wm[:, y, x, :, :, 1536:2304] = R.ga[:, y, x, :, :, 0:768]
    near(backward, nothing)
    backward((0, y, x), (0, 1), 0)
    backward((1, y, x), (1,), 1)
    rs_f.s3()
    tw_o = twin(R.ob)

    @pl.loop(0, 4)
    def _(t):
        rows = owned(t)
        R.ob[zh, rows] = (R.hid[rows] + rs_f.total(rows)).astype(BF)

    rs_f.end()
    tell(group, R.free.at[1])
    tw_o[0]()
    rs_m.t4()
    rs_k.t3()
    rs_m.t5()
    tell(ring, R.free.at[2])
    gb_m = give_back(R.wm, R.wlm)
    gb_m[0]()

    R.dgh[...] = jnp.zeros((8, 128), F32)

    @pl.loop(0, 4)
    def _(i):
        zi, ci = lax.div(i, 2), lax.rem(i, 2)
        for h in (0, 1):
            cols = pl.ds(pl.multiple_of(ci * 128, 128), 128)
            dq = R.oacc[zi, h * 128 : (h + 1) * 128, cols].T * SCALE
            dq = rope_back(dq, R.cos[i], R.sin[i])
            dv, dg = rms_back(R.qraw[i, :, h * 128 : (h + 1) * 128], R.qg[...], dq)
            R.dgh[0:1, :] += dg
            R.gsc[i, :, h * 128 : (h + 1) * 128] = dv.astype(BF)

    rs_k.t4()

    @pl.loop(0, 8)
    def _(n):
        at = block(n)
        g = mm(turned(R.nm, n), R.gated[...].reshape(512, 256))
        R.ga[at + (slice(0, 256),)] = g.astype(BF).reshape(4, 2, 32, 256)
        t = turned(R.xn, n)
        g = mm(t, R.gsc[:, :, 0:256].reshape(512, 256))
        R.ga[at + (slice(256, 512),)] = g.astype(BF).reshape(4, 2, 32, 256)
        g = mm(t, R.gsc[:, :, 512:640].reshape(512, 128))
        R.ga[at + (slice(512, 640),)] = g.astype(BF).reshape(4, 2, 32, 128)

    rs_e = scatter(R.ga, big, slice(0, 640))
    pl.semaphore_wait(R.free.at[2], 4)
    rs_k.t5()
    rs_e.start()

    @pl.loop(0, 4)
    def _(i):
        zi, ci = lax.div(i, 2), lax.rem(i, 2)
        dk = R.kv[zi, y, x, ci, :, 0:128].astype(F32) * LN2
        dk = rope_back(dk, R.cos[i], R.sin[i])
        dv, dg = rms_back(R.kraw[i], R.kg[...], dk)
        R.dgh[1:2, :] += dg
        R.gsc[i, :, 256:384] = dv.astype(BF)
        R.gsc[i, :, 384:512] = R.kv[zi, y, x, ci, :, 128:256]

    @pl.loop(0, 8)
    def _(n):
        w = R.wa[lax.div(n, 4), lax.rem(n, 4)].reshape(256, PROJ)
        cols, v = spread(n, mm_tb(R.gsc[...].reshape(512, PROJ), w))
        R.pb[:, :, :, cols] = v

    rs3 = reduce_rows(R.pb, R.rsib, R.rz)
    pl.semaphore_wait(R.free.at[1], 4)
    rs3.s0()

    @pl.loop(0, 8)
    def _(n):
        g = mm(turned(R.xn, n), R.gsc[:, :, 256:512].reshape(512, 256))
        R.ga[block(n) + (slice(640, 896),)] = g.astype(BF).reshape(4, 2, 32, 256)

    rs_l = scatter(R.ga, big, slice(640, 896))
    rs3.s1()
    rs_l.start()
    rs_e.onward()
    rs3.s2()
    rs_l.onward()
    rs_e.t3()
    rs_l.t3()
    rs3.s3()
    tw_i = twin(R.ib)

    @pl.loop(0, 4)
    def _(t):
        rows = owned(t)
        v = R.x[pl.ds(pl.multiple_of(zh * 64 + t * 16, 16), 16), :].astype(F32)
        dv, dg = rms_back(v, R.ag[...], rs3.total(rows))
        R.dgs[0:1, :] += dg
        R.ib[zh, rows] = (R.gh[rows] + dv).astype(BF)

    rs3.end()

    for r in range(16):
        R.sums[0, r : r + 1, :] = R.dgs[0:1, r * 128 : (r + 1) * 128]
        R.sums[0, 16 + r : 17 + r, :] = R.dgs[1:2, r * 128 : (r + 1) * 128]
    R.sums[0, 32:40, :] = R.dgh[...]

    def add_up(stage, devices):
        g, first = Group(len(devices)), (0, 7, 10)[stage]
        for i, d in enumerate(devices):
            g.go(R.sums.at[stage], R.came.at[first + i], d, i)

        def finish():
            v = R.sums[stage]
            for i in range(len(devices)):
                g.got(R.came.at[first + i], i)
                v = v + R.came[first + i]
            R.sums[stage + 1] = v
            g.end()

        return finish

    fin = add_up(0, group + zsib)
    tw_i[0]()
    rs_e.t4()
    rs_l.t4()
    fin()
    fin = add_up(1, xdev)
    rs_e.t5()
    rs_l.t5()
    gb_a = give_back(R.ga, R.wl8)
    gb_a[0]()
    fin()
    fin = add_up(2, ydev)
    gb_m[1]()
    R.o_fm[...] = R.wlm[...]
    tw_o[1]()
    R.o_out[...] = R.ob[...].reshape(128, WIDTH)
    tw_i[1]()
    R.o_in[...] = R.ib[...].reshape(128, WIDTH)
    fin()
    R.o_gain[...] = R.sums[3]
    gb_a[1]()
    R.o_fa[...] = R.wl8[...]
    ag_x[3]()
    ag_h.end()
    gb_m[2]()
    gb_a[2]()
    assert count[0] == COPIES, count


INPUTS = [
    *("x", "ct", "ag", "qg", "kg", "fgain"),
    *("qw", "kw", "vw", "gw", "ow", "fg", "fu", "fd"),
    *("cos", "sin"),
]
OUTPUTS = [
    ("o_out", (128, WIDTH), BF),
    ("o_in", (128, WIDTH), BF),
    ("o_gain", (40, 128), F32),
    ("o_fm", (4, 32, 2304), BF),
    ("o_fa", (4, 32, ATT), BF),
]
RESULTS = [
    ((128, WIDTH), BF),
    ((128, WIDTH), BF),
    ((1, 32), F32),
    ((32, 1024), F32),
    ((32, 512), F32),
    ((32, 512), F32),
    ((32, 8), F32),
    ((1, 128), F32),
    ((1, 128), F32),
    ((32, 1024), F32),
    ((1, 32), F32),
    ((32, 3072), F32),
    ((32, 3072), F32),
    ((32, 3072), F32),
]
SCRATCH = [
    ("wla", (4, 32, PROJ), BF),
    ("wlo", (4, 32, 256), BF),
    ("wl8", (4, 32, ATT), BF),
    ("wlm", (4, 32, 2304), BF),
    ("wa", (2, 4, 4, 2, 32, PROJ), BF),
    ("wo", (2, 4, 4, 2, 32, 256), BF),
    ("ga", (2, 4, 4, 2, 32, ATT), BF),
    ("wm", (2, 4, 4, 2, 32, 2304), BF),
    ("kv", (2, 4, 4, 2, 128, 256), BF),
    ("xn", (4, 2, 64, WIDTH), BF),
    ("cot", (4, 2, 64, WIDTH), BF),
    ("nm", (4, 2, 64, WIDTH), BF),
    ("qraw", (4, 128, 256), F32),
    ("kraw", (4, 128, 128), F32),
    ("gl", (4, 128, 128), F32),
    ("qx", (2, 2, 2, 128, 256), BF),
    ("dox", (2, 2, 2, 128, 256), BF),
    ("oacc", (2, 512, 256), F32),
    ("att", (4, 128, 256), F32),
    ("gated", (4, 128, 256), BF),
    ("gsc", (4, 128, PROJ), BF),
    ("act", (3, 512, 768), BF),
    ("hid", (64, WIDTH), F32),
    ("gh", (64, WIDTH), F32),
    ("dgs", (2, WIDTH), F32),
    ("dgh", (8, 128), F32),
    ("pb", (4, 2, 64, WIDTH), BF),
    ("pb2", (4, 2, 64, WIDTH), BF),
    ("rsib", (2, 2, 64, WIDTH), BF),
    ("rz", (3, 64, WIDTH), BF),
    ("m_r2", (2, 2, 4, 32, 2304), BF),
    ("m_r1", (2, 2, 4, 2, 32, 2304), BF),
    ("m_q2", (2, 2, 1, 32, 2304), BF),
    ("m_q1", (2, 2, 1, 2, 32, 2304), BF),
    ("k_r2", (2, 2, 4, 128, 256), BF),
    ("k_r1", (2, 2, 4, 2, 128, 256), BF),
    ("k_q2", (2, 2, 1, 128, 256), BF),
    ("k_q1", (2, 2, 1, 2, 128, 256), BF),
    ("ob", (2, 64, WIDTH), BF),
    ("ib", (2, 64, WIDTH), BF),
    ("sums", (4, 40, 128), F32),
    ("came", (13, 40, 128), F32),
]
COPIES = 308


def kernel(*refs):
    names = INPUTS + [o[0] for o in OUTPUTS] + [v[0] for v in SCRATCH] + ["send", "recv", "free"]
    body(SimpleNamespace(**dict(zip(names, refs))))


def finish(out, grad_in, gain, fm, fa, *to):
    to[0][...] = out[...]
    to[1][...] = grad_in[...]
    place = lax.axis_index("seq")
    for at, first in ((2, 0), (10, 16)):
        v = gain[pl.ds(first + lax.div(place, 4), 1), :]
        to[at][...] = pltpu.roll(v, lax.rem(128 - lax.rem(place, 4) * 32, 128), 1)[:, 0:32]
    to[7][...] = gain[32:33, :]
    to[8][...] = gain[33:34, :]
    gates = jnp.zeros((32, 8), F32)
    for i in range(4):
        wide = slice(i * 256, (i + 1) * 256)
        low = slice(i * 128, (i + 1) * 128)
        to[9][:, wide] = fa[i, :, 0:256].astype(F32)
        to[3][:, wide] = fa[i, :, 256:512].astype(F32)
        to[4][:, low] = fa[i, :, 640:768].astype(F32)
        to[5][:, low] = fa[i, :, 768:896].astype(F32)
        pick = select(lambda r, q, i=i: (q == r + 2 * i) & (r < 2), (128, 8))
        gates = gates + mm(fa[i, :, 512:640], pick)
        for k in range(3):
            cols = slice(k * 768, (k + 1) * 768)
            to[11 + k][:, i * 768 : (i + 1) * 768] = fm[i, :, cols].astype(F32)
    to[6][...] = gates


def per_device(
    inputs,
    attention_gain,
    query_weight,
    key_matrix,
    value_matrix,
    gate_weight,
    query_gain,
    key_gain,
    out_weight,
    feed_gain,
    feed_gate,
    feed_up,
    feed_down,
    cotangent,
):
    place = lax.axis_index("seq")
    run = lax.rem(lax.div(place, 2), 16)
    half = jnp.arange(4, dtype=jnp.int32)[:, None]
    row = jnp.arange(128, dtype=jnp.int32)[None, :]
    positions = (half // 2) * 4096 + run * 256 + (half % 2) * 128 + row
    inverse = ROPE_BASE ** (-(jnp.arange(HEAD // 2, dtype=F32) * 2.0) / HEAD)
    angles = positions.astype(F32)[:, :, None] * inverse
    cos, sin = jnp.cos(angles), jnp.sin(angles)
    cos = jnp.concatenate([cos, cos], axis=-1)
    sin = jnp.concatenate([-sin, sin], axis=-1)
    vmem = pl.BlockSpec(memory_space=pltpu.VMEM)
    out = pl.pallas_call(
        kernel,
        out_shape=[jax.ShapeDtypeStruct(shape, kind) for _, shape, kind in OUTPUTS],
        in_specs=[vmem] * len(INPUTS),
        out_specs=[vmem] * len(OUTPUTS),
        scratch_shapes=[pltpu.VMEM(shape, kind) for _, shape, kind in SCRATCH]
        + [pltpu.SemaphoreType.DMA((COPIES,)), pltpu.SemaphoreType.DMA((COPIES,))]
        + [pltpu.SemaphoreType.REGULAR((3,))],
        compiler_params=pltpu.CompilerParams(
            collective_id=0, has_side_effects=True, vmem_limit_bytes=63 * 2**20
        ),
        name="block",
    )(
        inputs,
        cotangent,
        attention_gain.reshape(1, WIDTH),
        query_gain.reshape(1, HEAD),
        key_gain.reshape(1, HEAD),
        feed_gain.reshape(1, WIDTH),
        query_weight,
        key_matrix,
        value_matrix,
        gate_weight,
        out_weight.T,
        feed_gate,
        feed_up,
        feed_down.T,
        cos,
        sin,
    )
    out = pl.pallas_call(
        finish,
        out_shape=[jax.ShapeDtypeStruct(shape, kind) for shape, kind in RESULTS],
        compiler_params=pltpu.CompilerParams(vmem_limit_bytes=60 * 2**20),
        name="results",
    )(*out)
    out = list(out)
    for i in (2, 7, 8, 10):
        out[i] = out[i].reshape(-1)
    for i in (9, 13):
        out[i] = out[i].T
    return tuple(out)


def solution(mesh):
    seq, both, turned = P("seq", None), P("seq", "grp"), P("grp", "seq")
    in_specs = (seq, P(), both, both, both, both, P(), P(), turned, P(), both, both, turned, seq)
    out_specs = (
        seq, seq, P("seq"), both, both, both, both, P(), P(), turned, P("seq"), both, both, turned,
    )
    return jax.shard_map(
        per_device, mesh=mesh, in_specs=in_specs, out_specs=out_specs, check_vma=False
    )
```

```python
from types import SimpleNamespace

import jax
import jax.numpy as jnp
import numpy as np
from jax import lax
from jax.experimental import pallas as pl
from jax.experimental.pallas import tpu as pltpu
from jax.sharding import PartitionSpec as P

EPSILON = 1e-06
ROPE_BASE = 1000000.0
WIDTH = 2048
HEAD = 128
EIGHTH = 768
ATT = 896
PROJ = 512
SCALE = HEAD**-0.5
LOG2E = 1.4426950408889634
LN2 = 0.6931471805599453
BF, F32 = jnp.bfloat16, jnp.float32
MESH = pl.DeviceIdType.MESH
ALL = slice(None)


def mm(a, b):
    return jnp.dot(a, b, preferred_element_type=F32)


def mm_tb(a, b):
    return lax.dot_general(a, b, (((1,), (1,)), ((), ())), preferred_element_type=F32)


def rms_scale(v):
    return lax.rsqrt(jnp.mean(v * v, axis=-1, keepdims=True) + EPSILON)


def rms_back(v, gain, dy):
    r = rms_scale(v)
    u = gain * dy
    dv = r * (u - v * (r * r * jnp.mean(u * v, axis=-1, keepdims=True)))
    return dv, jnp.sum(dy * v * r, axis=0, keepdims=True)


def rope(v, cos, sin):
    return v * cos + pltpu.roll(v, HEAD // 2, 1) * sin


def rope_back(v, cos, sin):
    return v * cos + pltpu.roll(v * sin, HEAD // 2, 1)


def three_parts(v, lanes):
    hi = v.astype(BF).astype(F32)
    mid = (v - hi).astype(BF).astype(F32)
    low = v - hi - mid
    return jnp.where(
        lanes == 0, hi, jnp.where(lanes == 1, mid, jnp.where(lanes == 2, low, 0.0))
    ).astype(BF)


def select(row_of, shape):
    row = lax.broadcasted_iota(jnp.int32, shape, 0)
    col = lax.broadcasted_iota(jnp.int32, shape, 1)
    return jnp.where(row_of(row, col), 1.0, 0.0).astype(BF)


def body(R):
    s, zh = lax.axis_index("seq"), lax.axis_index("grp")
    c = lax.rem(s, 2)
    x = lax.rem(lax.div(s, 2), 4)
    y = lax.rem(lax.div(s, 8), 4)
    zl = lax.div(s, 32)
    z = zh * 2 + zl
    j = y * 4 + x
    me = zl * 2 + c

    def up(v, k):
        return lax.rem(v + k, 4)

    def dev(zz, yy, xx, cc):
        return (lax.rem(zz, 2) * 32 + yy * 8 + xx * 2 + cc, lax.div(zz, 2))

    sib = dev(z, y, x, 1 - c)
    zs = [up(z, 1), up(z, 3), up(z, 2)]
    zdev = [dev(v, y, x, c) for v in zs]
    part = (zl_dev := (1 - zl) * 32 + y * 8 + x * 2 + c, zh)
    diag = ((1 - zl) * 32 + y * 8 + x * 2 + 1 - c, zh)
    other = (zl_dev, 1 - zh)
    xdev = [dev(z, y, up(x, k), c) for k in (1, 3, 2)]
    ydev = [dev(z, up(y, k), x, c) for k in (1, 3, 2)]

    barrier = pltpu.get_barrier_semaphore()
    zsib = [dev(v, y, x, 1 - c) for v in zs]
    greet = [sib] + zdev + zsib + xdev + ydev
    for d in greet:
        pl.semaphore_signal(barrier, inc=1, device_id=d, device_id_type=MESH)

    count = [0]

    def ids(k):
        count[0] += k
        return count[0] - k

    class Group:
        def __init__(self, k, base=None):
            self.base, self.sent = ids(k) if base is None else base, []

        def copy(self, src, dst, d, i):
            i += self.base
            return pltpu.make_async_remote_copy(
                src_ref=src, dst_ref=dst, send_sem=R.send.at[i], recv_sem=R.recv.at[i],
                device_id=d, device_id_type=MESH,
            )

        def go(self, src, dst, d, i):
            cp = self.copy(src, dst, d, i)
            cp.start()
            self.sent.append(cp)

        def got(self, ref, i):
            self.copy(ref, ref, sib, i).wait_recv()

        def end(self):
            for cp in self.sent:
                cp.wait_send()

    def exchange(buf, wl, base):
        g = Group(3, base)

        def start():
            buf[zl, y, x, c] = wl[me]
            dst = buf.at[zl, y, x, c]
            g.go(wl.at[zl * 2 + 1 - c], dst, sib, 0)
            g.go(wl.at[(1 - zl) * 2 + c], dst, part, 1)
            g.go(wl.at[(1 - zl) * 2 + 1 - c], dst, diag, 2)

        def wait():
            g.got(buf.at[zl, y, x, 1 - c], 0)
            g.got(buf.at[1 - zl, y, x, c], 1)
            g.got(buf.at[1 - zl, y, x, 1 - c], 2)

        return start, wait, g.end

    def give_back(src, dst, base):
        g = Group(3, base)

        def start():
            dst[me] = src[zl, y, x, c]
            g.go(src.at[zl, y, x, 1 - c], dst.at[me], sib, 0)
            g.go(src.at[1 - zl, y, x, c], dst.at[me], part, 1)
            g.go(src.at[1 - zl, y, x, 1 - c], dst.at[me], diag, 2)

        def wait():
            g.got(dst.at[zl * 2 + 1 - c], 0)
            g.got(dst.at[(1 - zl) * 2 + c], 1)
            g.got(dst.at[(1 - zl) * 2 + 1 - c], 2)

        return start, wait, g.end

    a_y = SimpleNamespace(
        full=lambda p: (0, p), half=lambda p, h: (0, p, ALL, h), elem=lambda p, k, h: (0, p, k, h),
        k=4, pos=y, dev=ydev,
    )
    a_x = SimpleNamespace(
        full=lambda p: (0, y, p), half=lambda p, h: (0, y, p, h), elem=lambda p, k, h: (0, y, p, h),
        k=1, pos=x, dev=xdev,
    )
    b_x = SimpleNamespace(
        full=lambda p: (1, ALL, p), half=lambda p, h: (1, ALL, p, h), elem=lambda p, k, h: (1, k, p, h),
        k=4, pos=x, dev=xdev,
    )
    b_y = SimpleNamespace(
        full=lambda p: (1, p, x), half=lambda p, h: (1, p, x, h), elem=lambda p, k, h: (1, p, x, h),
        k=1, pos=y, dev=ydev,
    )

    def gather_ring(buf, a, cs, base):
        g, p = Group(6, base), a.pos
        left, right, across = up(p, 3), up(p, 1), up(p, 2)

        def half(q, h):
            at = a.half(q, h)
            return buf.at[at if cs is None else at + (ALL,) * (5 - len(at)) + (cs,)]

        def s1():
            for i, (h, d) in enumerate(((0, 0), (1, 1), (1, 0), (0, 1))):
                g.go(half(p, h), half(p, h), a.dev[d], i)

        def s2():
            g.got(half(left, 0), 0)
            g.go(half(left, 0), half(left, 0), a.dev[0], 4)
            g.got(half(right, 1), 1)
            g.go(half(right, 1), half(right, 1), a.dev[1], 5)

        def s3():
            g.got(half(left, 1), 2)
            g.got(half(right, 0), 3)

        def s4():
            g.got(half(across, 0), 4)
            g.got(half(across, 1), 5)

        return s1, s2, s3, s4, g.end

    def gather(buf, base, cs=None):
        one = [gather_ring(buf, a_x, cs, base), gather_ring(buf, b_y, cs, base + 6)]
        two = [gather_ring(buf, a_y, cs, base + 12), gather_ring(buf, b_x, cs, base + 18)]

        def t1():
            for r in one:
                r[0]()

        def t2():
            for r in one:
                r[1]()

        def t3():
            for r, q in zip(one, two):
                r[2]()
                r[3]()
                q[0]()

        def t4():
            for r in two:
                r[1]()

        def t5():
            for r in two:
                r[2]()

        def t6():
            for r in two:
                r[3]()
            for r in one + two:
                r[4]()

        return t1, t2, t3, t4, t5, t6

    def reduce_ring(buf, a, r2, r1, cs, bs, rows, base):
        g, p, k = Group(6, base), a.pos, a.k
        first = ALL if k == 4 else 0

        def half(q, h):
            at = a.half(q, h)
            return buf.at[at + (ALL,) * (5 - len(at)) + (cs,)]

        def elem(q, n, h):
            return a.elem(q, n, h) + (ALL, cs)

        def far(i):
            return r2.at[i, first, rows, bs]

        def near(i, h):
            return r1.at[i, first, h, rows, bs]

        def loop(fn):
            if k == 1:
                fn(0)
            else:
                pl.loop(0, k)(fn)

        def s1():
            for i in (0, 1):
                g.go(half(up(p, 2), i), far(i), a.dev[i], i)

        def direct(i):
            g.go(half(up(p, 1 + 2 * i), 1 - i), near(i, 1 - i), a.dev[i], 2 + i)

        def s2(i):
            g.got(far(i), i)
            to = up(p, 1 + 2 * i)

            def add(n):
                at = elem(to, n, i)
                buf[at] = buf[at] + r2[i, n, rows, bs]

            loop(add)
            g.go(half(to, i), near(i, i), a.dev[i], 4 + i)

        def s3():
            for i in (0, 1):
                g.got(near(i, 1 - i), 2 + i)
                g.got(near(i, i), 4 + i)

            def add(n):
                for h in (0, 1):
                    at = elem(p, n, h)
                    total = (
                        buf[at].astype(F32)
                        + r1[0, n, h, rows, bs].astype(F32)
                        + r1[1, n, h, rows, bs].astype(F32)
                    )
                    buf[at] = total.astype(BF)

            loop(add)

        return s1, direct, s2, s3, g.end

    def scatter(buf, bufs, base, cs, bs=None, rows=ALL):
        bs = cs if bs is None else bs
        one = [
            reduce_ring(buf, a_y, bufs[0].at[0], bufs[1].at[0], cs, bs, rows, base),
            reduce_ring(buf, b_x, bufs[0].at[1], bufs[1].at[1], cs, bs, rows, base + 6),
        ]
        two = [
            reduce_ring(buf, a_x, bufs[2].at[0], bufs[3].at[0], cs, bs, rows, base + 12),
            reduce_ring(buf, b_y, bufs[2].at[1], bufs[3].at[1], cs, bs, rows, base + 18),
        ]

        def t0():
            for r in one:
                r[0]()

        def t1(i):
            for r in one:
                r[1](i)

        def t2(i):
            for r in one:
                r[2](i)

        def t3():
            for r, q in zip(one, two):
                r[3]()
                q[0]()
                q[1](0)
                q[1](1)

        def t4():
            for i in (0, 1):
                for r in two:
                    r[2](i)

        def t5():
            for r in two:
                r[3]()
            for r in one + two:
                r[4]()

        def start():
            t0()
            t1(0)
            t1(1)

        def onward():
            t2(0)
            t2(1)

        return SimpleNamespace(t0=t0, t1=t1, t2=t2, t3=t3, t4=t4, t5=t5, start=start, onward=onward)

    def place(zz, cc):
        return (lax.rem(zz, 2) * 2 + cc, lax.div(zz, 2))

    half_rows = (slice(0, 32), slice(32, 64))

    rows_base = ids(8)

    def reduce_rows(pb, rsib, rz):
        g = Group(8, rows_base)

        def mine(zz, h):
            return pb.at[place(zz, c) + (half_rows[h],)]

        def s0():
            for t in (0, 1):
                g.go(pb.at[t * 2 + 1 - c], rsib.at[t], sib, t)

        def s1():
            g.got(rsib.at[0], 0)
            g.got(rsib.at[1], 1)

            def add(zz):
                at = place(zz, c)
                pb[at] = pb[at] + rsib[lax.rem(zz, 2), lax.div(zz, 2)]

            add(zs[2])
            for i in (0, 1):
                g.go(mine(zs[2], i), rz.at[2, half_rows[i]], zdev[i], 2 + i)
            for i in (0, 1):
                add(zs[i])
                g.go(mine(zs[i], 1 - i), rz.at[i, half_rows[1 - i]], zdev[i], 4 + i)
            add(z)

        def s2():
            for i in (0, 1):
                rows = half_rows[i]
                g.got(rz.at[2, rows], 2 + i)
                at = place(zs[i], c) + (rows,)
                pb[at] = pb[at] + rz[2, rows]
                g.go(mine(zs[i], i), rz.at[i, rows], zdev[i], 6 + i)

        def s3():
            for i in (0, 1):
                g.got(rz.at[i, half_rows[1 - i]], 4 + i)
                g.got(rz.at[i, half_rows[i]], 6 + i)

        def total(rows):
            v = pb[me, zh, rows].astype(F32)
            return v + rz[0, rows].astype(F32) + rz[1, rows].astype(F32)

        return SimpleNamespace(s0=s0, s1=s1, s2=s2, s3=s3, end=g.end, total=total)

    spread_base = ids(10)

    def gather_rows(buf):
        g = Group(10, spread_base)

        def at(zz, h):
            return buf.at[place(zz, c) + (half_rows[h],)]

        def s0():
            for i, (h, d) in enumerate(((0, 0), (1, 1), (1, 0), (0, 1))):
                g.go(at(z, h), at(z, h), zdev[d], i)
            own = buf.at[place(z, c)]
            g.go(own, own, sib, 6)

        def s1():
            g.got(at(zs[1], 0), 0)
            g.go(at(zs[1], 0), at(zs[1], 0), zdev[0], 4)
            g.got(at(zs[0], 1), 1)
            g.go(at(zs[0], 1), at(zs[0], 1), zdev[1], 5)

        def s2():
            def hand_on(zz, i):
                whole = buf.at[place(zz, c)]
                g.go(whole, whole, sib, i)

            g.got(at(zs[1], 1), 2)
            hand_on(zs[1], 7)
            g.got(at(zs[0], 0), 3)
            hand_on(zs[0], 8)
            g.got(at(zs[2], 0), 4)
            g.got(at(zs[2], 1), 5)
            hand_on(zs[2], 9)

        def s3():
            for i, zz in ((6, z), (7, zs[1]), (8, zs[0]), (9, zs[2])):
                g.got(buf.at[place(zz, 1 - c)], i)

        return SimpleNamespace(s0=s0, s1=s1, s2=s2, s3=s3, end=g.end)

    def gather_blocks(buf):
        g = Group(5)

        def s0():
            g.go(buf.at[me, 0], buf.at[me, 0], part, 0)
            g.go(buf.at[me, 1], buf.at[me, 1], other, 1)
            g.go(buf.at[me], buf.at[me], sib, 2)

        def s1():
            for h in (0, 1):
                at = buf.at[(1 - zl) * 2 + c, h]
                g.got(at, h)
                g.go(at, at, sib, 3 + h)

        def s2():
            g.got(buf.at[zl * 2 + 1 - c], 2)
            for h in (0, 1):
                g.got(buf.at[(1 - zl) * 2 + 1 - c, h], 3 + h)

        return s0, s1, s2, g.end

    def twin(buf):
        g = Group(1)

        def start():
            g.go(buf.at[zh], buf.at[zh], zdev[2], 0)

        def wait():
            g.got(buf.at[1 - zh], 0)
            g.end()

        return start, wait

    for i in range(4):
        R.wla[i, :, 0:256] = R.qw[:, i * 256 : (i + 1) * 256]
        R.wla[i, :, 256:384] = R.kw[:, i * 128 : (i + 1) * 128]
        R.wla[i, :, 384:512] = R.vw[:, i * 128 : (i + 1) * 128]
    pairs, rings = [ids(3) for _ in range(3)], [ids(24) for _ in range(5)]
    ex_a = exchange(R.wa, R.wla, pairs[0])
    ex_o = exchange(R.wo, R.wlo, pairs[1])
    ex_m = exchange(R.wm, R.wlm, pairs[2])
    ag_a, ag_o = gather(R.wa, rings[0]), gather(R.wo, rings[1])
    ag_m = gather(R.wm, rings[2], slice(0, 1536))
    ag_d = gather(R.wm, rings[3], slice(1536, 2304))
    ag_x = gather_blocks(R.xn)
    ag_c = gather_blocks(R.cot)
    ag_kv = gather(R.kv, rings[4])

    pl.semaphore_wait(barrier, len(greet))
    ex_a[0]()

    @pl.loop(0, 4)
    def _(t):
        rows = pl.ds(pl.multiple_of(lax.rem(t, 2) * 32, 32), 32)
        v = R.x[pl.ds(pl.multiple_of(t * 32, 32), 32), :].astype(F32)
        R.xn[me, lax.div(t, 2), rows] = (v * rms_scale(v) * R.ag[...]).astype(BF)

    ag_x[0]()
    first = lax.broadcasted_iota(jnp.int32, (128, 128), 1) < 64
    for i in range(4):
        base = (i // 2) * 32 + j * 2 + i % 2
        cb, sb = R.cb[pl.ds(base, 1), :], R.sb[pl.ds(base, 1), :]
        sin = sb * R.cr[...] + cb * R.sr[...]
        R.cos[i] = cb * R.cr[...] - sb * R.sr[...]
        R.sin[i] = jnp.where(first, -sin, sin)
        R.wlo[i, :, 0:256] = R.ow[:, i * 256 : (i + 1) * 256]
        pick = select(lambda r, q, i=i: (r == q + 2 * i) & (q < 2), (8, 128))
        R.wlo[i, :, 256:384] = mm(R.gw[...].T, pick).astype(BF)
        R.wlm[i, :, 0:768] = R.fg[:, i * 768 : (i + 1) * 768]
        R.wlm[i, :, 768:1536] = R.fu[:, i * 768 : (i + 1) * 768]
        R.wlm[i, :, 1536:2304] = R.fd[:, i * 768 : (i + 1) * 768]
    R.cot[me] = R.ct[...].reshape(2, 64, WIDTH)
    ex_a[1]()
    ag_a[0]()
    ex_o[0]()
    ex_m[0]()
    ag_a[1]()
    ag_x[1]()
    ag_a[2]()
    ag_x[2]()
    ag_a[3]()
    ex_o[1]()
    ag_o[0]()
    ex_m[1]()
    ag_m[0]()
    ag_d[0]()
    ag_a[4]()
    ag_a[5]()

    @pl.loop(0, 2)
    def _(zi):
        w = R.wa[...].reshape(WIDTH, PROJ)
        both = mm(R.xn[pl.ds(zi * 2, 2)].reshape(256, WIDTH), w)
        for ci in (0, 1):
            i, raw = zi * 2 + ci, both[ci * 128 : (ci + 1) * 128]
            cos, sin = R.cos[i], R.sin[i]
            R.qraw[i] = raw[:, 0:256]
            R.kraw[i] = raw[:, 256:384]
            for h in (0, 1):
                v = raw[:, h * 128 : (h + 1) * 128]
                q = rope(v * rms_scale(v) * R.qg[...], cos, sin) * (SCALE * LOG2E)
                R.qx[zi, h, ci, :, 0:128] = q.astype(BF)
            v = raw[:, 256:384]
            k = rope(v * rms_scale(v) * R.kg[...], cos, sin)
            R.kv[zi, y, x, ci, :, 0:128] = k.astype(BF)
            R.kv[zi, y, x, ci, :, 128:256] = raw[:, 384:512].astype(BF)

    ag_kv[0]()
    ag_c[0]()

    ones = jnp.ones((256, 128), BF)
    key_i = lax.broadcasted_iota(jnp.int32, (512, 256), 1)
    row_i = lax.broadcasted_iota(jnp.int32, (512, 256), 0)
    seen = key_i <= lax.rem(row_i, 256)
    R.oacc[...] = jnp.zeros((2, 512, 256), F32)

    def forward(at, groups, diagonal):
        k = R.kv[at + (ALL, ALL, slice(0, 128))].reshape(256, 128)
        v = R.kv[at + (ALL, ALL, slice(128, 256))].reshape(256, 128)
        v = jnp.concatenate([v, ones], axis=1)
        for g in groups:
            p = jnp.exp2(mm_tb(R.qx[g, :, :, :, 0:128].reshape(512, 128), k))
            if g == diagonal:
                p = jnp.where(seen, p, 0.0)
            R.oacc[g] += mm(p.astype(BF), v)

    def tile_pair(fn, empty, at0, at1):
        t0, t1 = at0[0] * 4 + at0[1], at1[0] * 4 + at1[1]

        @pl.when(t0 < j)
        def _():
            fn((0,) + at0, (0, 1), None)

        @pl.when(t0 > j)
        def _():
            fn((0,) + at0, (1,), None)

        @pl.when(t1 < j)
        def _():
            fn((1,) + at1, (1,), None)

        if empty is not None:

            @pl.when(t1 > j)
            def _():
                empty((1,) + at1)

    def near(fn, empty=None):
        @pl.loop(1, 4)
        def _(k):
            tile_pair(fn, empty, (y, up(x, k)), (up(y, k), x))

    def side(fn, a, empty=None):
        @pl.loop(0, 4)
        def _(k):
            tile_pair(fn, empty, (up(y, a), k), (k, up(x, a)))

    ag_o[1]()
    ag_m[1]()
    ag_d[1]()
    forward((0, y, x), (0, 1), 0)
    forward((1, y, x), (1,), 1)
    ag_kv[1]()
    ag_kv[2]()
    near(forward)
    ag_c[1]()
    ag_kv[3]()
    ag_o[2]()
    ag_kv[4]()

    @pl.loop(0, 2)
    def _(k):
        side(forward, 1 + 2 * k)

    ag_o[3]()
    ag_m[2]()
    ag_kv[5]()
    side(forward, 2)
    ag_o[4]()
    ag_o[5]()

    @pl.loop(0, 2)
    def _(zi):
        w = R.wo[:, :, :, :, :, 256:384].reshape(WIDTH, 128)
        v = mm(R.xn[pl.ds(zi * 2, 2)].reshape(256, WIDTH), w)
        R.gl[pl.ds(zi * 2, 2)] = v.reshape(2, 128, 128)

    lanes = lax.broadcasted_iota(jnp.int32, (128, 128), 1)

    @pl.loop(0, 4)
    def _(i):
        zi, ci = lax.div(i, 2), lax.rem(i, 2)
        for h in (0, 1):
            rows = pl.ds(pl.multiple_of(h * 256 + ci * 128, 128), 128)
            total = R.oacc[zi, rows, 128:256]
            a = R.oacc[zi, rows, 0:128] / total
            R.att[i, :, h * 128 : (h + 1) * 128] = a
            R.qx[zi, h, ci, :, 128:256] = three_parts(-jnp.log2(total), lanes)
            gate = jax.nn.sigmoid(R.gl[i][:, h : h + 1])
            R.gated[i, :, h * 128 : (h + 1) * 128] = (a * gate).astype(BF)

    def spread(n, value):
        cols = pl.ds(pl.multiple_of(n * 256, 256), 256)
        return cols, value.reshape(4, 2, 64, 256).astype(BF)

    rs1 = reduce_rows(R.pb, R.rsib, R.rz)
    ag_n = gather_rows(R.nm)

    def project(cc):
        rows = jnp.concatenate([R.gated[cc], R.gated[2 + cc]], axis=0)

        @pl.loop(0, 8, unroll=4)
        def _(n):
            w = R.wo[lax.div(n, 4), lax.rem(n, 4), :, :, :, 0:256].reshape(256, 256)
            cols = pl.ds(pl.multiple_of(n * 256, 256), 256)
            v = mm_tb(rows, w).astype(BF).reshape(2, 2, 64, 256)
            R.pb[cc, :, :, cols] = v[0]
            R.pb[2 + cc, :, :, cols] = v[1]

    project(1 - c)
    rs1.s0()
    project(c)
    rs1.s1()
    rs1.s2()
    ag_m[3]()
    ag_d[2]()
    rs1.s3()

    def owned(t):
        return pl.ds(pl.multiple_of(t * 16, 16), 16)

    @pl.loop(0, 4)
    def _(t):
        rows = owned(t)
        v = R.x[pl.ds(pl.multiple_of(zh * 64 + t * 16, 16), 16), :].astype(F32)
        v = v + rs1.total(rows)
        R.hid[rows] = v
        R.nm[me, zh, rows] = (v * rms_scale(v) * R.fgain[...]).astype(BF)

    rs1.end()
    for g in (ex_a, ex_o, ex_m):
        g[2]()
    ag_n.s0()
    ag_c[2]()
    ag_n.s1()
    ag_m[4]()
    ag_n.s2()
    ag_m[5]()
    ag_d[3]()
    ag_n.s3()

    def weight(k, n):
        at = pl.ds(pl.multiple_of(k * 768 + n * 256, 256), 256)
        return R.wm[:, :, :, :, :, at].reshape(WIDTH, 256)

    @pl.loop(0, 3, unroll=3)
    def _(n):
        cols = pl.ds(pl.multiple_of(n * 256, 256), 256)
        rows = R.nm[...].reshape(512, WIDTH)
        gate = mm(rows, weight(0, n))
        upper = mm(rows, weight(1, n))
        sg = jax.nn.sigmoid(gate)
        silu = gate * sg
        R.act[0, :, cols] = (upper * (sg * (1.0 + gate * (1.0 - sg)))).astype(BF)
        R.act[1, :, cols] = silu.astype(BF)
        R.act[2, :, cols] = (silu * upper).astype(BF)

    def block(n):
        return (lax.div(n, 4), lax.rem(n, 4), ALL, ALL, ALL)

    def turned(ref, n):
        cols = pl.ds(pl.multiple_of(n * 256, 256), 256)
        return ref[:, :, :, cols].reshape(512, 256).T

    big = (R.m_r2, R.m_r1, R.m_q2, R.m_q1)
    rs_d = scatter(R.ga, big, rings[0], slice(0, 768))
    rs_m = scatter(R.wm, big, rings[1], slice(0, 1536), slice(768, 2304))

    @pl.loop(0, 8, unroll=4)
    def _(n):
        g = mm(turned(R.cot, n), R.act[2])
        R.ga[block(n) + (slice(0, 768),)] = g.astype(BF).reshape(4, 2, 32, 768)

    rs_d.start()
    ag_d[4]()
    ag_d[5]()

    @pl.loop(0, 3, unroll=3)
    def _(n):
        cols = pl.ds(pl.multiple_of(n * 256, 256), 256)
        grad = mm(R.cot[...].reshape(512, WIDTH), weight(2, n))
        R.act[0, :, cols] = (grad * R.act[0, :, cols].astype(F32)).astype(BF)
        R.act[1, :, cols] = (grad * R.act[1, :, cols].astype(F32)).astype(BF)

    @pl.loop(0, 8, unroll=4)
    def _(n):
        at = block(n)
        v = mm_tb(R.act[0], R.wm[at + (slice(0, 768),)].reshape(256, 768))
        v = v + mm_tb(R.act[1], R.wm[at + (slice(768, 1536),)].reshape(256, 768))
        cols, v = spread(n, v)
        R.pb[:, :, :, cols] = v

    rs2 = reduce_rows(R.pb, R.rsib, R.rz)
    rs_f = reduce_rows(R.pb2, R.rsib, R.rz)
    rs2.s0()

    def feed_weights(n):
        at = block(n)
        t = turned(R.nm, n)
        R.wm[at + (slice(0, 768),)] = mm(t, R.act[0]).astype(BF).reshape(4, 2, 32, 768)
        R.wm[at + (slice(768, 1536),)] = mm(t, R.act[1]).astype(BF).reshape(4, 2, 32, 768)

    pl.loop(0, 4, unroll=4)(feed_weights)
    rs2.s1()
    rs_d.onward()
    pl.loop(4, 8, unroll=4)(feed_weights)
    rs2.s2()

    def tell(devices, sem):
        for d in devices:
            pl.semaphore_signal(sem, inc=1, device_id=d, device_id_type=MESH)

    group = [sib] + zdev
    ring = xdev[:2] + ydev[:2]
    ag_n.end()
    tell(group, R.free.at[0])
    ag_h = gather_rows(R.nm)
    rs_m.start()

    @pl.loop(0, 8, unroll=4)
    def _(n):
        w = R.wm[block(n) + (slice(1536, 2304),)].reshape(256, 768)
        cols, v = spread(n, mm_tb(R.act[2], w))
        R.pb2[:, :, :, cols] = v

    R.dgs[...] = jnp.zeros((2, WIDTH), F32)
    ag_c[3]()
    rs2.s3()
    pl.semaphore_wait(R.free.at[0], 4)

    @pl.loop(0, 4)
    def _(t):
        rows = owned(t)
        dv, dg = rms_back(R.hid[rows], R.fgain[...], rs2.total(rows))
        dh = dv + R.ct[pl.ds(pl.multiple_of(zh * 64 + t * 16, 16), 16), :].astype(F32)
        R.dgs[1:2, :] += dg
        R.gh[rows] = dh
        R.nm[me, zh, rows] = dh.astype(BF)

    rs2.end()
    ag_h.s0()
    rs_d.t3()
    ag_h.s1()
    rs_m.onward()
    ag_h.s2()
    ag_h.s3()
    rs_f.s0()

    @pl.loop(0, 2)
    def _(zi):
        w = R.wo[:, :, :, :, :, 0:256].reshape(WIDTH, 256)
        both = mm(R.nm[pl.ds(zi * 2, 2)].reshape(256, WIDTH), w)
        for ci in (0, 1):
            i, grad = zi * 2 + ci, both[ci * 128 : (ci + 1) * 128]
            logits = jnp.zeros((128, 128), F32)
            for h in (0, 1):
                gate = jax.nn.sigmoid(R.gl[i][:, h : h + 1])
                gr = grad[:, h * 128 : (h + 1) * 128]
                a = R.att[i, :, h * 128 : (h + 1) * 128]
                low = (gr * gate).astype(BF)
                dl = jnp.sum(gr * a, axis=1, keepdims=True) * (gate * (1.0 - gate))
                logits = jnp.where(lanes == h, dl, logits)
                delta = jnp.sum(low.astype(F32) * a, axis=1, keepdims=True)
                R.dox[zi, h, ci, :, 0:128] = low
                R.dox[zi, h, ci, :, 128:256] = three_parts(-delta, lanes)
            R.gsc[i, :, 512:640] = logits.astype(BF)

    rs_d.t4()
    rs_f.s1()

    R.oacc[...] = jnp.zeros((2, 512, 256), F32)
    row_t = lax.broadcasted_iota(jnp.int32, (256, 512), 1)
    key_t = lax.broadcasted_iota(jnp.int32, (256, 512), 0)
    seen_t = key_t <= lax.rem(row_t, 256)

    def backward(at, groups, diagonal):
        k = R.kv[at + (ALL, ALL, slice(0, 128))].reshape(256, 128)
        v = R.kv[at + (ALL, ALL, slice(128, 256))].reshape(256, 128)
        kx = jnp.concatenate([k, ones], axis=1)
        vx = jnp.concatenate([v, ones], axis=1)
        kt = k.T
        dk = dv = None
        for g in groups:
            q, d = R.qx[g].reshape(512, 256), R.dox[g].reshape(512, 256)
            p = jnp.exp2(mm_tb(kx, q))
            if g == diagonal:
                p = jnp.where(seen_t, p, 0.0)
            ds = (p * mm_tb(vx, d)).astype(BF)
            dvg = mm(p.astype(BF), d[:, 0:128])
            dkg = mm(ds, q[:, 0:128])
            dk, dv = (dkg, dvg) if dk is None else (dk + dkg, dv + dvg)
            dq = mm(kt, ds)
            R.oacc[g, 0:128] += dq[:, 0:256]
            R.oacc[g, 128:256] += dq[:, 256:512]
        R.kv[at + (ALL, ALL, slice(0, 128))] = dk.astype(BF).reshape(2, 128, 128)
        R.kv[at + (ALL, ALL, slice(128, 256))] = dv.astype(BF).reshape(2, 128, 128)

    def nothing(at):
        R.kv[at] = jnp.zeros((2, 128, 256), BF)

    small = (R.k_r2, R.k_r1, R.k_q2, R.k_q1)
    rs_k = scatter(R.kv, small, rings[4], slice(0, 256))
    side(backward, 2, nothing)
    rs_k.t0()
    side(backward, 1, nothing)
    rs_k.t1(0)
    side(backward, 3, nothing)
    rs_k.t1(1)
    rs_f.s2()
    rs_k.t2(0)
    rs_k.t2(1)
    rs_m.t3()
    rs_d.t5()
    tell(ring, R.free.at[2])
    R.wm[:, y, x, :, :, 1536:2304] = R.ga[:, y, x, :, :, 0:768]
    near(backward, nothing)
    backward((0, y, x), (0, 1), 0)
    backward((1, y, x), (1,), 1)
    rs_f.s3()
    tw_o = twin(R.ob)

    @pl.loop(0, 4)
    def _(t):
        rows = owned(t)
        R.ob[zh, rows] = (R.hid[rows] + rs_f.total(rows)).astype(BF)

    rs_f.end()
    tell(group, R.free.at[1])
    tw_o[0]()

    R.dgh[...] = jnp.zeros((8, 128), F32)

    @pl.loop(0, 4)
    def _(i):
        zi, ci = lax.div(i, 2), lax.rem(i, 2)
        for h in (0, 1):
            cols = pl.ds(pl.multiple_of(ci * 128, 128), 128)
            dq = R.oacc[zi, h * 128 : (h + 1) * 128, cols].T * SCALE
            dq = rope_back(dq, R.cos[i], R.sin[i])
            dv, dg = rms_back(R.qraw[i, :, h * 128 : (h + 1) * 128], R.qg[...], dq)
            R.dgh[0:1, :] += dg
            R.gsc[i, :, h * 128 : (h + 1) * 128] = dv.astype(BF)

    rs_m.t4()

    @pl.loop(0, 8, unroll=4)
    def _(n):
        at = block(n)
        g = mm(turned(R.nm, n), R.gated[...].reshape(512, 256))
        R.ga[at + (slice(0, 256),)] = g.astype(BF).reshape(4, 2, 32, 256)
        t = turned(R.xn, n)
        g = mm(t, R.gsc[:, :, 0:256].reshape(512, 256))
        R.ga[at + (slice(256, 512),)] = g.astype(BF).reshape(4, 2, 32, 256)
        g = mm(t, R.gsc[:, :, 512:640].reshape(512, 128))
        R.ga[at + (slice(512, 640),)] = g.astype(BF).reshape(4, 2, 32, 128)

    rs_e = scatter(R.ga, big, rings[2], slice(0, 640))
    pl.semaphore_wait(R.free.at[2], 4)
    rs_k.t3()
    rs_m.t5()
    gb_m = give_back(R.wm, R.wlm, pairs[0])
    gb_m[0]()
    rs_k.t4()
    rs_e.start()
    rs_k.t5()

    @pl.loop(0, 4)
    def _(i):
        zi, ci = lax.div(i, 2), lax.rem(i, 2)
        dk = R.kv[zi, y, x, ci, :, 0:128].astype(F32) * LN2
        dk = rope_back(dk, R.cos[i], R.sin[i])
        dv, dg = rms_back(R.kraw[i], R.kg[...], dk)
        R.dgh[1:2, :] += dg
        R.gsc[i, :, 256:384] = dv.astype(BF)
        R.gsc[i, :, 384:512] = R.kv[zi, y, x, ci, :, 128:256]

    @pl.loop(0, 8, unroll=4)
    def _(n):
        g = mm(turned(R.xn, n), R.gsc[:, :, 256:512].reshape(512, 256))
        R.ga[block(n) + (slice(640, 896),)] = g.astype(BF).reshape(4, 2, 32, 256)

    rs_l = scatter(R.ga, small, rings[3], slice(640, 896), slice(0, 256), slice(0, 32))
    rs_l.start()

    @pl.loop(0, 8, unroll=4)
    def _(n):
        at = block(n)
        v = mm_tb(R.gsc[:, :, 0:512].reshape(512, 512), R.wa[at].reshape(256, PROJ))
        w = R.wo[at + (slice(256, 384),)].reshape(256, 128)
        v = v + mm_tb(R.gsc[:, :, 512:640].reshape(512, 128), w)
        cols = pl.ds(pl.multiple_of(n * 256, 256), 256)
        dg = jnp.sum(v * R.xn[:, :, :, cols].reshape(512, 256).astype(F32), axis=0, keepdims=True)
        R.dgs[0:1, cols] = dg / R.ag[:, cols]
        cols, v = spread(n, v)
        R.pb[:, :, :, cols] = v

    rs3 = reduce_rows(R.pb, R.rsib, R.rz)
    pl.semaphore_wait(R.free.at[1], 4)
    rs3.s0()

    for r in range(16):
        R.sums[0, r : r + 1, :] = R.dgs[0:1, r * 128 : (r + 1) * 128]
        R.sums[0, 16 + r : 17 + r, :] = R.dgs[1:2, r * 128 : (r + 1) * 128]
    R.sums[0, 32:40, :] = R.dgh[...]

    def add_up(stage, devices):
        g, first = Group(len(devices)), (0, 7, 10)[stage]
        for i, d in enumerate(devices):
            g.go(R.sums.at[stage], R.came.at[first + i], d, i)

        def finish():
            v = R.sums[stage]
            for i in range(len(devices)):
                g.got(R.came.at[first + i], i)
                v = v + R.came[first + i]
            R.sums[stage + 1] = v
            g.end()

        return finish

    fin = add_up(0, group + zsib)
    rs_e.onward()
    rs3.s1()
    rs_l.onward()
    fin()
    fin = add_up(1, xdev)
    rs3.s2()
    rs_e.t3()
    fin()
    fin = add_up(2, ydev)
    rs_l.t3()
    rs3.s3()
    tw_i = twin(R.ib)

    @pl.loop(0, 4)
    def _(t):
        rows = owned(t)
        v = R.x[pl.ds(pl.multiple_of(zh * 64 + t * 16, 16), 16), :].astype(F32)
        dv, _ = rms_back(v, R.ag[...], rs3.total(rows))
        R.ib[zh, rows] = (R.gh[rows] + dv).astype(BF)

    tw_i[0]()
    rs3.end()
    rs_e.t4()
    rs_l.t4()
    def put(i, src, dst):
        cp = pltpu.make_async_copy(src, dst, R.put.at[i])
        cp.start()
        return cp

    gb_m[1]()
    puts = [put(0, R.wlm, R.o_fm)]
    tw_o[1]()
    puts.append(put(1, R.ob, R.o_out))
    fin()
    puts.append(put(2, R.sums.at[3], R.o_gain))
    rs_e.t5()
    rs_l.t5()
    gb_a = give_back(R.ga, R.wl8, pairs[1])
    gb_a[0]()
    tw_i[1]()
    puts.append(put(3, R.ib, R.o_in))
    gb_a[1]()
    puts.append(put(4, R.wl8, R.o_fa))
    for cp in puts:
        cp.wait()
    ag_x[3]()
    ag_h.end()
    gb_m[2]()
    gb_a[2]()
    assert count[0] == COPIES, count


INPUTS = [
    *("x", "ct", "ag", "qg", "kg", "fgain"),
    *("qw", "kw", "vw", "gw", "ow", "fg", "fu", "fd"),
    *("cr", "sr", "cb", "sb"),
]
OUTPUTS = [
    ("o_out", (2, 64, WIDTH), BF),
    ("o_in", (2, 64, WIDTH), BF),
    ("o_gain", (40, 128), F32),
    ("o_fm", (4, 32, 2304), BF),
    ("o_fa", (4, 32, ATT), BF),
]
RESULTS = [
    ((128, WIDTH), BF),
    ((128, WIDTH), BF),
    ((1, 32), F32),
    ((32, 1024), F32),
    ((32, 512), F32),
    ((32, 512), F32),
    ((8, 32), F32),
    ((1, 128), F32),
    ((1, 128), F32),
    ((32, 1024), F32),
    ((1, 32), F32),
    ((32, 3072), F32),
    ((32, 3072), F32),
    ((32, 3072), F32),
]
SCRATCH = [
    ("wla", (4, 32, PROJ), BF),
    ("wlo", (4, 32, 384), BF),
    ("wl8", (4, 32, ATT), BF),
    ("wlm", (4, 32, 2304), BF),
    ("wa", (2, 4, 4, 2, 32, PROJ), BF),
    ("wo", (2, 4, 4, 2, 32, 384), BF),
    ("ga", (2, 4, 4, 2, 32, ATT), BF),
    ("wm", (2, 4, 4, 2, 32, 2304), BF),
    ("kv", (2, 4, 4, 2, 128, 256), BF),
    ("xn", (4, 2, 64, WIDTH), BF),
    ("cot", (4, 2, 64, WIDTH), BF),
    ("nm", (4, 2, 64, WIDTH), BF),
    ("cos", (4, 128, 128), F32),
    ("sin", (4, 128, 128), F32),
    ("qraw", (4, 128, 256), F32),
    ("kraw", (4, 128, 128), F32),
    ("gl", (4, 128, 128), F32),
    ("qx", (2, 2, 2, 128, 256), BF),
    ("dox", (2, 2, 2, 128, 256), BF),
    ("oacc", (2, 512, 256), F32),
    ("att", (4, 128, 256), F32),
    ("gated", (4, 128, 256), BF),
    ("gsc", (4, 128, 640), BF),
    ("act", (3, 512, 768), BF),
    ("hid", (64, WIDTH), F32),
    ("gh", (64, WIDTH), F32),
    ("dgs", (2, WIDTH), F32),
    ("dgh", (8, 128), F32),
    ("pb", (4, 2, 64, WIDTH), BF),
    ("pb2", (4, 2, 64, WIDTH), BF),
    ("rsib", (2, 2, 64, WIDTH), BF),
    ("rz", (3, 64, WIDTH), BF),
    ("m_r2", (2, 2, 4, 32, 2304), BF),
    ("m_r1", (2, 2, 4, 2, 32, 2304), BF),
    ("m_q2", (2, 2, 1, 32, 2304), BF),
    ("m_q1", (2, 2, 1, 2, 32, 2304), BF),
    ("k_r2", (2, 2, 4, 128, 256), BF),
    ("k_r1", (2, 2, 4, 2, 128, 256), BF),
    ("k_q2", (2, 2, 1, 128, 256), BF),
    ("k_q1", (2, 2, 1, 2, 128, 256), BF),
    ("ob", (2, 64, WIDTH), BF),
    ("ib", (2, 64, WIDTH), BF),
    ("sums", (4, 40, 128), F32),
    ("came", (13, 40, 128), F32),
]
COPIES = 172


def kernel(*refs):
    names = INPUTS + [o[0] for o in OUTPUTS] + [v[0] for v in SCRATCH] + ["send", "recv", "free", "put"]
    body(SimpleNamespace(**dict(zip(names, refs))))


def finish(out, grad_in, gain, fm, fa, *to):
    to[0][...] = out[...].reshape(128, WIDTH)
    to[1][...] = grad_in[...].reshape(128, WIDTH)
    place = lax.axis_index("seq")
    for at, first in ((2, 0), (10, 16)):
        v = gain[pl.ds(first + lax.div(place, 4), 1), :]
        to[at][...] = pltpu.roll(v, lax.rem(128 - lax.rem(place, 4) * 32, 128), 1)[:, 0:32]
    to[7][...] = gain[32:33, :]
    to[8][...] = gain[33:34, :]
    gates = jnp.zeros((8, 32), F32)
    for i in range(4):
        wide = slice(i * 256, (i + 1) * 256)
        low = slice(i * 128, (i + 1) * 128)
        to[9][:, wide] = fa[i, :, 0:256].astype(F32)
        to[3][:, wide] = fa[i, :, 256:512].astype(F32)
        to[4][:, low] = fa[i, :, 640:768].astype(F32)
        to[5][:, low] = fa[i, :, 768:896].astype(F32)
        pick = select(lambda r, q, i=i: (r == q + 2 * i) & (q < 2), (8, 128))
        gates = gates + mm_tb(pick, fa[i, :, 512:640])
        for k in range(3):
            cols = slice(k * 768, (k + 1) * 768)
            to[11 + k][:, i * 768 : (i + 1) * 768] = fm[i, :, cols].astype(F32)
    to[6][...] = gates


def rope_tables():
    inverse = ROPE_BASE ** (-np.arange(HEAD // 2) * 2.0 / HEAD)
    inverse = np.concatenate([inverse, inverse]).astype(np.float32).astype(np.float64)
    rows = np.arange(128)[:, None] * inverse
    blocks = np.arange(64)[:, None] * 128 * inverse
    return [jnp.asarray(f(a), F32) for a in (rows, blocks) for f in (np.cos, np.sin)]


def per_device(
    inputs,
    attention_gain,
    query_weight,
    key_matrix,
    value_matrix,
    gate_weight,
    query_gain,
    key_gain,
    out_weight,
    feed_gain,
    feed_gate,
    feed_up,
    feed_down,
    cotangent,
):
    vmem = pl.BlockSpec(memory_space=pltpu.VMEM)
    out = pl.pallas_call(
        kernel,
        out_shape=[jax.ShapeDtypeStruct(shape, kind) for _, shape, kind in OUTPUTS],
        in_specs=[vmem] * len(INPUTS),
        out_specs=[pl.BlockSpec(memory_space=pl.ANY)] * len(OUTPUTS),
        scratch_shapes=[pltpu.VMEM(shape, kind) for _, shape, kind in SCRATCH]
        + [pltpu.SemaphoreType.DMA((COPIES,)), pltpu.SemaphoreType.DMA((COPIES,))]
        + [pltpu.SemaphoreType.REGULAR((3,)), pltpu.SemaphoreType.DMA((5,))],
        compiler_params=pltpu.CompilerParams(
            collective_id=0, has_side_effects=True, vmem_limit_bytes=63 * 2**20
        ),
        name="block",
    )(
        inputs,
        cotangent,
        attention_gain.reshape(1, WIDTH),
        query_gain.reshape(1, HEAD),
        key_gain.reshape(1, HEAD),
        feed_gain.reshape(1, WIDTH),
        query_weight,
        key_matrix,
        value_matrix,
        gate_weight.T,
        out_weight.T,
        feed_gate,
        feed_up,
        feed_down.T,
        *rope_tables(),
    )
    out = pl.pallas_call(
        finish,
        out_shape=[jax.ShapeDtypeStruct(shape, kind) for shape, kind in RESULTS],
        compiler_params=pltpu.CompilerParams(vmem_limit_bytes=60 * 2**20),
        name="results",
    )(*out)
    out = list(out)
    for i in (2, 7, 8, 10):
        out[i] = out[i].reshape(-1)
    for i in (6, 9, 13):
        out[i] = out[i].T
    return tuple(out)


def solution(mesh):
    seq, both, turned = P("seq", None), P("seq", "grp"), P("grp", "seq")
    in_specs = (seq, P(), both, both, both, both, P(), P(), turned, P(), both, both, turned, seq)
    out_specs = (
        seq, seq, P("seq"), both, both, both, both, P(), P(), turned, P("seq"), both, both, turned,
    )
    return jax.shard_map(
        per_device, mesh=mesh, in_specs=in_specs, out_specs=out_specs, check_vma=False
    )
```

```python
from types import SimpleNamespace

import jax
import jax.numpy as jnp
import numpy as np
from jax import lax
from jax.experimental import pallas as pl
from jax.experimental.pallas import tpu as pltpu
from jax.sharding import PartitionSpec as P

EPSILON = 1e-06
ROPE_BASE = 1000000.0
WIDTH = 2048
HEAD = 128
EIGHTH = 768
ATT = 896
PROJ = 512
SCALE = HEAD**-0.5
LOG2E = 1.4426950408889634
LN2 = 0.6931471805599453
BF, F32 = jnp.bfloat16, jnp.float32
MESH = pl.DeviceIdType.MESH
ALL = slice(None)


def mm(a, b):
    return jnp.dot(a, b, preferred_element_type=F32)


def mm_tb(a, b):
    return lax.dot_general(a, b, (((1,), (1,)), ((), ())), preferred_element_type=F32)


def rms_scale(v):
    return lax.rsqrt(jnp.mean(v * v, axis=-1, keepdims=True) + EPSILON)


def rms_back(v, gain, dy):
    r = rms_scale(v)
    u = gain * dy
    dv = r * (u - v * (r * r * jnp.mean(u * v, axis=-1, keepdims=True)))
    return dv, jnp.sum(dy * v * r, axis=0, keepdims=True)


def rope(v, cos, sin):
    return v * cos + pltpu.roll(v, HEAD // 2, 1) * sin


def rope_back(v, cos, sin):
    return v * cos + pltpu.roll(v * sin, HEAD // 2, 1)


def three_parts(v, lanes):
    hi = v.astype(BF).astype(F32)
    mid = (v - hi).astype(BF).astype(F32)
    low = v - hi - mid
    return jnp.where(
        lanes == 0, hi, jnp.where(lanes == 1, mid, jnp.where(lanes == 2, low, 0.0))
    ).astype(BF)


def select(row_of, shape):
    row = lax.broadcasted_iota(jnp.int32, shape, 0)
    col = lax.broadcasted_iota(jnp.int32, shape, 1)
    return jnp.where(row_of(row, col), 1.0, 0.0).astype(BF)


def body(R):
    s, zh = lax.axis_index("seq"), lax.axis_index("grp")
    c = lax.rem(s, 2)
    x = lax.rem(lax.div(s, 2), 4)
    y = lax.rem(lax.div(s, 8), 4)
    zl = lax.div(s, 32)
    z = zh * 2 + zl
    j = y * 4 + x
    me = zl * 2 + c

    def up(v, k):
        return lax.rem(v + k, 4)

    def dev(zz, yy, xx, cc):
        return (lax.rem(zz, 2) * 32 + yy * 8 + xx * 2 + cc, lax.div(zz, 2))

    sib = dev(z, y, x, 1 - c)
    zs = [up(z, 1), up(z, 3), up(z, 2)]
    zdev = [dev(v, y, x, c) for v in zs]
    part = (zl_dev := (1 - zl) * 32 + y * 8 + x * 2 + c, zh)
    diag = ((1 - zl) * 32 + y * 8 + x * 2 + 1 - c, zh)
    other = (zl_dev, 1 - zh)
    xdev = [dev(z, y, up(x, k), c) for k in (1, 3, 2)]
    ydev = [dev(z, up(y, k), x, c) for k in (1, 3, 2)]

    barrier = pltpu.get_barrier_semaphore()
    zsib = [dev(v, y, x, 1 - c) for v in zs]
    greet = [sib] + zdev + zsib + xdev + ydev
    for d in greet:
        pl.semaphore_signal(barrier, inc=1, device_id=d, device_id_type=MESH)

    count = [0]

    def ids(k):
        count[0] += k
        return count[0] - k

    class Group:
        def __init__(self, k, base=None):
            self.base, self.sent = ids(k) if base is None else base, []

        def copy(self, src, dst, d, i):
            i += self.base
            return pltpu.make_async_remote_copy(
                src_ref=src, dst_ref=dst, send_sem=R.send.at[i], recv_sem=R.recv.at[i],
                device_id=d, device_id_type=MESH,
            )

        def go(self, src, dst, d, i):
            cp = self.copy(src, dst, d, i)
            cp.start()
            self.sent.append(cp)

        def got(self, ref, i):
            self.copy(ref, ref, sib, i).wait_recv()

        def end(self):
            for cp in self.sent:
                cp.wait_send()

    def exchange(buf, wl, base, cs=ALL):
        g = Group(3, base)

        def start():
            buf[zl, y, x, c, :, cs] = wl[me, :, cs]
            dst = buf.at[zl, y, x, c, :, cs]
            g.go(wl.at[zl * 2 + 1 - c, :, cs], dst, sib, 0)
            g.go(wl.at[(1 - zl) * 2 + c, :, cs], dst, part, 1)
            g.go(wl.at[(1 - zl) * 2 + 1 - c, :, cs], dst, diag, 2)

        def wait():
            g.got(buf.at[zl, y, x, 1 - c, :, cs], 0)
            g.got(buf.at[1 - zl, y, x, c, :, cs], 1)
            g.got(buf.at[1 - zl, y, x, 1 - c, :, cs], 2)

        return start, wait, g.end

    def give_back(src, dst, base):
        g = Group(3, base)

        def start():
            dst[me] = src[zl, y, x, c]
            g.go(src.at[zl, y, x, 1 - c], dst.at[me], sib, 0)
            g.go(src.at[1 - zl, y, x, c], dst.at[me], part, 1)
            g.go(src.at[1 - zl, y, x, 1 - c], dst.at[me], diag, 2)

        def wait():
            g.got(dst.at[zl * 2 + 1 - c], 0)
            g.got(dst.at[(1 - zl) * 2 + c], 1)
            g.got(dst.at[(1 - zl) * 2 + 1 - c], 2)

        return start, wait, g.end

    a_y = SimpleNamespace(
        full=lambda p: (0, p), half=lambda p, h: (0, p, ALL, h), elem=lambda p, k, h: (0, p, k, h),
        k=4, pos=y, dev=ydev,
    )
    a_x = SimpleNamespace(
        full=lambda p: (0, y, p), half=lambda p, h: (0, y, p, h), elem=lambda p, k, h: (0, y, p, h),
        k=1, pos=x, dev=xdev,
    )
    b_x = SimpleNamespace(
        full=lambda p: (1, ALL, p), half=lambda p, h: (1, ALL, p, h), elem=lambda p, k, h: (1, k, p, h),
        k=4, pos=x, dev=xdev,
    )
    b_y = SimpleNamespace(
        full=lambda p: (1, p, x), half=lambda p, h: (1, p, x, h), elem=lambda p, k, h: (1, p, x, h),
        k=1, pos=y, dev=ydev,
    )

    def gather_ring(buf, a, cs, base):
        g, p = Group(6, base), a.pos
        left, right, across = up(p, 3), up(p, 1), up(p, 2)

        def half(q, h):
            at = a.half(q, h)
            return buf.at[at if cs is None else at + (ALL,) * (5 - len(at)) + (cs,)]

        def s1():
            for i, (h, d) in enumerate(((0, 0), (1, 1), (1, 0), (0, 1))):
                g.go(half(p, h), half(p, h), a.dev[d], i)

        def s2():
            g.got(half(left, 0), 0)
            g.go(half(left, 0), half(left, 0), a.dev[0], 4)
            g.got(half(right, 1), 1)
            g.go(half(right, 1), half(right, 1), a.dev[1], 5)

        def s3():
            g.got(half(left, 1), 2)
            g.got(half(right, 0), 3)

        def s4():
            g.got(half(across, 0), 4)
            g.got(half(across, 1), 5)

        return s1, s2, s3, s4, g.end

    def gather(buf, base, cs=None):
        one = [gather_ring(buf, a_x, cs, base), gather_ring(buf, b_y, cs, base + 6)]
        two = [gather_ring(buf, a_y, cs, base + 12), gather_ring(buf, b_x, cs, base + 18)]

        def t1():
            for r in one:
                r[0]()

        def t2():
            for r in one:
                r[1]()

        def t3():
            for r, q in zip(one, two):
                r[2]()
                r[3]()
                q[0]()

        def t4():
            for r in two:
                r[1]()

        def t5():
            for r in two:
                r[2]()

        def t6():
            for r in two:
                r[3]()
            for r in one + two:
                r[4]()

        return t1, t2, t3, t4, t5, t6

    def reduce_ring(buf, a, r2, r1, cs, bs, rows, base):
        g, p, k = Group(6, base), a.pos, a.k
        first = ALL if k == 4 else 0

        def half(q, h):
            at = a.half(q, h)
            return buf.at[at + (ALL,) * (5 - len(at)) + (cs,)]

        def elem(q, n, h):
            return a.elem(q, n, h) + (ALL, cs)

        def far(i):
            return r2.at[i, first, rows, bs]

        def near(i, h):
            return r1.at[i, first, h, rows, bs]

        def loop(fn):
            if k == 1:
                fn(0)
            else:
                pl.loop(0, k)(fn)

        def s1():
            for i in (0, 1):
                g.go(half(up(p, 2), i), far(i), a.dev[i], i)

        def direct(i):
            g.go(half(up(p, 1 + 2 * i), 1 - i), near(i, 1 - i), a.dev[i], 2 + i)

        def s2(i):
            g.got(far(i), i)
            to = up(p, 1 + 2 * i)

            def add(n):
                at = elem(to, n, i)
                buf[at] = buf[at] + r2[i, n, rows, bs]

            loop(add)
            g.go(half(to, i), near(i, i), a.dev[i], 4 + i)

        def s3():
            for i in (0, 1):
                g.got(near(i, 1 - i), 2 + i)
                g.got(near(i, i), 4 + i)

            def add(n):
                for h in (0, 1):
                    at = elem(p, n, h)
                    total = (
                        buf[at].astype(F32)
                        + r1[0, n, h, rows, bs].astype(F32)
                        + r1[1, n, h, rows, bs].astype(F32)
                    )
                    buf[at] = total.astype(BF)

            loop(add)

        return s1, direct, s2, s3, g.end

    def scatter(buf, bufs, base, cs, bs=None, rows=ALL):
        bs = cs if bs is None else bs
        one = [
            reduce_ring(buf, a_y, bufs[0].at[0], bufs[1].at[0], cs, bs, rows, base),
            reduce_ring(buf, b_x, bufs[0].at[1], bufs[1].at[1], cs, bs, rows, base + 6),
        ]
        two = [
            reduce_ring(buf, a_x, bufs[2].at[0], bufs[3].at[0], cs, bs, rows, base + 12),
            reduce_ring(buf, b_y, bufs[2].at[1], bufs[3].at[1], cs, bs, rows, base + 18),
        ]

        def t0():
            for r in one:
                r[0]()

        def t1(i):
            for r in one:
                r[1](i)

        def t2(i):
            for r in one:
                r[2](i)

        def t3():
            for r, q in zip(one, two):
                r[3]()
                q[0]()
                q[1](0)
                q[1](1)

        def t4():
            for i in (0, 1):
                for r in two:
                    r[2](i)

        def t5():
            for r in two:
                r[3]()
            for r in one + two:
                r[4]()

        def start():
            t0()
            t1(0)
            t1(1)

        def onward():
            t2(0)
            t2(1)

        return SimpleNamespace(t0=t0, t1=t1, t2=t2, t3=t3, t4=t4, t5=t5, start=start, onward=onward)

    def place(zz, cc):
        return (lax.rem(zz, 2) * 2 + cc, lax.div(zz, 2))

    half_rows = (slice(0, 32), slice(32, 64))

    rows_base = ids(8)

    def reduce_rows(pb, rsib, rz):
        g = Group(8, rows_base)

        def mine(zz, h):
            return pb.at[place(zz, c) + (half_rows[h],)]

        def s0():
            for i, t in enumerate((zl, 1 - zl)):
                g.go(pb.at[t * 2 + 1 - c], rsib.at[t], sib, i)

        def s1():
            def add(zz):
                at = place(zz, c)
                pb[at] = pb[at] + rsib[lax.rem(zz, 2), lax.div(zz, 2)]

            g.got(rsib.at[zl], 0)
            add(zs[2])
            for i in (0, 1):
                g.go(mine(zs[2], i), rz.at[2, half_rows[i]], zdev[i], 2 + i)
            g.got(rsib.at[1 - zl], 1)
            for i in (0, 1):
                add(zs[i])
                g.go(mine(zs[i], 1 - i), rz.at[i, half_rows[1 - i]], zdev[i], 4 + i)
            add(z)

        def s2():
            for i in (0, 1):
                rows = half_rows[i]
                g.got(rz.at[2, rows], 2 + i)
                at = place(zs[i], c) + (rows,)
                pb[at] = pb[at] + rz[2, rows]
                g.go(mine(zs[i], i), rz.at[i, rows], zdev[i], 6 + i)

        def s3():
            for i in (0, 1):
                g.got(rz.at[i, half_rows[1 - i]], 4 + i)
                g.got(rz.at[i, half_rows[i]], 6 + i)

        def total(rows):
            v = pb[me, zh, rows].astype(F32)
            return v + rz[0, rows].astype(F32) + rz[1, rows].astype(F32)

        return SimpleNamespace(s0=s0, s1=s1, s2=s2, s3=s3, end=g.end, total=total)

    spread_base = ids(10)

    def gather_rows(buf):
        g = Group(10, spread_base)

        def at(zz, h):
            return buf.at[place(zz, c) + (half_rows[h],)]

        def s0():
            for i, (h, d) in enumerate(((0, 0), (1, 1), (1, 0), (0, 1))):
                g.go(at(z, h), at(z, h), zdev[d], i)
            own = buf.at[place(z, c)]
            g.go(own, own, sib, 6)

        def s1():
            g.got(at(zs[1], 0), 0)
            g.go(at(zs[1], 0), at(zs[1], 0), zdev[0], 4)
            g.got(at(zs[0], 1), 1)
            g.go(at(zs[0], 1), at(zs[0], 1), zdev[1], 5)

        def s2():
            def hand_on(zz, i):
                whole = buf.at[place(zz, c)]
                g.go(whole, whole, sib, i)

            g.got(at(zs[1], 1), 2)
            hand_on(zs[1], 7)
            g.got(at(zs[0], 0), 3)
            hand_on(zs[0], 8)
            g.got(at(zs[2], 0), 4)
            g.got(at(zs[2], 1), 5)
            hand_on(zs[2], 9)

        def s3():
            for i, zz in ((6, z), (7, zs[1]), (8, zs[0]), (9, zs[2])):
                g.got(buf.at[place(zz, 1 - c)], i)

        return SimpleNamespace(s0=s0, s1=s1, s2=s2, s3=s3, end=g.end)

    def gather_blocks(buf):
        g = Group(5)

        def s0():
            g.go(buf.at[me, 0], buf.at[me, 0], part, 0)
            g.go(buf.at[me, 1], buf.at[me, 1], other, 1)
            g.go(buf.at[me], buf.at[me], sib, 2)

        def s1():
            for h in (0, 1):
                at = buf.at[(1 - zl) * 2 + c, h]
                g.got(at, h)
                g.go(at, at, sib, 3 + h)

        def s2():
            g.got(buf.at[zl * 2 + 1 - c], 2)
            for h in (0, 1):
                g.got(buf.at[(1 - zl) * 2 + 1 - c, h], 3 + h)

        return s0, s1, s2, g.end

    def twin(buf):
        g = Group(1)

        def start():
            g.go(buf.at[zh], buf.at[zh], zdev[2], 0)

        def wait():
            g.got(buf.at[1 - zh], 0)
            g.end()

        return start, wait

    for i in range(4):
        R.wla[i, :, 0:256] = R.qw[:, i * 256 : (i + 1) * 256]
        R.wla[i, :, 256:384] = R.kw[:, i * 128 : (i + 1) * 128]
        R.wla[i, :, 384:512] = R.vw[:, i * 128 : (i + 1) * 128]
    pairs, rings = [ids(3) for _ in range(4)], [ids(24) for _ in range(5)]
    ex_a = exchange(R.wa, R.wla, pairs[0])
    ex_o = exchange(R.wo, R.wlo, pairs[1])
    ex_m = exchange(R.wm, R.wlm, pairs[2], slice(0, 1536))
    ex_d = exchange(R.wm, R.wlm, pairs[3], slice(1536, 2304))
    ag_a, ag_o = gather(R.wa, rings[0]), gather(R.wo, rings[1])
    ag_m = gather(R.wm, rings[2], slice(0, 1536))
    ag_d = gather(R.wm, rings[3], slice(1536, 2304))
    ag_x = gather_blocks(R.xn)
    ag_c = gather_blocks(R.cot)
    ag_kv = gather(R.kv, rings[4])

    pl.semaphore_wait(barrier, len(greet))
    ex_a[0]()
    for i in range(4):
        R.wlo[i, :, 0:256] = R.ow[:, i * 256 : (i + 1) * 256]
        pick = select(lambda r, q, i=i: (r == q + 2 * i) & (q < 2), (8, 128))
        R.wlo[i, :, 256:384] = mm(R.gw[...].T, pick).astype(BF)
        R.wlm[i, :, 1536:2304] = R.fd[:, i * 768 : (i + 1) * 768]
    ex_o[0]()
    ex_d[0]()

    @pl.loop(0, 4)
    def _(t):
        rows = pl.ds(pl.multiple_of(lax.rem(t, 2) * 32, 32), 32)
        v = R.x[pl.ds(pl.multiple_of(t * 32, 32), 32), :].astype(F32)
        R.xn[me, lax.div(t, 2), rows] = (v * rms_scale(v) * R.ag[...]).astype(BF)

    ag_x[0]()
    for i in range(4):
        R.wlm[i, :, 0:768] = R.fg[:, i * 768 : (i + 1) * 768]
        R.wlm[i, :, 768:1536] = R.fu[:, i * 768 : (i + 1) * 768]
    ex_m[0]()
    first = lax.broadcasted_iota(jnp.int32, (128, 128), 1) < 64
    for i in range(4):
        base = (i // 2) * 32 + j * 2 + i % 2
        cb, sb = R.cb[pl.ds(base, 1), :], R.sb[pl.ds(base, 1), :]
        sin = sb * R.cr[...] + cb * R.sr[...]
        R.cos[i] = cb * R.cr[...] - sb * R.sr[...]
        R.sin[i] = jnp.where(first, -sin, sin)
    R.cot[me] = R.ct[...].reshape(2, 64, WIDTH)
    ex_a[1]()
    ag_a[0]()
    ex_o[1]()
    ag_o[0]()
    ag_a[1]()
    ex_d[1]()
    ag_d[0]()
    ag_o[1]()
    ag_x[1]()
    ag_a[2]()
    ag_d[1]()
    ag_x[2]()
    ag_a[3]()
    ex_m[1]()
    ag_m[0]()
    ag_a[4]()
    ag_a[5]()

    @pl.loop(0, 2)
    def _(zi):
        w = R.wa[...].reshape(WIDTH, PROJ)
        both = mm(R.xn[pl.ds(zi * 2, 2)].reshape(256, WIDTH), w)
        for ci in (0, 1):
            i, raw = zi * 2 + ci, both[ci * 128 : (ci + 1) * 128]
            cos, sin = R.cos[i], R.sin[i]
            R.qraw[i] = raw[:, 0:256]
            R.kraw[i] = raw[:, 256:384]
            for h in (0, 1):
                v = raw[:, h * 128 : (h + 1) * 128]
                q = rope(v * rms_scale(v) * R.qg[...], cos, sin) * (SCALE * LOG2E)
                R.qx[zi, h, ci, :, 0:128] = q.astype(BF)
            v = raw[:, 256:384]
            k = rope(v * rms_scale(v) * R.kg[...], cos, sin)
            R.kv[zi, y, x, ci, :, 0:128] = k.astype(BF)
            R.kv[zi, y, x, ci, :, 128:256] = raw[:, 384:512].astype(BF)

    ag_kv[0]()
    ag_c[0]()
    ag_m[1]()

    ones = jnp.ones((256, 128), BF)
    key_i = lax.broadcasted_iota(jnp.int32, (512, 256), 1)
    row_i = lax.broadcasted_iota(jnp.int32, (512, 256), 0)
    seen = key_i <= lax.rem(row_i, 256)
    R.oacc[...] = jnp.zeros((2, 512, 256), F32)

    def keys_of(at):
        return R.kv[at + (ALL, ALL, slice(0, 128))].reshape(256, 128)

    def values_of(at):
        v = R.kv[at + (ALL, ALL, slice(128, 256))].reshape(256, 128)
        return jnp.concatenate([v, ones], axis=1)

    def forward(tiles):
        work = []
        for g in (0, 1):
            mine = [u for u in tiles if g in u[1]]
            if mine:
                k = jnp.concatenate([keys_of(u[0]) for u in mine], axis=0)
                v = jnp.concatenate([values_of(u[0]) for u in mine], axis=0)
                scores = mm_tb(R.qx[g, :, :, :, 0:128].reshape(512, 128), k)
                work.append((g, mine, v, scores))
        for g, mine, v, scores in work:
            p = jnp.exp2(scores)
            if any(u[2] == g for u in mine):
                parts = [p[:, i * 256 : (i + 1) * 256] for i in range(len(mine))]
                parts = [jnp.where(seen, q, 0.0) if u[2] == g else q for u, q in zip(mine, parts)]
                p = jnp.concatenate(parts, axis=1)
            R.oacc[g] += mm(p.astype(BF), v)

    def tile_pair(fn, empty, at0, at1):
        t0, t1 = at0[0] * 4 + at0[1], at1[0] * 4 + at1[1]
        at0, at1 = (0,) + at0, (1,) + at1

        @pl.when((t0 < j) & (t1 < j))
        def _():
            fn([(at0, (0, 1), None), (at1, (1,), None)])

        @pl.when((t0 < j) & (t1 > j))
        def _():
            fn([(at0, (0, 1), None)])

        @pl.when((t0 > j) & (t1 < j))
        def _():
            fn([(at0, (1,), None), (at1, (1,), None)])

        @pl.when((t0 > j) & (t1 > j))
        def _():
            fn([(at0, (1,), None)])

        if empty is not None:

            @pl.when(t1 > j)
            def _():
                empty(at1)

    own = [((0, y, x), (0, 1), 0), ((1, y, x), (1,), 1)]

    def near(fn, empty=None):
        @pl.loop(1, 4)
        def _(k):
            tile_pair(fn, empty, (y, up(x, k)), (up(y, k), x))

    def side(fn, a, empty=None):
        @pl.loop(0, 4)
        def _(k):
            tile_pair(fn, empty, (up(y, a), k), (k, up(x, a)))

    forward(own)
    ag_kv[1]()
    ag_kv[2]()
    near(forward)
    ag_c[1]()
    ag_kv[3]()
    ag_o[2]()
    ag_kv[4]()

    @pl.loop(0, 2)
    def _(k):
        side(forward, 1 + 2 * k)

    ag_o[3]()
    ag_m[2]()
    ag_kv[5]()
    side(forward, 2)
    ag_o[4]()
    ag_o[5]()

    @pl.loop(0, 2)
    def _(zi):
        w = R.wo[:, :, :, :, :, 256:384].reshape(WIDTH, 128)
        v = mm(R.xn[pl.ds(zi * 2, 2)].reshape(256, WIDTH), w)
        R.gl[pl.ds(zi * 2, 2)] = v.reshape(2, 128, 128)

    lanes = lax.broadcasted_iota(jnp.int32, (128, 128), 1)

    @pl.loop(0, 4)
    def _(i):
        zi, ci = lax.div(i, 2), lax.rem(i, 2)
        for h in (0, 1):
            rows = pl.ds(pl.multiple_of(h * 256 + ci * 128, 128), 128)
            total = R.oacc[zi, rows, 128:256]
            a = R.oacc[zi, rows, 0:128] / total
            R.att[i, :, h * 128 : (h + 1) * 128] = a
            R.qx[zi, h, ci, :, 128:256] = three_parts(-jnp.log2(total), lanes)
            gate = jax.nn.sigmoid(R.gl[i][:, h : h + 1])
            R.gated[i, :, h * 128 : (h + 1) * 128] = (a * gate).astype(BF)

    def spread(n, value):
        cols = pl.ds(pl.multiple_of(n * 256, 256), 256)
        return cols, value.reshape(4, 2, 64, 256).astype(BF)

    rs1 = reduce_rows(R.pb, R.rsib, R.rz)
    ag_n = gather_rows(R.nm)

    def project(cc):
        rows = jnp.concatenate([R.gated[cc], R.gated[2 + cc]], axis=0)

        @pl.loop(0, 8, unroll=4)
        def _(n):
            w = R.wo[lax.div(n, 4), lax.rem(n, 4), :, :, :, 0:256].reshape(256, 256)
            cols = pl.ds(pl.multiple_of(n * 256, 256), 256)
            v = mm_tb(rows, w).astype(BF).reshape(2, 2, 64, 256)
            R.pb[cc, :, :, cols] = v[0]
            R.pb[2 + cc, :, :, cols] = v[1]

    project(1 - c)
    rs1.s0()
    project(c)
    rs1.s1()
    rs1.s2()
    ag_m[3]()
    ag_d[2]()
    rs1.s3()

    def owned(t):
        return pl.ds(pl.multiple_of(t * 16, 16), 16)

    @pl.loop(0, 4)
    def _(t):
        rows = owned(t)
        v = R.x[pl.ds(pl.multiple_of(zh * 64 + t * 16, 16), 16), :].astype(F32)
        v = v + rs1.total(rows)
        R.hid[rows] = v
        R.nm[me, zh, rows] = (v * rms_scale(v) * R.fgain[...]).astype(BF)

    rs1.end()
    for g in (ex_a, ex_o, ex_m, ex_d):
        g[2]()
    ag_n.s0()
    ag_c[2]()
    ag_n.s1()
    ag_m[4]()
    ag_n.s2()
    ag_m[5]()
    ag_d[3]()
    ag_n.s3()

    def weight(k, n):
        at = pl.ds(pl.multiple_of(k * 768 + n * 256, 256), 256)
        return R.wm[:, :, :, :, :, at].reshape(WIDTH, 256)

    @pl.loop(0, 3, unroll=3)
    def _(n):
        cols = pl.ds(pl.multiple_of(n * 256, 256), 256)
        rows = R.nm[...].reshape(512, WIDTH)
        gate = mm(rows, weight(0, n))
        upper = mm(rows, weight(1, n))
        sg = jax.nn.sigmoid(gate)
        silu = gate * sg
        R.act[0, :, cols] = (upper * (sg * (1.0 + gate * (1.0 - sg)))).astype(BF)
        R.act[1, :, cols] = silu.astype(BF)
        R.act[2, :, cols] = (silu * upper).astype(BF)

    def block(n):
        return (lax.div(n, 4), lax.rem(n, 4), ALL, ALL, ALL)

    def turned(ref, n):
        cols = pl.ds(pl.multiple_of(n * 256, 256), 256)
        return ref[:, :, :, cols].reshape(512, 256).T

    big = (R.m_r2, R.m_r1, R.m_q2, R.m_q1)
    rs_d = scatter(R.ga, big, rings[0], slice(0, 768))
    rs_m = scatter(R.wm, big, rings[1], slice(0, 1536), slice(768, 2304))

    @pl.loop(0, 8, unroll=4)
    def _(n):
        g = mm(turned(R.cot, n), R.act[2])
        R.ga[block(n) + (slice(0, 768),)] = g.astype(BF).reshape(4, 2, 32, 768)

    rs_d.start()
    ag_d[4]()
    ag_d[5]()

    @pl.loop(0, 3, unroll=3)
    def _(n):
        cols = pl.ds(pl.multiple_of(n * 256, 256), 256)
        grad = mm(R.cot[...].reshape(512, WIDTH), weight(2, n))
        R.act[0, :, cols] = (grad * R.act[0, :, cols].astype(F32)).astype(BF)
        R.act[1, :, cols] = (grad * R.act[1, :, cols].astype(F32)).astype(BF)

    @pl.loop(0, 8, unroll=4)
    def _(n):
        at = block(n)
        v = mm_tb(R.act[0], R.wm[at + (slice(0, 768),)].reshape(256, 768))
        v = v + mm_tb(R.act[1], R.wm[at + (slice(768, 1536),)].reshape(256, 768))
        cols, v = spread(n, v)
        R.pb[:, :, :, cols] = v

    rs2 = reduce_rows(R.pb, R.rsib, R.rz)
    rs_f = reduce_rows(R.pb2, R.rsib, R.rz)
    rs2.s0()

    def feed_weights(n):
        at = block(n)
        t = turned(R.nm, n)
        R.wm[at + (slice(0, 768),)] = mm(t, R.act[0]).astype(BF).reshape(4, 2, 32, 768)
        R.wm[at + (slice(768, 1536),)] = mm(t, R.act[1]).astype(BF).reshape(4, 2, 32, 768)

    pl.loop(0, 4, unroll=4)(feed_weights)
    rs2.s1()
    rs_d.onward()
    pl.loop(4, 8, unroll=4)(feed_weights)
    rs2.s2()

    def tell(devices, sem):
        for d in devices:
            pl.semaphore_signal(sem, inc=1, device_id=d, device_id_type=MESH)

    group = [sib] + zdev
    ring = xdev[:2] + ydev[:2]
    ag_n.end()
    tell(group, R.free.at[0])
    ag_h = gather_rows(R.nm)
    rs_m.start()

    @pl.loop(0, 8, unroll=4)
    def _(n):
        w = R.wm[block(n) + (slice(1536, 2304),)].reshape(256, 768)
        cols, v = spread(n, mm_tb(R.act[2], w))
        R.pb2[:, :, :, cols] = v

    R.dgs[...] = jnp.zeros((2, WIDTH), F32)
    ag_c[3]()
    rs2.s3()
    pl.semaphore_wait(R.free.at[0], 4)

    @pl.loop(0, 4)
    def _(t):
        rows = owned(t)
        dv, dg = rms_back(R.hid[rows], R.fgain[...], rs2.total(rows))
        dh = dv + R.ct[pl.ds(pl.multiple_of(zh * 64 + t * 16, 16), 16), :].astype(F32)
        R.dgs[1:2, :] += dg
        R.gh[rows] = dh
        R.nm[me, zh, rows] = dh.astype(BF)

    rs2.end()
    ag_h.s0()
    rs_d.t3()
    ag_h.s1()
    rs_m.onward()
    ag_h.s2()
    ag_h.s3()
    rs_f.s0()

    @pl.loop(0, 2)
    def _(zi):
        w = R.wo[:, :, :, :, :, 0:256].reshape(WIDTH, 256)
        both = mm(R.nm[pl.ds(zi * 2, 2)].reshape(256, WIDTH), w)
        for ci in (0, 1):
            i, grad = zi * 2 + ci, both[ci * 128 : (ci + 1) * 128]
            logits = jnp.zeros((128, 128), F32)
            for h in (0, 1):
                gate = jax.nn.sigmoid(R.gl[i][:, h : h + 1])
                gr = grad[:, h * 128 : (h + 1) * 128]
                a = R.att[i, :, h * 128 : (h + 1) * 128]
                low = (gr * gate).astype(BF)
                dl = jnp.sum(gr * a, axis=1, keepdims=True) * (gate * (1.0 - gate))
                logits = jnp.where(lanes == h, dl, logits)
                delta = jnp.sum(low.astype(F32) * a, axis=1, keepdims=True)
                R.dox[zi, h, ci, :, 0:128] = low
                R.dox[zi, h, ci, :, 128:256] = three_parts(-delta, lanes)
            R.gsc[i, :, 512:640] = logits.astype(BF)

    rs_d.t4()
    rs_f.s1()

    R.oacc[...] = jnp.zeros((2, 512, 256), F32)
    row_t = lax.broadcasted_iota(jnp.int32, (256, 512), 1)
    key_t = lax.broadcasted_iota(jnp.int32, (256, 512), 0)
    seen_t = key_t <= lax.rem(row_t, 256)

    def backward(tiles):
        at = [u[0] for u in tiles]
        k = [keys_of(u) for u in at]
        kx = [jnp.concatenate([u, ones], axis=1) for u in k]
        vx = [values_of(u) for u in at]
        kt = [u.T for u in k]
        q = [R.qx[g].reshape(512, 256) for g in (0, 1)]
        d = [R.dox[g].reshape(512, 256) for g in (0, 1)]
        units = [(i, g, u[2] == g) for i, u in enumerate(tiles) for g in u[1]]
        p = [mm_tb(kx[i], q[g]) for i, g, _ in units]
        dp = [mm_tb(vx[i], d[g]) for i, g, _ in units]
        p = [jnp.exp2(u) for u in p]
        p = [jnp.where(seen_t, u, 0.0) if cut else u for u, (_, _, cut) in zip(p, units)]
        ds = [(u * w).astype(BF) for u, w in zip(p, dp)]
        p = [u.astype(BF) for u in p]
        dv = [mm(u, d[g][:, 0:128]) for u, (_, g, _) in zip(p, units)]
        dk = [mm(u, q[g][:, 0:128]) for u, (_, g, _) in zip(ds, units)]
        dq = [mm(kt[i], u) for u, (i, _, _) in zip(ds, units)]
        for g in (0, 1):
            mine = [u for u, (_, h, _) in zip(dq, units) if h == g]
            if mine:
                total = sum(mine[1:], mine[0])
                R.oacc[g, 0:128] += total[:, 0:256]
                R.oacc[g, 128:256] += total[:, 256:512]
        for i, place in enumerate(at):
            mine = [n for n, u in enumerate(units) if u[0] == i]
            first, rest = mine[0], mine[1:]
            total = sum([dk[n] for n in rest], dk[first])
            R.kv[place + (ALL, ALL, slice(0, 128))] = total.astype(BF).reshape(2, 128, 128)
            total = sum([dv[n] for n in rest], dv[first])
            R.kv[place + (ALL, ALL, slice(128, 256))] = total.astype(BF).reshape(2, 128, 128)

    def nothing(at):
        R.kv[at] = jnp.zeros((2, 128, 256), BF)

    small = (R.k_r2, R.k_r1, R.k_q2, R.k_q1)
    rs_k = scatter(R.kv, small, rings[4], slice(0, 256))
    side(backward, 2, nothing)
    rs_k.t0()
    side(backward, 1, nothing)
    rs_k.t1(0)
    side(backward, 3, nothing)
    rs_k.t1(1)
    rs_f.s2()
    rs_k.t2(0)
    rs_k.t2(1)
    rs_m.t3()
    rs_d.t5()
    tell(ring, R.free.at[2])
    R.wm[:, y, x, :, :, 1536:2304] = R.ga[:, y, x, :, :, 0:768]
    near(backward, nothing)
    backward(own)
    rs_f.s3()
    tw_o = twin(R.ob)

    @pl.loop(0, 4)
    def _(t):
        rows = owned(t)
        R.ob[zh, rows] = (R.hid[rows] + rs_f.total(rows)).astype(BF)

    rs_f.end()
    tell(group, R.free.at[1])
    tw_o[0]()

    rs_k.t3()

    R.dgh[...] = jnp.zeros((8, 128), F32)

    @pl.loop(0, 4)
    def _(i):
        zi, ci = lax.div(i, 2), lax.rem(i, 2)
        for h in (0, 1):
            cols = pl.ds(pl.multiple_of(ci * 128, 128), 128)
            dq = R.oacc[zi, h * 128 : (h + 1) * 128, cols].T * SCALE
            dq = rope_back(dq, R.cos[i], R.sin[i])
            dv, dg = rms_back(R.qraw[i, :, h * 128 : (h + 1) * 128], R.qg[...], dq)
            R.dgh[0:1, :] += dg
            R.gsc[i, :, h * 128 : (h + 1) * 128] = dv.astype(BF)

    rs_m.t4()

    @pl.loop(0, 8, unroll=4)
    def _(n):
        at = block(n)
        g = mm(turned(R.nm, n), R.gated[...].reshape(512, 256))
        R.ga[at + (slice(0, 256),)] = g.astype(BF).reshape(4, 2, 32, 256)
        t = turned(R.xn, n)
        g = mm(t, R.gsc[:, :, 0:256].reshape(512, 256))
        R.ga[at + (slice(256, 512),)] = g.astype(BF).reshape(4, 2, 32, 256)
        g = mm(t, R.gsc[:, :, 512:640].reshape(512, 128))
        R.ga[at + (slice(512, 640),)] = g.astype(BF).reshape(4, 2, 32, 128)

    rs_e = scatter(R.ga, big, rings[2], slice(0, 640))
    pl.semaphore_wait(R.free.at[2], 4)
    rs_k.t4()
    rs_e.start()
    rs_k.t5()

    @pl.loop(0, 4)
    def _(i):
        zi, ci = lax.div(i, 2), lax.rem(i, 2)
        dk = R.kv[zi, y, x, ci, :, 0:128].astype(F32) * LN2
        dk = rope_back(dk, R.cos[i], R.sin[i])
        dv, dg = rms_back(R.kraw[i], R.kg[...], dk)
        R.dgh[1:2, :] += dg
        R.gsc[i, :, 256:384] = dv.astype(BF)
        R.gsc[i, :, 384:512] = R.kv[zi, y, x, ci, :, 128:256]

    @pl.loop(0, 8, unroll=4)
    def _(n):
        g = mm(turned(R.xn, n), R.gsc[:, :, 256:512].reshape(512, 256))
        R.ga[block(n) + (slice(640, 896),)] = g.astype(BF).reshape(4, 2, 32, 256)

    rs_l = scatter(R.ga, small, rings[3], slice(640, 896), slice(0, 256), slice(0, 32))
    rs_l.start()
    rs_m.t5()
    gb_m = give_back(R.wm, R.wlm, pairs[0])
    gb_m[0]()

    @pl.loop(0, 8, unroll=4)
    def _(n):
        at = block(n)
        v = mm_tb(R.gsc[:, :, 0:512].reshape(512, 512), R.wa[at].reshape(256, PROJ))
        w = R.wo[at + (slice(256, 384),)].reshape(256, 128)
        v = v + mm_tb(R.gsc[:, :, 512:640].reshape(512, 128), w)
        cols = pl.ds(pl.multiple_of(n * 256, 256), 256)
        dg = jnp.sum(v * R.xn[:, :, :, cols].reshape(512, 256).astype(F32), axis=0, keepdims=True)
        R.dgs[0:1, cols] = dg / R.ag[:, cols]
        cols, v = spread(n, v)
        R.pb[:, :, :, cols] = v

    rs3 = reduce_rows(R.pb, R.rsib, R.rz)
    pl.semaphore_wait(R.free.at[1], 4)
    rs3.s0()

    for r in range(16):
        R.sums[0, r : r + 1, :] = R.dgs[0:1, r * 128 : (r + 1) * 128]
        R.sums[0, 16 + r : 17 + r, :] = R.dgs[1:2, r * 128 : (r + 1) * 128]
    R.sums[0, 32:40, :] = R.dgh[...]

    def add_up(stage, devices):
        g, first = Group(len(devices)), (0, 7, 10)[stage]
        for i, d in enumerate(devices):
            g.go(R.sums.at[stage], R.came.at[first + i], d, i)

        def finish():
            v = R.sums[stage]
            for i in range(len(devices)):
                g.got(R.came.at[first + i], i)
                v = v + R.came[first + i]
            R.sums[stage + 1] = v
            g.end()

        return finish

    fin = add_up(0, group + zsib)
    rs_e.onward()
    rs3.s1()
    rs_l.onward()
    rs3.s2()
    fin()
    fin = add_up(1, xdev)
    rs_e.t3()
    fin()
    fin = add_up(2, ydev)
    rs_l.t3()
    rs3.s3()
    tw_i = twin(R.ib)

    @pl.loop(0, 4)
    def _(t):
        rows = owned(t)
        v = R.x[pl.ds(pl.multiple_of(zh * 64 + t * 16, 16), 16), :].astype(F32)
        dv, _ = rms_back(v, R.ag[...], rs3.total(rows))
        R.ib[zh, rows] = (R.gh[rows] + dv).astype(BF)

    tw_i[0]()
    rs3.end()
    rs_e.t4()
    rs_l.t4()
    def put(i, src, dst):
        cp = pltpu.make_async_copy(src, dst, R.put.at[i])
        cp.start()
        return cp

    gb_m[1]()
    puts = [put(0, R.wlm, R.o_fm)]
    tw_o[1]()
    puts.append(put(1, R.ob, R.o_out))
    fin()
    puts.append(put(2, R.sums.at[3], R.o_gain))
    rs_e.t5()
    rs_l.t5()
    gb_a = give_back(R.ga, R.wl8, pairs[1])
    gb_a[0]()
    tw_i[1]()
    puts.append(put(3, R.ib, R.o_in))
    gb_a[1]()
    puts.append(put(4, R.wl8, R.o_fa))
    for cp in puts:
        cp.wait()
    ag_x[3]()
    ag_h.end()
    gb_m[2]()
    gb_a[2]()
    assert count[0] == COPIES, count


INPUTS = [
    *("x", "ct", "ag", "qg", "kg", "fgain"),
    *("qw", "kw", "vw", "gw", "ow", "fg", "fu", "fd"),
    *("cr", "sr", "cb", "sb"),
]
OUTPUTS = [
    ("o_out", (2, 64, WIDTH), BF),
    ("o_in", (2, 64, WIDTH), BF),
    ("o_gain", (40, 128), F32),
    ("o_fm", (4, 32, 2304), BF),
    ("o_fa", (4, 32, ATT), BF),
]
RESULTS = [
    ((128, WIDTH), BF),
    ((128, WIDTH), BF),
    ((1, 32), F32),
    ((32, 1024), F32),
    ((32, 512), F32),
    ((32, 512), F32),
    ((8, 32), F32),
    ((1, 128), F32),
    ((1, 128), F32),
    ((32, 1024), F32),
    ((1, 32), F32),
    ((32, 3072), F32),
    ((32, 3072), F32),
    ((32, 3072), F32),
]
SCRATCH = [
    ("wla", (4, 32, PROJ), BF),
    ("wlo", (4, 32, 384), BF),
    ("wl8", (4, 32, ATT), BF),
    ("wlm", (4, 32, 2304), BF),
    ("wa", (2, 4, 4, 2, 32, PROJ), BF),
    ("wo", (2, 4, 4, 2, 32, 384), BF),
    ("ga", (2, 4, 4, 2, 32, ATT), BF),
    ("wm", (2, 4, 4, 2, 32, 2304), BF),
    ("kv", (2, 4, 4, 2, 128, 256), BF),
    ("xn", (4, 2, 64, WIDTH), BF),
    ("cot", (4, 2, 64, WIDTH), BF),
    ("nm", (4, 2, 64, WIDTH), BF),
    ("cos", (4, 128, 128), F32),
    ("sin", (4, 128, 128), F32),
    ("qraw", (4, 128, 256), F32),
    ("kraw", (4, 128, 128), F32),
    ("gl", (4, 128, 128), F32),
    ("qx", (2, 2, 2, 128, 256), BF),
    ("dox", (2, 2, 2, 128, 256), BF),
    ("oacc", (2, 512, 256), F32),
    ("att", (4, 128, 256), F32),
    ("gated", (4, 128, 256), BF),
    ("gsc", (4, 128, 640), BF),
    ("act", (3, 512, 768), BF),
    ("hid", (64, WIDTH), F32),
    ("gh", (64, WIDTH), F32),
    ("dgs", (2, WIDTH), F32),
    ("dgh", (8, 128), F32),
    ("pb", (4, 2, 64, WIDTH), BF),
    ("pb2", (4, 2, 64, WIDTH), BF),
    ("rsib", (2, 2, 64, WIDTH), BF),
    ("rz", (3, 64, WIDTH), BF),
    ("m_r2", (2, 2, 4, 32, 2304), BF),
    ("m_r1", (2, 2, 4, 2, 32, 2304), BF),
    ("m_q2", (2, 2, 1, 32, 2304), BF),
    ("m_q1", (2, 2, 1, 2, 32, 2304), BF),
    ("k_r2", (2, 2, 4, 128, 256), BF),
    ("k_r1", (2, 2, 4, 2, 128, 256), BF),
    ("k_q2", (2, 2, 1, 128, 256), BF),
    ("k_q1", (2, 2, 1, 2, 128, 256), BF),
    ("ob", (2, 64, WIDTH), BF),
    ("ib", (2, 64, WIDTH), BF),
    ("sums", (4, 40, 128), F32),
    ("came", (13, 40, 128), F32),
]
COPIES = 175


def kernel(*refs):
    names = INPUTS + [o[0] for o in OUTPUTS] + [v[0] for v in SCRATCH] + ["send", "recv", "free", "put"]
    body(SimpleNamespace(**dict(zip(names, refs))))


def finish(out, grad_in, gain, fm, fa, *to):
    to[0][...] = out[...].reshape(128, WIDTH)
    to[1][...] = grad_in[...].reshape(128, WIDTH)
    place = lax.axis_index("seq")
    for at, first in ((2, 0), (10, 16)):
        v = gain[pl.ds(first + lax.div(place, 4), 1), :]
        to[at][...] = pltpu.roll(v, lax.rem(128 - lax.rem(place, 4) * 32, 128), 1)[:, 0:32]
    to[7][...] = gain[32:33, :]
    to[8][...] = gain[33:34, :]
    gates = jnp.zeros((8, 32), F32)
    for i in range(4):
        wide = slice(i * 256, (i + 1) * 256)
        low = slice(i * 128, (i + 1) * 128)
        to[9][:, wide] = fa[i, :, 0:256].astype(F32)
        to[3][:, wide] = fa[i, :, 256:512].astype(F32)
        to[4][:, low] = fa[i, :, 640:768].astype(F32)
        to[5][:, low] = fa[i, :, 768:896].astype(F32)
        pick = select(lambda r, q, i=i: (r == q + 2 * i) & (q < 2), (8, 128))
        gates = gates + mm_tb(pick, fa[i, :, 512:640])
        for k in range(3):
            cols = slice(k * 768, (k + 1) * 768)
            to[11 + k][:, i * 768 : (i + 1) * 768] = fm[i, :, cols].astype(F32)
    to[6][...] = gates


def rope_tables():
    inverse = ROPE_BASE ** (-np.arange(HEAD // 2) * 2.0 / HEAD)
    inverse = np.concatenate([inverse, inverse]).astype(np.float32).astype(np.float64)
    rows = np.arange(128)[:, None] * inverse
    blocks = np.arange(64)[:, None] * 128 * inverse
    return [jnp.asarray(f(a), F32) for a in (rows, blocks) for f in (np.cos, np.sin)]


def per_device(
    inputs,
    attention_gain,
    query_weight,
    key_matrix,
    value_matrix,
    gate_weight,
    query_gain,
    key_gain,
    out_weight,
    feed_gain,
    feed_gate,
    feed_up,
    feed_down,
    cotangent,
):
    vmem = pl.BlockSpec(memory_space=pltpu.VMEM)
    out = pl.pallas_call(
        kernel,
        out_shape=[jax.ShapeDtypeStruct(shape, kind) for _, shape, kind in OUTPUTS],
        in_specs=[vmem] * len(INPUTS),
        out_specs=[pl.BlockSpec(memory_space=pl.ANY)] * len(OUTPUTS),
        scratch_shapes=[pltpu.VMEM(shape, kind) for _, shape, kind in SCRATCH]
        + [pltpu.SemaphoreType.DMA((COPIES,)), pltpu.SemaphoreType.DMA((COPIES,))]
        + [pltpu.SemaphoreType.REGULAR((3,)), pltpu.SemaphoreType.DMA((5,))],
        compiler_params=pltpu.CompilerParams(
            collective_id=0, has_side_effects=True, vmem_limit_bytes=63 * 2**20
        ),
        name="block",
    )(
        inputs,
        cotangent,
        attention_gain.reshape(1, WIDTH),
        query_gain.reshape(1, HEAD),
        key_gain.reshape(1, HEAD),
        feed_gain.reshape(1, WIDTH),
        query_weight,
        key_matrix,
        value_matrix,
        gate_weight.T,
        out_weight.T,
        feed_gate,
        feed_up,
        feed_down.T,
        *rope_tables(),
    )
    out = pl.pallas_call(
        finish,
        out_shape=[jax.ShapeDtypeStruct(shape, kind) for shape, kind in RESULTS],
        compiler_params=pltpu.CompilerParams(vmem_limit_bytes=60 * 2**20),
        name="results",
    )(*out)
    out = list(out)
    for i in (2, 7, 8, 10):
        out[i] = out[i].reshape(-1)
    for i in (6, 9, 13):
        out[i] = out[i].T
    return tuple(out)


def solution(mesh):
    seq, both, turned = P("seq", None), P("seq", "grp"), P("grp", "seq")
    in_specs = (seq, P(), both, both, both, both, P(), P(), turned, P(), both, both, turned, seq)
    out_specs = (
        seq, seq, P("seq"), both, both, both, both, P(), P(), turned, P("seq"), both, both, turned,
    )
    return jax.shard_map(
        per_device, mesh=mesh, in_specs=in_specs, out_specs=out_specs, check_vma=False
    )
```

```python
from types import SimpleNamespace

import jax
import jax.numpy as jnp
import numpy as np
from jax import lax
from jax.experimental import pallas as pl
from jax.experimental.pallas import tpu as pltpu
from jax.sharding import PartitionSpec as P

EPSILON = 1e-06
ROPE_BASE = 1000000.0
WIDTH = 2048
HEAD = 128
EIGHTH = 768
ATT = 896
PROJ = 512
SCALE = HEAD**-0.5
LOG2E = 1.4426950408889634
LN2 = 0.6931471805599453
BF, F32 = jnp.bfloat16, jnp.float32
MESH = pl.DeviceIdType.MESH
ALL = slice(None)


def mm(a, b):
    return jnp.dot(a, b, preferred_element_type=F32)


def mm_tb(a, b):
    return lax.dot_general(a, b, (((1,), (1,)), ((), ())), preferred_element_type=F32)


def rms_scale(v):
    return lax.rsqrt(jnp.mean(v * v, axis=-1, keepdims=True) + EPSILON)


def rms_back(v, gain, dy):
    r = rms_scale(v)
    u = gain * dy
    dv = r * (u - v * (r * r * jnp.mean(u * v, axis=-1, keepdims=True)))
    return dv, jnp.sum(dy * v * r, axis=0, keepdims=True)


def rope(v, cos, sin):
    return v * cos + pltpu.roll(v, HEAD // 2, 1) * sin


def rope_back(v, cos, sin):
    return v * cos + pltpu.roll(v * sin, HEAD // 2, 1)


def three_parts(v, lanes):
    hi = v.astype(BF).astype(F32)
    mid = (v - hi).astype(BF).astype(F32)
    low = v - hi - mid
    return jnp.where(
        lanes == 0, hi, jnp.where(lanes == 1, mid, jnp.where(lanes == 2, low, 0.0))
    ).astype(BF)


def select(row_of, shape):
    row = lax.broadcasted_iota(jnp.int32, shape, 0)
    col = lax.broadcasted_iota(jnp.int32, shape, 1)
    return jnp.where(row_of(row, col), 1.0, 0.0).astype(BF)


def body(R):
    s, zh = lax.axis_index("seq"), lax.axis_index("grp")
    c = lax.rem(s, 2)
    x = lax.rem(lax.div(s, 2), 4)
    y = lax.rem(lax.div(s, 8), 4)
    zl = lax.div(s, 32)
    z = zh * 2 + zl
    j = y * 4 + x
    me = zl * 2 + c

    def up(v, k):
        return lax.rem(v + k, 4)

    def dev(zz, yy, xx, cc):
        return (lax.rem(zz, 2) * 32 + yy * 8 + xx * 2 + cc, lax.div(zz, 2))

    sib = dev(z, y, x, 1 - c)
    zs = [up(z, 1), up(z, 3), up(z, 2)]
    zdev = [dev(v, y, x, c) for v in zs]
    part = (zl_dev := (1 - zl) * 32 + y * 8 + x * 2 + c, zh)
    diag = ((1 - zl) * 32 + y * 8 + x * 2 + 1 - c, zh)
    other = (zl_dev, 1 - zh)
    xdev = [dev(z, y, up(x, k), c) for k in (1, 3, 2)]
    ydev = [dev(z, up(y, k), x, c) for k in (1, 3, 2)]

    barrier = pltpu.get_barrier_semaphore()
    zsib = [dev(v, y, x, 1 - c) for v in zs]
    greet = [sib] + zdev + zsib + xdev + ydev
    for d in greet:
        pl.semaphore_signal(barrier, inc=1, device_id=d, device_id_type=MESH)

    count = [0]

    def ids(k):
        count[0] += k
        return count[0] - k

    class Group:
        def __init__(self, k, base=None):
            self.base, self.sent = ids(k) if base is None else base, []

        def copy(self, src, dst, d, i):
            i += self.base
            return pltpu.make_async_remote_copy(
                src_ref=src, dst_ref=dst, send_sem=R.send.at[i], recv_sem=R.recv.at[i],
                device_id=d, device_id_type=MESH,
            )

        def run(self, ends, d, i):
            self.copy(*ends(), d, i).start()
            self.sent.append(lambda: self.copy(*ends(), d, i))

        def go(self, src, dst, d, i):
            self.run(lambda: (src, dst), d, i)

        def got(self, ref, i):
            self.copy(ref, ref, sib, i).wait_recv()

        def end(self):
            for cp in self.sent:
                cp().wait_send()

    def exchange(buf, wl, base, cs=ALL):
        g = Group(3, base)

        def start():
            buf[zl, y, x, c, :, cs] = wl[me, :, cs]
            dst = buf.at[zl, y, x, c, :, cs]
            g.go(wl.at[zl * 2 + 1 - c, :, cs], dst, sib, 0)
            g.go(wl.at[(1 - zl) * 2 + c, :, cs], dst, part, 1)
            g.go(wl.at[(1 - zl) * 2 + 1 - c, :, cs], dst, diag, 2)

        def wait():
            g.got(buf.at[zl, y, x, 1 - c, :, cs], 0)
            g.got(buf.at[1 - zl, y, x, c, :, cs], 1)
            g.got(buf.at[1 - zl, y, x, 1 - c, :, cs], 2)

        return start, wait, g.end

    def give_back(src, dst, base):
        g = Group(3, base)

        def start():
            dst[me] = src[zl, y, x, c]
            g.go(src.at[zl, y, x, 1 - c], dst.at[me], sib, 0)
            g.go(src.at[1 - zl, y, x, c], dst.at[me], part, 1)
            g.go(src.at[1 - zl, y, x, 1 - c], dst.at[me], diag, 2)

        def wait():
            g.got(dst.at[zl * 2 + 1 - c], 0)
            g.got(dst.at[(1 - zl) * 2 + c], 1)
            g.got(dst.at[(1 - zl) * 2 + 1 - c], 2)

        return start, wait, g.end

    a_y = SimpleNamespace(
        full=lambda p: (0, p), half=lambda p, h: (0, p, ALL, h), elem=lambda p, k, h: (0, p, k, h),
        k=4, pos=y, dev=ydev,
    )
    a_x = SimpleNamespace(
        full=lambda p: (0, y, p), half=lambda p, h: (0, y, p, h), elem=lambda p, k, h: (0, y, p, h),
        k=1, pos=x, dev=xdev,
    )
    b_x = SimpleNamespace(
        full=lambda p: (1, ALL, p), half=lambda p, h: (1, ALL, p, h), elem=lambda p, k, h: (1, k, p, h),
        k=4, pos=x, dev=xdev,
    )
    b_y = SimpleNamespace(
        full=lambda p: (1, p, x), half=lambda p, h: (1, p, x, h), elem=lambda p, k, h: (1, p, x, h),
        k=1, pos=y, dev=ydev,
    )

    def gather_ring(buf, a, cs, base):
        g, p = Group(6, base), a.pos
        left, right, across = up(p, 3), up(p, 1), up(p, 2)

        def half(q, h):
            at = a.half(q, h)
            return buf.at[at if cs is None else at + (ALL,) * (5 - len(at)) + (cs,)]

        def s1():
            for i, (h, d) in enumerate(((0, 0), (1, 1), (1, 0), (0, 1))):
                g.run(lambda h=h: (half(p, h), half(p, h)), a.dev[d], i)

        def s2():
            g.got(half(left, 0), 0)
            g.run(lambda: (half(left, 0), half(left, 0)), a.dev[0], 4)
            g.got(half(right, 1), 1)
            g.run(lambda: (half(right, 1), half(right, 1)), a.dev[1], 5)

        def s3():
            g.got(half(left, 1), 2)
            g.got(half(right, 0), 3)

        def s4():
            g.got(half(across, 0), 4)
            g.got(half(across, 1), 5)

        return s1, s2, s3, s4, g.end

    def gather(buf, base, cs=None):
        one = [gather_ring(buf, a_x, cs, base), gather_ring(buf, b_y, cs, base + 6)]
        two = [gather_ring(buf, a_y, cs, base + 12), gather_ring(buf, b_x, cs, base + 18)]

        def t1():
            for r in one:
                r[0]()

        def t2():
            for r in one:
                r[1]()

        def t3():
            for r, q in zip(one, two):
                r[2]()
                r[3]()
                q[0]()

        def t4():
            for r in two:
                r[1]()

        def t5():
            for r in two:
                r[2]()

        def t6():
            for r in two:
                r[3]()
            for r in one + two:
                r[4]()

        return t1, t2, t3, t4, t5, t6

    def reduce_ring(buf, a, r2, r1, cs, bs, rows, base):
        g, p, k = Group(6, base), a.pos, a.k
        first = ALL if k == 4 else 0
        across, beside = up(p, 2), (up(p, 1), up(p, 3))

        def half(q, h):
            at = a.half(q, h)
            return buf.at[at + (ALL,) * (5 - len(at)) + (cs,)]

        def elem(q, n, h):
            return a.elem(q, n, h) + (ALL, cs)

        def far(i):
            return r2.at[i, first, rows, bs]

        def near(i, h):
            return r1.at[i, first, h, rows, bs]

        def loop(fn):
            if k == 1:
                fn(0)
            else:
                pl.loop(0, k)(fn)

        def s1():
            for i in (0, 1):
                g.run(lambda i=i: (half(across, i), far(i)), a.dev[i], i)

        def direct(i):
            g.run(lambda: (half(beside[i], 1 - i), near(i, 1 - i)), a.dev[i], 2 + i)

        def s2(i):
            g.got(far(i), i)
            to = beside[i]

            def add(n):
                at = elem(to, n, i)
                buf[at] = buf[at] + r2[i, n, rows, bs]

            loop(add)
            g.run(lambda: (half(to, i), near(i, i)), a.dev[i], 4 + i)

        def s3():
            for i in (0, 1):
                g.got(near(i, 1 - i), 2 + i)
                g.got(near(i, i), 4 + i)

            def add(n):
                for h in (0, 1):
                    at = elem(p, n, h)
                    total = (
                        buf[at].astype(F32)
                        + r1[0, n, h, rows, bs].astype(F32)
                        + r1[1, n, h, rows, bs].astype(F32)
                    )
                    buf[at] = total.astype(BF)

            loop(add)

        return s1, direct, s2, s3, g.end

    def scatter(buf, bufs, base, cs, bs=None, rows=ALL):
        bs = cs if bs is None else bs
        one = [
            reduce_ring(buf, a_y, bufs[0].at[0], bufs[1].at[0], cs, bs, rows, base),
            reduce_ring(buf, b_x, bufs[0].at[1], bufs[1].at[1], cs, bs, rows, base + 6),
        ]
        two = [
            reduce_ring(buf, a_x, bufs[2].at[0], bufs[3].at[0], cs, bs, rows, base + 12),
            reduce_ring(buf, b_y, bufs[2].at[1], bufs[3].at[1], cs, bs, rows, base + 18),
        ]

        def t0():
            for r in one:
                r[0]()

        def t1(i):
            for r in one:
                r[1](i)

        def t2(i):
            for r in one:
                r[2](i)

        def t3():
            for r, q in zip(one, two):
                r[3]()
                q[0]()
                q[1](0)
                q[1](1)

        def t4():
            for i in (0, 1):
                for r in two:
                    r[2](i)

        def t5():
            for r in two:
                r[3]()
            for r in one + two:
                r[4]()

        def start():
            t0()
            t1(0)
            t1(1)

        def onward():
            t2(0)
            t2(1)

        return SimpleNamespace(t0=t0, t1=t1, t2=t2, t3=t3, t4=t4, t5=t5, start=start, onward=onward)

    def place(zz, cc):
        return (lax.rem(zz, 2) * 2 + cc, lax.div(zz, 2))

    half_rows = (slice(0, 32), slice(32, 64))

    rows_base = ids(8)

    def reduce_rows(pb, rsib, rz):
        g = Group(8, rows_base)

        def mine(zz, h):
            return pb.at[place(zz, c) + (half_rows[h],)]

        def s0():
            for i, t in enumerate((zl, 1 - zl)):
                g.go(pb.at[t * 2 + 1 - c], rsib.at[t], sib, i)

        def s1():
            def add(zz):
                at = place(zz, c)
                pb[at] = pb[at] + rsib[lax.rem(zz, 2), lax.div(zz, 2)]

            g.got(rsib.at[zl], 0)
            add(zs[2])
            for i in (0, 1):
                g.go(mine(zs[2], i), rz.at[2, half_rows[i]], zdev[i], 2 + i)
            g.got(rsib.at[1 - zl], 1)
            for i in (0, 1):
                add(zs[i])
                g.go(mine(zs[i], 1 - i), rz.at[i, half_rows[1 - i]], zdev[i], 4 + i)
            add(z)

        def s2():
            for i in (0, 1):
                rows = half_rows[i]
                g.got(rz.at[2, rows], 2 + i)
                at = place(zs[i], c) + (rows,)
                pb[at] = pb[at] + rz[2, rows]
                g.go(mine(zs[i], i), rz.at[i, rows], zdev[i], 6 + i)

        def s3():
            for i in (0, 1):
                g.got(rz.at[i, half_rows[1 - i]], 4 + i)
                g.got(rz.at[i, half_rows[i]], 6 + i)

        def total(rows):
            v = pb[me, zh, rows].astype(F32)
            return v + rz[0, rows].astype(F32) + rz[1, rows].astype(F32)

        return SimpleNamespace(s0=s0, s1=s1, s2=s2, s3=s3, end=g.end, total=total)

    spread_base = ids(10)

    def gather_rows(buf):
        g = Group(10, spread_base)

        def at(zz, h):
            return buf.at[place(zz, c) + (half_rows[h],)]

        def s0():
            for i, (h, d) in enumerate(((0, 0), (1, 1), (1, 0), (0, 1))):
                g.go(at(z, h), at(z, h), zdev[d], i)
            own = buf.at[place(z, c)]
            g.go(own, own, sib, 6)

        def s1():
            g.got(at(zs[1], 0), 0)
            g.go(at(zs[1], 0), at(zs[1], 0), zdev[0], 4)
            g.got(at(zs[0], 1), 1)
            g.go(at(zs[0], 1), at(zs[0], 1), zdev[1], 5)

        def s2():
            def hand_on(zz, i):
                whole = buf.at[place(zz, c)]
                g.go(whole, whole, sib, i)

            g.got(at(zs[1], 1), 2)
            hand_on(zs[1], 7)
            g.got(at(zs[0], 0), 3)
            hand_on(zs[0], 8)
            g.got(at(zs[2], 0), 4)
            g.got(at(zs[2], 1), 5)
            hand_on(zs[2], 9)

        def s3():
            for i, zz in ((6, z), (7, zs[1]), (8, zs[0]), (9, zs[2])):
                g.got(buf.at[place(zz, 1 - c)], i)

        return SimpleNamespace(s0=s0, s1=s1, s2=s2, s3=s3, end=g.end)

    def gather_blocks(buf):
        g = Group(5)

        def s0():
            g.go(buf.at[me, 0], buf.at[me, 0], part, 0)
            g.go(buf.at[me, 1], buf.at[me, 1], other, 1)
            g.go(buf.at[me], buf.at[me], sib, 2)

        def s1():
            for h in (0, 1):
                at = buf.at[(1 - zl) * 2 + c, h]
                g.got(at, h)
                g.go(at, at, sib, 3 + h)

        def s2():
            g.got(buf.at[zl * 2 + 1 - c], 2)
            for h in (0, 1):
                g.got(buf.at[(1 - zl) * 2 + 1 - c, h], 3 + h)

        return s0, s1, s2, g.end

    def twin(buf):
        g = Group(1)

        def start():
            g.go(buf.at[zh], buf.at[zh], zdev[2], 0)

        def wait():
            g.got(buf.at[1 - zh], 0)
            g.end()

        return start, wait

    for i in range(4):
        R.wla[i, :, 0:256] = R.qw[:, i * 256 : (i + 1) * 256]
        R.wla[i, :, 256:384] = R.kw[:, i * 128 : (i + 1) * 128]
        R.wla[i, :, 384:512] = R.vw[:, i * 128 : (i + 1) * 128]
    pairs, rings = [ids(3) for _ in range(4)], [ids(24) for _ in range(5)]
    ex_a = exchange(R.wa, R.wla, pairs[0])
    ex_o = exchange(R.wo, R.wlo, pairs[1])
    ex_m = exchange(R.wm, R.wlm, pairs[2], slice(0, 1536))
    ex_d = exchange(R.wm, R.wlm, pairs[3], slice(1536, 2304))
    ag_a, ag_o = gather(R.wa, rings[0]), gather(R.wo, rings[1])
    ag_m = gather(R.wm, rings[2], slice(0, 1536))
    ag_d = gather(R.wm, rings[3], slice(1536, 2304))
    ag_x = gather_blocks(R.xn)
    ag_c = gather_blocks(R.cot)
    ag_kv = gather(R.kv, rings[4])

    pl.semaphore_wait(barrier, len(greet))
    ex_a[0]()
    for i in range(4):
        R.wlo[i, :, 0:256] = R.ow[:, i * 256 : (i + 1) * 256]
        pick = select(lambda r, q, i=i: (r == q + 2 * i) & (q < 2), (8, 128))
        R.wlo[i, :, 256:384] = mm(R.gw[...].T, pick).astype(BF)
        R.wlm[i, :, 1536:2304] = R.fd[:, i * 768 : (i + 1) * 768]
    ex_o[0]()
    ex_d[0]()

    @pl.loop(0, 4)
    def _(t):
        rows = pl.ds(pl.multiple_of(lax.rem(t, 2) * 32, 32), 32)
        v = R.x[pl.ds(pl.multiple_of(t * 32, 32), 32), :].astype(F32)
        R.xn[me, lax.div(t, 2), rows] = (v * rms_scale(v) * R.ag[...]).astype(BF)

    ag_x[0]()
    for i in range(4):
        R.wlm[i, :, 0:768] = R.fg[:, i * 768 : (i + 1) * 768]
        R.wlm[i, :, 768:1536] = R.fu[:, i * 768 : (i + 1) * 768]
    ex_m[0]()
    first = lax.broadcasted_iota(jnp.int32, (128, 128), 1) < 64
    for i in range(4):
        base = (i // 2) * 32 + j * 2 + i % 2
        cb, sb = R.cb[pl.ds(base, 1), :], R.sb[pl.ds(base, 1), :]
        sin = sb * R.cr[...] + cb * R.sr[...]
        R.cos[i] = cb * R.cr[...] - sb * R.sr[...]
        R.sin[i] = jnp.where(first, -sin, sin)
    R.cot[me] = R.ct[...].reshape(2, 64, WIDTH)
    ex_a[1]()
    ag_a[0]()
    ex_o[1]()
    ag_o[0]()
    ag_a[1]()
    ex_d[1]()
    ag_d[0]()
    ag_o[1]()
    ag_x[1]()
    ag_a[2]()
    ag_d[1]()
    ag_x[2]()
    ag_a[3]()
    ex_m[1]()
    ag_m[0]()
    ag_a[4]()
    ag_a[5]()

    @pl.loop(0, 2)
    def _(zi):
        w = R.wa[...].reshape(WIDTH, PROJ)
        both = mm(R.xn[pl.ds(zi * 2, 2)].reshape(256, WIDTH), w)
        for ci in (0, 1):
            i, raw = zi * 2 + ci, both[ci * 128 : (ci + 1) * 128]
            cos, sin = R.cos[i], R.sin[i]
            R.qraw[i] = raw[:, 0:256]
            R.kraw[i] = raw[:, 256:384]
            for h in (0, 1):
                v = raw[:, h * 128 : (h + 1) * 128]
                q = rope(v * rms_scale(v) * R.qg[...], cos, sin) * (SCALE * LOG2E)
                R.qx[zi, h, ci, :, 0:128] = q.astype(BF)
            v = raw[:, 256:384]
            k = rope(v * rms_scale(v) * R.kg[...], cos, sin)
            R.kv[zi, y, x, ci, :, 0:128] = k.astype(BF)
            R.kv[zi, y, x, ci, :, 128:256] = raw[:, 384:512].astype(BF)

    ag_kv[0]()
    ag_c[0]()
    ag_m[1]()

    ones = jnp.ones((256, 128), BF)
    key_i = lax.broadcasted_iota(jnp.int32, (512, 256), 1)
    row_i = lax.broadcasted_iota(jnp.int32, (512, 256), 0)
    seen = key_i <= lax.rem(row_i, 256)
    R.oacc[...] = jnp.zeros((2, 512, 256), F32)

    def keys_of(at):
        return R.kv[at + (ALL, ALL, slice(0, 128))].reshape(256, 128)

    def values_of(at):
        v = R.kv[at + (ALL, ALL, slice(128, 256))].reshape(256, 128)
        return jnp.concatenate([v, ones], axis=1)

    def forward(tiles):
        work = []
        for g in (0, 1):
            mine = [u for u in tiles if g in u[1]]
            if mine:
                k = jnp.concatenate([keys_of(u[0]) for u in mine], axis=0)
                v = jnp.concatenate([values_of(u[0]) for u in mine], axis=0)
                scores = mm_tb(R.qx[g, :, :, :, 0:128].reshape(512, 128), k)
                work.append((g, mine, v, scores))
        for g, mine, v, scores in work:
            p = jnp.exp2(scores)
            if any(u[2] == g for u in mine):
                parts = [p[:, i * 256 : (i + 1) * 256] for i in range(len(mine))]
                parts = [jnp.where(seen, q, 0.0) if u[2] == g else q for u, q in zip(mine, parts)]
                p = jnp.concatenate(parts, axis=1)
            R.oacc[g] += mm(p.astype(BF), v)

    def tile_pair(fn, empty, at0, at1):
        t0, t1 = at0[0] * 4 + at0[1], at1[0] * 4 + at1[1]
        at0, at1 = (0,) + at0, (1,) + at1

        @pl.when((t0 < j) & (t1 < j))
        def _():
            fn([(at0, (0, 1), None), (at1, (1,), None)])

        @pl.when((t0 < j) & (t1 > j))
        def _():
            fn([(at0, (0, 1), None)])

        @pl.when((t0 > j) & (t1 < j))
        def _():
            fn([(at0, (1,), None), (at1, (1,), None)])

        @pl.when((t0 > j) & (t1 > j))
        def _():
            fn([(at0, (1,), None)])

        if empty is not None:

            @pl.when(t1 > j)
            def _():
                empty(at1)

    own = [((0, y, x), (0, 1), 0), ((1, y, x), (1,), 1)]

    def near(fn, empty=None):
        @pl.loop(1, 4)
        def _(k):
            tile_pair(fn, empty, (y, up(x, k)), (up(y, k), x))

    def side(fn, a, empty=None):
        @pl.loop(0, 4)
        def _(k):
            tile_pair(fn, empty, (up(y, a), k), (k, up(x, a)))

    forward(own)
    ag_kv[1]()
    ag_kv[2]()
    near(forward)
    ag_c[1]()
    ag_kv[3]()
    ag_o[2]()
    ag_kv[4]()

    @pl.loop(0, 3)
    def _(k):
        @pl.when(k == 2)
        def _():
            ag_o[3]()
            ag_m[2]()
            ag_kv[5]()

        side(forward, 1 + 2 * k - 3 * lax.div(k, 2))

    ag_o[4]()
    ag_o[5]()

    @pl.loop(0, 2)
    def _(zi):
        w = R.wo[:, :, :, :, :, 256:384].reshape(WIDTH, 128)
        v = mm(R.xn[pl.ds(zi * 2, 2)].reshape(256, WIDTH), w)
        R.gl[pl.ds(zi * 2, 2)] = v.reshape(2, 128, 128)

    lanes = lax.broadcasted_iota(jnp.int32, (128, 128), 1)

    @pl.loop(0, 4)
    def _(i):
        zi, ci = lax.div(i, 2), lax.rem(i, 2)
        for h in (0, 1):
            rows = pl.ds(pl.multiple_of(h * 256 + ci * 128, 128), 128)
            total = R.oacc[zi, rows, 128:256]
            a = R.oacc[zi, rows, 0:128] / total
            R.att[i, :, h * 128 : (h + 1) * 128] = a
            R.qx[zi, h, ci, :, 128:256] = three_parts(-jnp.log2(total), lanes)
            gate = jax.nn.sigmoid(R.gl[i][:, h : h + 1])
            R.gated[i, :, h * 128 : (h + 1) * 128] = (a * gate).astype(BF)

    def spread(n, value):
        cols = pl.ds(pl.multiple_of(n * 256, 256), 256)
        return cols, value.reshape(4, 2, 64, 256).astype(BF)

    rs1 = reduce_rows(R.pb, R.rsib, R.rz)
    ag_n = gather_rows(R.nm)

    def project(cc):
        rows = jnp.concatenate([R.gated[cc], R.gated[2 + cc]], axis=0)

        @pl.loop(0, 8, unroll=4)
        def _(n):
            w = R.wo[lax.div(n, 4), lax.rem(n, 4), :, :, :, 0:256].reshape(256, 256)
            cols = pl.ds(pl.multiple_of(n * 256, 256), 256)
            v = mm_tb(rows, w).astype(BF).reshape(2, 2, 64, 256)
            R.pb[cc, :, :, cols] = v[0]
            R.pb[2 + cc, :, :, cols] = v[1]

    project(1 - c)
    rs1.s0()
    project(c)
    rs1.s1()
    rs1.s2()
    ag_m[3]()
    ag_d[2]()
    rs1.s3()

    def owned(t):
        return pl.ds(pl.multiple_of(t * 16, 16), 16)

    @pl.loop(0, 4)
    def _(t):
        rows = owned(t)
        v = R.x[pl.ds(pl.multiple_of(zh * 64 + t * 16, 16), 16), :].astype(F32)
        v = v + rs1.total(rows)
        R.hid[rows] = v
        R.nm[me, zh, rows] = (v * rms_scale(v) * R.fgain[...]).astype(BF)

    rs1.end()
    for g in (ex_a, ex_o, ex_m, ex_d):
        g[2]()
    ag_n.s0()
    ag_c[2]()
    ag_n.s1()
    ag_m[4]()
    ag_n.s2()
    ag_m[5]()
    ag_d[3]()
    ag_n.s3()

    def weight(k, n):
        at = pl.ds(pl.multiple_of(k * 768 + n * 256, 256), 256)
        return R.wm[:, :, :, :, :, at].reshape(WIDTH, 256)

    @pl.loop(0, 3, unroll=3)
    def _(n):
        cols = pl.ds(pl.multiple_of(n * 256, 256), 256)
        rows = R.nm[...].reshape(512, WIDTH)
        gate = mm(rows, weight(0, n))
        upper = mm(rows, weight(1, n))
        sg = jax.nn.sigmoid(gate)
        silu = gate * sg
        R.act[0, :, cols] = (upper * (sg * (1.0 + gate * (1.0 - sg)))).astype(BF)
        R.act[1, :, cols] = silu.astype(BF)
        R.act[2, :, cols] = (silu * upper).astype(BF)

    def block(n):
        return (lax.div(n, 4), lax.rem(n, 4), ALL, ALL, ALL)

    def turned(ref, n):
        cols = pl.ds(pl.multiple_of(n * 256, 256), 256)
        return ref[:, :, :, cols].reshape(512, 256).T

    big = (R.m_r2, R.m_r1, R.m_q2, R.m_q1)
    rs_d = scatter(R.ga, big, rings[0], slice(0, 768))
    rs_m = scatter(R.wm, big, rings[1], slice(0, 1536), slice(768, 2304))

    @pl.loop(0, 8, unroll=4)
    def _(n):
        g = mm(turned(R.cot, n), R.act[2])
        R.ga[block(n) + (slice(0, 768),)] = g.astype(BF).reshape(4, 2, 32, 768)

    rs_d.start()
    ag_d[4]()
    ag_d[5]()

    @pl.loop(0, 3, unroll=3)
    def _(n):
        cols = pl.ds(pl.multiple_of(n * 256, 256), 256)
        grad = mm(R.cot[...].reshape(512, WIDTH), weight(2, n))
        R.act[0, :, cols] = (grad * R.act[0, :, cols].astype(F32)).astype(BF)
        R.act[1, :, cols] = (grad * R.act[1, :, cols].astype(F32)).astype(BF)

    @pl.loop(0, 8, unroll=4)
    def _(n):
        at = block(n)
        v = mm_tb(R.act[0], R.wm[at + (slice(0, 768),)].reshape(256, 768))
        v = v + mm_tb(R.act[1], R.wm[at + (slice(768, 1536),)].reshape(256, 768))
        cols, v = spread(n, v)
        R.pb[:, :, :, cols] = v

    rs2 = reduce_rows(R.pb, R.rsib, R.rz)
    rs_f = reduce_rows(R.pb2, R.rsib, R.rz)
    rs2.s0()

    def feed_weights(n):
        at = block(n)
        t = turned(R.nm, n)
        R.wm[at + (slice(0, 768),)] = mm(t, R.act[0]).astype(BF).reshape(4, 2, 32, 768)
        R.wm[at + (slice(768, 1536),)] = mm(t, R.act[1]).astype(BF).reshape(4, 2, 32, 768)

    pl.loop(0, 4, unroll=4)(feed_weights)
    rs2.s1()
    rs_d.onward()
    pl.loop(4, 8, unroll=4)(feed_weights)
    rs2.s2()

    def tell(devices, sem):
        for d in devices:
            pl.semaphore_signal(sem, inc=1, device_id=d, device_id_type=MESH)

    group = [sib] + zdev
    ring = xdev[:2] + ydev[:2]
    ag_n.end()
    tell(group, R.free.at[0])
    ag_h = gather_rows(R.nm)
    rs_m.start()

    @pl.loop(0, 8, unroll=4)
    def _(n):
        w = R.wm[block(n) + (slice(1536, 2304),)].reshape(256, 768)
        cols, v = spread(n, mm_tb(R.act[2], w))
        R.pb2[:, :, :, cols] = v

    R.dgs[...] = jnp.zeros((2, WIDTH), F32)
    ag_c[3]()
    rs2.s3()
    pl.semaphore_wait(R.free.at[0], 4)

    @pl.loop(0, 4)
    def _(t):
        rows = owned(t)
        dv, dg = rms_back(R.hid[rows], R.fgain[...], rs2.total(rows))
        dh = dv + R.ct[pl.ds(pl.multiple_of(zh * 64 + t * 16, 16), 16), :].astype(F32)
        R.dgs[1:2, :] += dg
        R.gh[rows] = dh
        R.nm[me, zh, rows] = dh.astype(BF)

    rs2.end()
    ag_h.s0()
    rs_d.t3()
    ag_h.s1()
    rs_m.onward()
    ag_h.s2()
    ag_h.s3()
    rs_f.s0()

    @pl.loop(0, 2)
    def _(zi):
        w = R.wo[:, :, :, :, :, 0:256].reshape(WIDTH, 256)
        both = mm(R.nm[pl.ds(zi * 2, 2)].reshape(256, WIDTH), w)
        for ci in (0, 1):
            i, grad = zi * 2 + ci, both[ci * 128 : (ci + 1) * 128]
            logits = jnp.zeros((128, 128), F32)
            for h in (0, 1):
                gate = jax.nn.sigmoid(R.gl[i][:, h : h + 1])
                gr = grad[:, h * 128 : (h + 1) * 128]
                a = R.att[i, :, h * 128 : (h + 1) * 128]
                low = (gr * gate).astype(BF)
                dl = jnp.sum(gr * a, axis=1, keepdims=True) * (gate * (1.0 - gate))
                logits = jnp.where(lanes == h, dl, logits)
                delta = jnp.sum(low.astype(F32) * a, axis=1, keepdims=True)
                R.dox[zi, h, ci, :, 0:128] = low
                R.dox[zi, h, ci, :, 128:256] = three_parts(-delta, lanes)
            R.gsc[i, :, 512:640] = logits.astype(BF)

    rs_d.t4()
    rs_f.s1()

    R.oacc[...] = jnp.zeros((2, 512, 256), F32)
    row_t = lax.broadcasted_iota(jnp.int32, (256, 512), 1)
    key_t = lax.broadcasted_iota(jnp.int32, (256, 512), 0)
    seen_t = key_t <= lax.rem(row_t, 256)

    def backward(tiles):
        at = [u[0] for u in tiles]
        k = [keys_of(u) for u in at]
        kx = [jnp.concatenate([u, ones], axis=1) for u in k]
        vx = [values_of(u) for u in at]
        kt = [u.T for u in k]
        q = [R.qx[g].reshape(512, 256) for g in (0, 1)]
        d = [R.dox[g].reshape(512, 256) for g in (0, 1)]
        units = [(i, g, u[2] == g) for i, u in enumerate(tiles) for g in u[1]]
        p = [mm_tb(kx[i], q[g]) for i, g, _ in units]
        dp = [mm_tb(vx[i], d[g]) for i, g, _ in units]
        p = [jnp.exp2(u) for u in p]
        p = [jnp.where(seen_t, u, 0.0) if cut else u for u, (_, _, cut) in zip(p, units)]
        ds = [(u * w).astype(BF) for u, w in zip(p, dp)]
        p = [u.astype(BF) for u in p]
        dv = [mm(u, d[g][:, 0:128]) for u, (_, g, _) in zip(p, units)]
        dk = [mm(u, q[g][:, 0:128]) for u, (_, g, _) in zip(ds, units)]
        dq = [mm(kt[i], u) for u, (i, _, _) in zip(ds, units)]
        for g in (0, 1):
            mine = [u for u, (_, h, _) in zip(dq, units) if h == g]
            if mine:
                total = sum(mine[1:], mine[0])
                R.oacc[g, 0:128] += total[:, 0:256]
                R.oacc[g, 128:256] += total[:, 256:512]
        for i, place in enumerate(at):
            mine = [n for n, u in enumerate(units) if u[0] == i]
            first, rest = mine[0], mine[1:]
            total = sum([dk[n] for n in rest], dk[first])
            R.kv[place + (ALL, ALL, slice(0, 128))] = total.astype(BF).reshape(2, 128, 128)
            total = sum([dv[n] for n in rest], dv[first])
            R.kv[place + (ALL, ALL, slice(128, 256))] = total.astype(BF).reshape(2, 128, 128)

    def nothing(at):
        R.kv[at] = jnp.zeros((2, 128, 256), BF)

    small = (R.k_r2, R.k_r1, R.k_q2, R.k_q1)
    rs_k = scatter(R.kv, small, rings[4], slice(0, 256))

    @pl.loop(0, 3)
    def _(k):
        side(backward, 2 - k + 3 * lax.div(k, 2), nothing)

        @pl.when(k == 0)
        def _():
            rs_k.t0()

        @pl.when(k == 1)
        def _():
            rs_k.t1(0)

        @pl.when(k == 2)
        def _():
            rs_k.t1(1)

    rs_f.s2()
    rs_k.t2(0)
    rs_k.t2(1)
    rs_m.t3()
    rs_d.t5()
    tell(ring, R.free.at[2])
    R.wm[:, y, x, :, :, 1536:2304] = R.ga[:, y, x, :, :, 0:768]
    near(backward, nothing)
    backward(own)
    rs_f.s3()
    tw_o = twin(R.ob)

    @pl.loop(0, 4)
    def _(t):
        rows = owned(t)
        R.ob[zh, rows] = (R.hid[rows] + rs_f.total(rows)).astype(BF)

    rs_f.end()
    tell(group, R.free.at[1])
    tw_o[0]()

    rs_k.t3()

    R.dgh[...] = jnp.zeros((8, 128), F32)

    @pl.loop(0, 4)
    def _(i):
        zi, ci = lax.div(i, 2), lax.rem(i, 2)
        for h in (0, 1):
            cols = pl.ds(pl.multiple_of(ci * 128, 128), 128)
            dq = R.oacc[zi, h * 128 : (h + 1) * 128, cols].T * SCALE
            dq = rope_back(dq, R.cos[i], R.sin[i])
            dv, dg = rms_back(R.qraw[i, :, h * 128 : (h + 1) * 128], R.qg[...], dq)
            R.dgh[0:1, :] += dg
            R.gsc[i, :, h * 128 : (h + 1) * 128] = dv.astype(BF)

    rs_m.t4()

    @pl.loop(0, 8, unroll=4)
    def _(n):
        at = block(n)
        g = mm(turned(R.nm, n), R.gated[...].reshape(512, 256))
        R.ga[at + (slice(0, 256),)] = g.astype(BF).reshape(4, 2, 32, 256)
        t = turned(R.xn, n)
        g = mm(t, R.gsc[:, :, 0:256].reshape(512, 256))
        R.ga[at + (slice(256, 512),)] = g.astype(BF).reshape(4, 2, 32, 256)
        g = mm(t, R.gsc[:, :, 512:640].reshape(512, 128))
        R.ga[at + (slice(512, 640),)] = g.astype(BF).reshape(4, 2, 32, 128)

    rs_e = scatter(R.ga, big, rings[2], slice(0, 640))
    pl.semaphore_wait(R.free.at[2], 4)
    rs_k.t4()
    rs_e.start()
    rs_k.t5()

    @pl.loop(0, 4)
    def _(i):
        zi, ci = lax.div(i, 2), lax.rem(i, 2)
        dk = R.kv[zi, y, x, ci, :, 0:128].astype(F32) * LN2
        dk = rope_back(dk, R.cos[i], R.sin[i])
        dv, dg = rms_back(R.kraw[i], R.kg[...], dk)
        R.dgh[1:2, :] += dg
        R.gsc[i, :, 256:384] = dv.astype(BF)
        R.gsc[i, :, 384:512] = R.kv[zi, y, x, ci, :, 128:256]

    @pl.loop(0, 8, unroll=4)
    def _(n):
        g = mm(turned(R.xn, n), R.gsc[:, :, 256:512].reshape(512, 256))
        R.ga[block(n) + (slice(640, 896),)] = g.astype(BF).reshape(4, 2, 32, 256)

    rs_l = scatter(R.ga, small, rings[3], slice(640, 896), slice(0, 256), slice(0, 32))
    rs_l.start()
    rs_m.t5()
    gb_m = give_back(R.wm, R.wlm, pairs[0])
    gb_m[0]()

    @pl.loop(0, 8, unroll=4)
    def _(n):
        at = block(n)
        v = mm_tb(R.gsc[:, :, 0:512].reshape(512, 512), R.wa[at].reshape(256, PROJ))
        w = R.wo[at + (slice(256, 384),)].reshape(256, 128)
        v = v + mm_tb(R.gsc[:, :, 512:640].reshape(512, 128), w)
        cols = pl.ds(pl.multiple_of(n * 256, 256), 256)
        dg = jnp.sum(v * R.xn[:, :, :, cols].reshape(512, 256).astype(F32), axis=0, keepdims=True)
        R.dgs[0:1, cols] = dg / R.ag[:, cols]
        cols, v = spread(n, v)
        R.pb[:, :, :, cols] = v

    rs3 = reduce_rows(R.pb, R.rsib, R.rz)
    pl.semaphore_wait(R.free.at[1], 4)
    rs3.s0()

    for r in range(16):
        R.sums[0, r : r + 1, :] = R.dgs[0:1, r * 128 : (r + 1) * 128]
        R.sums[0, 16 + r : 17 + r, :] = R.dgs[1:2, r * 128 : (r + 1) * 128]
    R.sums[0, 32:40, :] = R.dgh[...]

    def add_up(stage, devices):
        g, first = Group(len(devices)), (0, 7, 10)[stage]
        for i, d in enumerate(devices):
            g.go(R.sums.at[stage], R.came.at[first + i], d, i)

        def finish():
            v = R.sums[stage]
            for i in range(len(devices)):
                g.got(R.came.at[first + i], i)
                v = v + R.came[first + i]
            R.sums[stage + 1] = v
            g.end()

        return finish

    fin = add_up(0, group + zsib)
    rs_e.onward()
    rs3.s1()
    rs_l.onward()
    rs3.s2()
    fin()
    fin = add_up(1, xdev)
    rs_e.t3()
    fin()
    fin = add_up(2, ydev)
    rs_l.t3()
    rs3.s3()
    tw_i = twin(R.ib)

    @pl.loop(0, 4)
    def _(t):
        rows = owned(t)
        v = R.x[pl.ds(pl.multiple_of(zh * 64 + t * 16, 16), 16), :].astype(F32)
        dv, _ = rms_back(v, R.ag[...], rs3.total(rows))
        R.ib[zh, rows] = (R.gh[rows] + dv).astype(BF)

    tw_i[0]()
    rs3.end()
    rs_e.t4()
    rs_l.t4()
    def put(i, src, dst):
        cp = pltpu.make_async_copy(src, dst, R.put.at[i])
        cp.start()
        return cp

    gb_m[1]()
    puts = [put(0, R.wlm, R.o_fm)]
    tw_o[1]()
    puts.append(put(1, R.ob, R.o_out))
    fin()
    puts.append(put(2, R.sums.at[3], R.o_gain))
    rs_e.t5()
    rs_l.t5()
    gb_a = give_back(R.ga, R.wl8, pairs[1])
    gb_a[0]()
    tw_i[1]()
    puts.append(put(3, R.ib, R.o_in))
    gb_a[1]()
    puts.append(put(4, R.wl8, R.o_fa))
    for cp in puts:
        cp.wait()
    ag_x[3]()
    ag_h.end()
    gb_m[2]()
    gb_a[2]()
    assert count[0] == COPIES, count


INPUTS = [
    *("x", "ct", "ag", "qg", "kg", "fgain"),
    *("qw", "kw", "vw", "gw", "ow", "fg", "fu", "fd"),
    *("cr", "sr", "cb", "sb"),
]
OUTPUTS = [
    ("o_out", (2, 64, WIDTH), BF),
    ("o_in", (2, 64, WIDTH), BF),
    ("o_gain", (40, 128), F32),
    ("o_fm", (4, 32, 2304), BF),
    ("o_fa", (4, 32, ATT), BF),
]
RESULTS = [
    ((128, WIDTH), BF),
    ((128, WIDTH), BF),
    ((1, 32), F32),
    ((32, 1024), F32),
    ((32, 512), F32),
    ((32, 512), F32),
    ((8, 32), F32),
    ((1, 128), F32),
    ((1, 128), F32),
    ((32, 1024), F32),
    ((1, 32), F32),
    ((32, 3072), F32),
    ((32, 3072), F32),
    ((32, 3072), F32),
]
SCRATCH = [
    ("wla", (4, 32, PROJ), BF),
    ("wlo", (4, 32, 384), BF),
    ("wl8", (4, 32, ATT), BF),
    ("wlm", (4, 32, 2304), BF),
    ("wa", (2, 4, 4, 2, 32, PROJ), BF),
    ("wo", (2, 4, 4, 2, 32, 384), BF),
    ("ga", (2, 4, 4, 2, 32, ATT), BF),
    ("wm", (2, 4, 4, 2, 32, 2304), BF),
    ("kv", (2, 4, 4, 2, 128, 256), BF),
    ("xn", (4, 2, 64, WIDTH), BF),
    ("cot", (4, 2, 64, WIDTH), BF),
    ("nm", (4, 2, 64, WIDTH), BF),
    ("cos", (4, 128, 128), F32),
    ("sin", (4, 128, 128), F32),
    ("qraw", (4, 128, 256), F32),
    ("kraw", (4, 128, 128), F32),
    ("gl", (4, 128, 128), F32),
    ("qx", (2, 2, 2, 128, 256), BF),
    ("dox", (2, 2, 2, 128, 256), BF),
    ("oacc", (2, 512, 256), F32),
    ("att", (4, 128, 256), F32),
    ("gated", (4, 128, 256), BF),
    ("gsc", (4, 128, 640), BF),
    ("act", (3, 512, 768), BF),
    ("hid", (64, WIDTH), F32),
    ("gh", (64, WIDTH), F32),
    ("dgs", (2, WIDTH), F32),
    ("dgh", (8, 128), F32),
    ("pb", (4, 2, 64, WIDTH), BF),
    ("pb2", (4, 2, 64, WIDTH), BF),
    ("rsib", (2, 2, 64, WIDTH), BF),
    ("rz", (3, 64, WIDTH), BF),
    ("m_r2", (2, 2, 4, 32, 2304), BF),
    ("m_r1", (2, 2, 4, 2, 32, 2304), BF),
    ("m_q2", (2, 2, 1, 32, 2304), BF),
    ("m_q1", (2, 2, 1, 2, 32, 2304), BF),
    ("k_r2", (2, 2, 4, 128, 256), BF),
    ("k_r1", (2, 2, 4, 2, 128, 256), BF),
    ("k_q2", (2, 2, 1, 128, 256), BF),
    ("k_q1", (2, 2, 1, 2, 128, 256), BF),
    ("ob", (2, 64, WIDTH), BF),
    ("ib", (2, 64, WIDTH), BF),
    ("sums", (4, 40, 128), F32),
    ("came", (13, 40, 128), F32),
]
COPIES = 175


def kernel(*refs):
    names = INPUTS + [o[0] for o in OUTPUTS] + [v[0] for v in SCRATCH] + ["send", "recv", "free", "put"]
    body(SimpleNamespace(**dict(zip(names, refs))))


def finish(out, grad_in, gain, fm, fa, *to):
    to[0][...] = out[...].reshape(128, WIDTH)
    to[1][...] = grad_in[...].reshape(128, WIDTH)
    place = lax.axis_index("seq")
    for at, first in ((2, 0), (10, 16)):
        v = gain[pl.ds(first + lax.div(place, 4), 1), :]
        to[at][...] = pltpu.roll(v, lax.rem(128 - lax.rem(place, 4) * 32, 128), 1)[:, 0:32]
    to[7][...] = gain[32:33, :]
    to[8][...] = gain[33:34, :]
    gates = jnp.zeros((8, 32), F32)
    for i in range(4):
        wide = slice(i * 256, (i + 1) * 256)
        low = slice(i * 128, (i + 1) * 128)
        to[9][:, wide] = fa[i, :, 0:256].astype(F32)
        to[3][:, wide] = fa[i, :, 256:512].astype(F32)
        to[4][:, low] = fa[i, :, 640:768].astype(F32)
        to[5][:, low] = fa[i, :, 768:896].astype(F32)
        pick = select(lambda r, q, i=i: (r == q + 2 * i) & (q < 2), (8, 128))
        gates = gates + mm_tb(pick, fa[i, :, 512:640])
        for k in range(3):
            cols = slice(k * 768, (k + 1) * 768)
            to[11 + k][:, i * 768 : (i + 1) * 768] = fm[i, :, cols].astype(F32)
    to[6][...] = gates


def rope_tables():
    inverse = ROPE_BASE ** (-np.arange(HEAD // 2) * 2.0 / HEAD)
    inverse = np.concatenate([inverse, inverse]).astype(np.float32).astype(np.float64)
    rows = np.arange(128)[:, None] * inverse
    blocks = np.arange(64)[:, None] * 128 * inverse
    return [jnp.asarray(f(a), F32) for a in (rows, blocks) for f in (np.cos, np.sin)]


def per_device(
    inputs,
    attention_gain,
    query_weight,
    key_matrix,
    value_matrix,
    gate_weight,
    query_gain,
    key_gain,
    out_weight,
    feed_gain,
    feed_gate,
    feed_up,
    feed_down,
    cotangent,
):
    vmem = pl.BlockSpec(memory_space=pltpu.VMEM)
    out = pl.pallas_call(
        kernel,
        out_shape=[jax.ShapeDtypeStruct(shape, kind) for _, shape, kind in OUTPUTS],
        in_specs=[vmem] * len(INPUTS),
        out_specs=[pl.BlockSpec(memory_space=pl.ANY)] * len(OUTPUTS),
        scratch_shapes=[pltpu.VMEM(shape, kind) for _, shape, kind in SCRATCH]
        + [pltpu.SemaphoreType.DMA((COPIES,)), pltpu.SemaphoreType.DMA((COPIES,))]
        + [pltpu.SemaphoreType.REGULAR((3,)), pltpu.SemaphoreType.DMA((5,))],
        compiler_params=pltpu.CompilerParams(
            collective_id=0, has_side_effects=True, vmem_limit_bytes=63 * 2**20
        ),
        name="block",
    )(
        inputs,
        cotangent,
        attention_gain.reshape(1, WIDTH),
        query_gain.reshape(1, HEAD),
        key_gain.reshape(1, HEAD),
        feed_gain.reshape(1, WIDTH),
        query_weight,
        key_matrix,
        value_matrix,
        gate_weight.T,
        out_weight.T,
        feed_gate,
        feed_up,
        feed_down.T,
        *rope_tables(),
    )
    out = pl.pallas_call(
        finish,
        out_shape=[jax.ShapeDtypeStruct(shape, kind) for shape, kind in RESULTS],
        compiler_params=pltpu.CompilerParams(vmem_limit_bytes=60 * 2**20),
        name="results",
    )(*out)
    out = list(out)
    for i in (2, 7, 8, 10):
        out[i] = out[i].reshape(-1)
    for i in (6, 9, 13):
        out[i] = out[i].T
    return tuple(out)


def solution(mesh):
    seq, both, turned = P("seq", None), P("seq", "grp"), P("grp", "seq")
    in_specs = (seq, P(), both, both, both, both, P(), P(), turned, P(), both, both, turned, seq)
    out_specs = (
        seq, seq, P("seq"), both, both, both, both, P(), P(), turned, P("seq"), both, both, turned,
    )
    return jax.shard_map(
        per_device, mesh=mesh, in_specs=in_specs, out_specs=out_specs, check_vma=False
    )
```

```python
from types import SimpleNamespace

import jax
import jax.numpy as jnp
import numpy as np
from jax import lax
from jax.experimental import pallas as pl
from jax.experimental.pallas import tpu as pltpu
from jax.sharding import PartitionSpec as P

EPSILON = 1e-06
ROPE_BASE = 1000000.0
WIDTH = 2048
HEAD = 128
EIGHTH = 768
ATT = 768
PROJ = 512
SCALE = HEAD**-0.5
LOG2E = 1.4426950408889634
LN2 = 0.6931471805599453
BF, F32 = jnp.bfloat16, jnp.float32
MESH = pl.DeviceIdType.MESH
ALL = slice(None)


def mm(a, b):
    return jnp.dot(a, b, preferred_element_type=F32)


def mm_tb(a, b):
    return lax.dot_general(a, b, (((1,), (1,)), ((), ())), preferred_element_type=F32)


def rms_scale(v):
    return lax.rsqrt(jnp.mean(v * v, axis=-1, keepdims=True) + EPSILON)


def rms_back(v, gain, dy):
    r = rms_scale(v)
    u = gain * dy
    dv = r * (u - v * (r * r * jnp.mean(u * v, axis=-1, keepdims=True)))
    return dv, jnp.sum(dy * v * r, axis=0, keepdims=True)


def rope(v, cos, sin):
    return v * cos + pltpu.roll(v, HEAD // 2, 1) * sin


def rope_back(v, cos, sin):
    return v * cos + pltpu.roll(v * sin, HEAD // 2, 1)


def three_parts(v, lanes):
    hi = v.astype(BF).astype(F32)
    mid = (v - hi).astype(BF).astype(F32)
    low = v - hi - mid
    return jnp.where(
        lanes == 0, hi, jnp.where(lanes == 1, mid, jnp.where(lanes == 2, low, 0.0))
    ).astype(BF)


def select(row_of, shape):
    row = lax.broadcasted_iota(jnp.int32, shape, 0)
    col = lax.broadcasted_iota(jnp.int32, shape, 1)
    return jnp.where(row_of(row, col), 1.0, 0.0).astype(BF)


def body(R):
    s, zh = lax.axis_index("seq"), lax.axis_index("grp")
    c = lax.rem(s, 2)
    x = lax.rem(lax.div(s, 2), 4)
    y = lax.rem(lax.div(s, 8), 4)
    zl = lax.div(s, 32)
    z = zh * 2 + zl
    j = y * 4 + x
    me = zl * 2 + c

    def up(v, k):
        return lax.rem(v + k, 4)

    def dev(zz, yy, xx, cc):
        return (lax.rem(zz, 2) * 32 + yy * 8 + xx * 2 + cc, lax.div(zz, 2))

    sib = dev(z, y, x, 1 - c)
    zs = [up(z, 1), up(z, 3), up(z, 2)]
    zdev = [dev(v, y, x, c) for v in zs]
    part = (zl_dev := (1 - zl) * 32 + y * 8 + x * 2 + c, zh)
    diag = ((1 - zl) * 32 + y * 8 + x * 2 + 1 - c, zh)
    other = (zl_dev, 1 - zh)
    xdev = [dev(z, y, up(x, k), c) for k in (1, 3, 2)]
    ydev = [dev(z, up(y, k), x, c) for k in (1, 3, 2)]

    barrier = pltpu.get_barrier_semaphore()
    zsib = [dev(v, y, x, 1 - c) for v in zs]
    greet = [sib] + zdev + zsib + xdev + ydev
    for d in greet:
        pl.semaphore_signal(barrier, inc=1, device_id=d, device_id_type=MESH)

    count = [0]

    def ids(k):
        count[0] += k
        return count[0] - k

    class Group:
        def __init__(self, k, base=None):
            self.base, self.sent = ids(k) if base is None else base, []

        def copy(self, src, dst, d, i):
            i += self.base
            return pltpu.make_async_remote_copy(
                src_ref=src, dst_ref=dst, send_sem=R.send.at[i], recv_sem=R.recv.at[i],
                device_id=d, device_id_type=MESH,
            )

        def run(self, ends, d, i):
            self.copy(*ends(), d, i).start()
            self.sent.append(lambda: self.copy(*ends(), d, i))

        def go(self, src, dst, d, i):
            self.run(lambda: (src, dst), d, i)

        def got(self, ref, i):
            self.copy(ref, ref, sib, i).wait_recv()

        def end(self):
            for cp in self.sent:
                cp().wait_send()

    def exchange(buf, wl, base, cs=ALL):
        g = Group(3, base)

        def start():
            buf[zl, y, x, c, :, cs] = wl[me, :, cs]
            dst = buf.at[zl, y, x, c, :, cs]
            g.go(wl.at[zl * 2 + 1 - c, :, cs], dst, sib, 0)
            g.go(wl.at[(1 - zl) * 2 + c, :, cs], dst, part, 1)
            g.go(wl.at[(1 - zl) * 2 + 1 - c, :, cs], dst, diag, 2)

        def wait():
            g.got(buf.at[zl, y, x, 1 - c, :, cs], 0)
            g.got(buf.at[1 - zl, y, x, c, :, cs], 1)
            g.got(buf.at[1 - zl, y, x, 1 - c, :, cs], 2)

        return start, wait, g.end

    def give_back(src, dst, base):
        g = Group(3, base)

        def start():
            dst[me] = src[zl, y, x, c]
            g.go(src.at[zl, y, x, 1 - c], dst.at[me], sib, 0)
            g.go(src.at[1 - zl, y, x, c], dst.at[me], part, 1)
            g.go(src.at[1 - zl, y, x, 1 - c], dst.at[me], diag, 2)

        def wait():
            g.got(dst.at[zl * 2 + 1 - c], 0)
            g.got(dst.at[(1 - zl) * 2 + c], 1)
            g.got(dst.at[(1 - zl) * 2 + 1 - c], 2)

        return start, wait, g.end

    a_y = SimpleNamespace(
        full=lambda p: (0, p), half=lambda p, h: (0, p, ALL, h), elem=lambda p, k, h: (0, p, k, h),
        k=4, pos=y, dev=ydev,
    )
    a_x = SimpleNamespace(
        full=lambda p: (0, y, p), half=lambda p, h: (0, y, p, h), elem=lambda p, k, h: (0, y, p, h),
        k=1, pos=x, dev=xdev,
    )
    b_x = SimpleNamespace(
        full=lambda p: (1, ALL, p), half=lambda p, h: (1, ALL, p, h), elem=lambda p, k, h: (1, k, p, h),
        k=4, pos=x, dev=xdev,
    )
    b_y = SimpleNamespace(
        full=lambda p: (1, p, x), half=lambda p, h: (1, p, x, h), elem=lambda p, k, h: (1, p, x, h),
        k=1, pos=y, dev=ydev,
    )

    def gather_ring(buf, a, cs, base):
        g, p = Group(6, base), a.pos
        left, right, across = up(p, 3), up(p, 1), up(p, 2)

        def half(q, h):
            at = a.half(q, h)
            return buf.at[at if cs is None else at + (ALL,) * (5 - len(at)) + (cs,)]

        def s1():
            for i, (h, d) in enumerate(((0, 0), (1, 1), (1, 0), (0, 1))):
                g.run(lambda h=h: (half(p, h), half(p, h)), a.dev[d], i)

        def s2():
            g.got(half(left, 0), 0)
            g.run(lambda: (half(left, 0), half(left, 0)), a.dev[0], 4)
            g.got(half(right, 1), 1)
            g.run(lambda: (half(right, 1), half(right, 1)), a.dev[1], 5)

        def s3():
            g.got(half(left, 1), 2)
            g.got(half(right, 0), 3)

        def s4():
            g.got(half(across, 0), 4)
            g.got(half(across, 1), 5)

        return s1, s2, s3, s4, g.end

    def gather(buf, base, cs=None):
        one = [gather_ring(buf, a_x, cs, base), gather_ring(buf, b_y, cs, base + 6)]
        two = [gather_ring(buf, a_y, cs, base + 12), gather_ring(buf, b_x, cs, base + 18)]

        def t1():
            for r in one:
                r[0]()

        def t2():
            for r in one:
                r[1]()

        def t3():
            for r, q in zip(one, two):
                r[2]()
                r[3]()
                q[0]()

        def t4():
            for r in two:
                r[1]()

        def t5():
            for r in two:
                r[2]()

        def t6():
            for r in two:
                r[3]()
            for r in one + two:
                r[4]()

        return t1, t2, t3, t4, t5, t6

    def reduce_ring(buf, a, r2, r1, cs, bs, rows, base):
        g, p, k = Group(6, base), a.pos, a.k
        first = ALL if k == 4 else 0
        across, beside = up(p, 2), (up(p, 1), up(p, 3))

        def half(q, h):
            at = a.half(q, h)
            return buf.at[at + (ALL,) * (5 - len(at)) + (cs,)]

        def elem(q, n, h):
            return a.elem(q, n, h) + (ALL, cs)

        def far(i):
            return r2.at[i, first, rows, bs]

        def near(i, h):
            return r1.at[i, first, h, rows, bs]

        def loop(fn):
            if k == 1:
                fn(0)
            else:
                pl.loop(0, k)(fn)

        def s1():
            for i in (0, 1):
                g.run(lambda i=i: (half(across, i), far(i)), a.dev[i], i)

        def direct(i):
            g.run(lambda: (half(beside[i], 1 - i), near(i, 1 - i)), a.dev[i], 2 + i)

        def s2(i):
            g.got(far(i), i)
            to = beside[i]

            def add(n):
                at = elem(to, n, i)
                buf[at] = buf[at] + r2[i, n, rows, bs]

            loop(add)
            g.run(lambda: (half(to, i), near(i, i)), a.dev[i], 4 + i)

        def s3():
            for i in (0, 1):
                g.got(near(i, 1 - i), 2 + i)
                g.got(near(i, i), 4 + i)

            def add(n):
                for h in (0, 1):
                    at = elem(p, n, h)
                    total = (
                        buf[at].astype(F32)
                        + r1[0, n, h, rows, bs].astype(F32)
                        + r1[1, n, h, rows, bs].astype(F32)
                    )
                    buf[at] = total.astype(BF)

            loop(add)

        return s1, direct, s2, s3, g.end

    def scatter(buf, bufs, base, cs, bs=None, rows=ALL):
        bs = cs if bs is None else bs
        one = [
            reduce_ring(buf, a_y, bufs[0].at[0], bufs[1].at[0], cs, bs, rows, base),
            reduce_ring(buf, b_x, bufs[0].at[1], bufs[1].at[1], cs, bs, rows, base + 6),
        ]
        two = [
            reduce_ring(buf, a_x, bufs[2].at[0], bufs[3].at[0], cs, bs, rows, base + 12),
            reduce_ring(buf, b_y, bufs[2].at[1], bufs[3].at[1], cs, bs, rows, base + 18),
        ]

        def t0():
            for r in one:
                r[0]()

        def t1(i):
            for r in one:
                r[1](i)

        def t2(i):
            for r in one:
                r[2](i)

        def t3():
            for r, q in zip(one, two):
                r[3]()
                q[0]()
                q[1](0)
                q[1](1)

        def t4():
            for i in (0, 1):
                for r in two:
                    r[2](i)

        def t5():
            for r in two:
                r[3]()
            for r in one + two:
                r[4]()

        def start():
            t0()
            t1(0)
            t1(1)

        def onward():
            t2(0)
            t2(1)

        return SimpleNamespace(t0=t0, t1=t1, t2=t2, t3=t3, t4=t4, t5=t5, start=start, onward=onward)

    def place(zz, cc):
        return (lax.rem(zz, 2) * 2 + cc, lax.div(zz, 2))

    half_rows = (slice(0, 32), slice(32, 64))

    rows_base = ids(8)

    def reduce_rows(pb, rsib, rz):
        g = Group(8, rows_base)

        def mine(zz, h):
            return pb.at[place(zz, c) + (half_rows[h],)]

        def s0():
            for i, t in enumerate((zl, 1 - zl)):
                g.go(pb.at[t * 2 + 1 - c], rsib.at[t], sib, i)

        def s1():
            def add(zz):
                at = place(zz, c)
                pb[at] = pb[at] + rsib[lax.rem(zz, 2), lax.div(zz, 2)]

            g.got(rsib.at[zl], 0)
            add(zs[2])
            for i in (0, 1):
                g.go(mine(zs[2], i), rz.at[2, half_rows[i]], zdev[i], 2 + i)
            g.got(rsib.at[1 - zl], 1)
            for i in (0, 1):
                add(zs[i])
                g.go(mine(zs[i], 1 - i), rz.at[i, half_rows[1 - i]], zdev[i], 4 + i)
            add(z)

        def s2():
            for i in (0, 1):
                rows = half_rows[i]
                g.got(rz.at[2, rows], 2 + i)
                at = place(zs[i], c) + (rows,)
                pb[at] = pb[at] + rz[2, rows]
                g.go(mine(zs[i], i), rz.at[i, rows], zdev[i], 6 + i)

        def s3():
            for i in (0, 1):
                g.got(rz.at[i, half_rows[1 - i]], 4 + i)
                g.got(rz.at[i, half_rows[i]], 6 + i)

        def total(rows):
            v = pb[me, zh, rows].astype(F32)
            return v + rz[0, rows].astype(F32) + rz[1, rows].astype(F32)

        return SimpleNamespace(s0=s0, s1=s1, s2=s2, s3=s3, end=g.end, total=total)

    spread_base = ids(10)

    def gather_rows(buf):
        g = Group(10, spread_base)

        def at(zz, h):
            return buf.at[place(zz, c) + (half_rows[h],)]

        def s0():
            for i, (h, d) in enumerate(((0, 0), (1, 1), (1, 0), (0, 1))):
                g.go(at(z, h), at(z, h), zdev[d], i)
            own = buf.at[place(z, c)]
            g.go(own, own, sib, 6)

        def s1():
            g.got(at(zs[1], 0), 0)
            g.go(at(zs[1], 0), at(zs[1], 0), zdev[0], 4)
            g.got(at(zs[0], 1), 1)
            g.go(at(zs[0], 1), at(zs[0], 1), zdev[1], 5)

        def s2():
            def hand_on(zz, i):
                whole = buf.at[place(zz, c)]
                g.go(whole, whole, sib, i)

            g.got(at(zs[1], 1), 2)
            hand_on(zs[1], 7)
            g.got(at(zs[0], 0), 3)
            hand_on(zs[0], 8)
            g.got(at(zs[2], 0), 4)
            g.got(at(zs[2], 1), 5)
            hand_on(zs[2], 9)

        def s3():
            for i, zz in ((6, z), (7, zs[1]), (8, zs[0]), (9, zs[2])):
                g.got(buf.at[place(zz, 1 - c)], i)

        return SimpleNamespace(s0=s0, s1=s1, s2=s2, s3=s3, end=g.end)

    def gather_blocks(buf):
        g = Group(5)

        def s0():
            g.go(buf.at[me, 0], buf.at[me, 0], part, 0)
            g.go(buf.at[me, 1], buf.at[me, 1], other, 1)
            g.go(buf.at[me], buf.at[me], sib, 2)

        def s1():
            for h in (0, 1):
                at = buf.at[(1 - zl) * 2 + c, h]
                g.got(at, h)
                g.go(at, at, sib, 3 + h)

        def s2():
            g.got(buf.at[zl * 2 + 1 - c], 2)
            for h in (0, 1):
                g.got(buf.at[(1 - zl) * 2 + 1 - c, h], 3 + h)

        return s0, s1, s2, g.end

    def twin(buf):
        g = Group(1)

        def start():
            g.go(buf.at[zh], buf.at[zh], zdev[2], 0)

        def wait():
            g.got(buf.at[1 - zh], 0)
            g.end()

        return start, wait

    for i in range(4):
        R.wla[i, :, 0:256] = R.qw[:, i * 256 : (i + 1) * 256]
        R.wla[i, :, 256:384] = R.kw[:, i * 128 : (i + 1) * 128]
        R.wla[i, :, 384:512] = R.vw[:, i * 128 : (i + 1) * 128]
    pairs, rings = [ids(3) for _ in range(4)], [ids(24) for _ in range(5)]
    ex_a = exchange(R.wa, R.wla, pairs[0])
    ex_o = exchange(R.wo, R.wlo, pairs[1])
    ex_m = exchange(R.wm, R.wlm, pairs[2], slice(0, 1536))
    ex_d = exchange(R.wm, R.wlm, pairs[3], slice(1536, 2304))
    ag_a, ag_o = gather(R.wa, rings[0]), gather(R.wo, rings[1])
    ag_m = gather(R.wm, rings[2], slice(0, 1536))
    ag_d = gather(R.wm, rings[3], slice(1536, 2304))
    ag_x = gather_blocks(R.xn)
    ag_c = gather_blocks(R.cot)
    ag_kv = gather(R.kv, rings[4])

    pl.semaphore_wait(barrier, len(greet))
    ex_a[0]()
    for i in range(4):
        R.wlo[i] = R.ow[:, i * 256 : (i + 1) * 256]
        R.wlm[i, :, 1536:2304] = R.fd[:, i * 768 : (i + 1) * 768]
    ex_o[0]()

    shift = select(lambda r, q: q == r + me * 32, (32, 128))
    wide = mm(R.gw[...], shift).astype(BF)
    for i in range(4):
        pick = select(lambda r, q, i=i: (q == r + 2 * i) & (r < 2), (16, 8))
        R.gt_l[i] = mm(pick, wide).astype(BF)
    gates = Group(9)
    steps = (1, 3, 2)
    near_group = [(zl * 2 + 1 - c, sib), ((1 - zl) * 2 + c, part), ((1 - zl) * 2 + 1 - c, diag)]
    R.gt_in[me] = R.gt_l[me]
    for n, (i, d) in enumerate(near_group):
        gates.go(R.gt_l.at[i], R.gt_in.at[me], d, n)
    ex_d[0]()

    @pl.loop(0, 4)
    def _(t):
        rows = pl.ds(pl.multiple_of(lax.rem(t, 2) * 32, 32), 32)
        v = R.x[pl.ds(pl.multiple_of(t * 32, 32), 32), :].astype(F32)
        R.xn[me, lax.div(t, 2), rows] = (v * rms_scale(v) * R.ag[...]).astype(BF)

    ag_x[0]()
    for i in range(4):
        R.wlm[i, :, 0:768] = R.fg[:, i * 768 : (i + 1) * 768]
        R.wlm[i, :, 768:1536] = R.fu[:, i * 768 : (i + 1) * 768]
    ex_m[0]()
    first = lax.broadcasted_iota(jnp.int32, (128, 128), 1) < 64
    for i in range(4):
        base = (i // 2) * 32 + j * 2 + i % 2
        cb, sb = R.cb[pl.ds(base, 1), :], R.sb[pl.ds(base, 1), :]
        sin = sb * R.cr[...] + cb * R.sr[...]
        R.cos[i] = cb * R.cr[...] - sb * R.sr[...]
        R.sin[i] = jnp.where(first, -sin, sin)
    R.cot[me] = R.ct[...].reshape(2, 64, WIDTH)
    ex_a[1]()
    ag_a[0]()
    ex_o[1]()
    ag_o[0]()
    for n, (i, _) in enumerate(near_group):
        gates.got(R.gt_in.at[i], n)
    R.gt[y, x] = (R.gt_in[0] + R.gt_in[1]) + (R.gt_in[2] + R.gt_in[3])
    for n in range(3):
        gates.go(R.gt.at[y, x], R.gt.at[y, x], xdev[n], 3 + n)
    ag_a[1]()
    ex_d[1]()
    ag_d[0]()
    ag_o[1]()
    ag_a[2]()
    ag_x[1]()
    ag_d[1]()
    ag_a[3]()
    for n, k in enumerate(steps):
        gates.got(R.gt.at[y, up(x, 4 - k)], 3 + n)
    for n in range(3):
        gates.go(R.gt.at[y], R.gt.at[y], ydev[n], 6 + n)
    ex_m[1]()
    ag_m[0]()
    ag_a[4]()
    ag_x[2]()
    ag_a[5]()

    @pl.loop(0, 2)
    def _(zi):
        w = R.wa[...].reshape(WIDTH, PROJ)
        both = mm(R.xn[pl.ds(zi * 2, 2)].reshape(256, WIDTH), w)
        for ci in (0, 1):
            i, raw = zi * 2 + ci, both[ci * 128 : (ci + 1) * 128]
            cos, sin = R.cos[i], R.sin[i]
            R.qraw[i] = raw[:, 0:256]
            R.kraw[i] = raw[:, 256:384]
            for h in (0, 1):
                v = raw[:, h * 128 : (h + 1) * 128]
                q = rope(v * rms_scale(v) * R.qg[...], cos, sin) * (SCALE * LOG2E)
                R.qx[zi, h, ci, :, 0:128] = q.astype(BF)
            v = raw[:, 256:384]
            k = rope(v * rms_scale(v) * R.kg[...], cos, sin)
            R.kv[zi, y, x, ci, :, 0:128] = k.astype(BF)
            R.kv[zi, y, x, ci, :, 128:256] = raw[:, 384:512].astype(BF)

    ag_kv[0]()
    ag_c[0]()
    ag_m[1]()

    ones = jnp.ones((256, 128), BF)
    key_i = lax.broadcasted_iota(jnp.int32, (512, 256), 1)
    row_i = lax.broadcasted_iota(jnp.int32, (512, 256), 0)
    seen = key_i <= lax.rem(row_i, 256)
    R.oacc[...] = jnp.zeros((2, 512, 256), F32)

    def keys_of(at):
        return R.kv[at + (ALL, ALL, slice(0, 128))].reshape(256, 128)

    def values_of(at):
        v = R.kv[at + (ALL, ALL, slice(128, 256))].reshape(256, 128)
        return jnp.concatenate([v, ones], axis=1)

    def forward(tiles):
        work = []
        for g in (0, 1):
            mine = [u for u in tiles if g in u[1]]
            if mine:
                k = jnp.concatenate([keys_of(u[0]) for u in mine], axis=0)
                v = jnp.concatenate([values_of(u[0]) for u in mine], axis=0)
                scores = mm_tb(R.qx[g, :, :, :, 0:128].reshape(512, 128), k)
                work.append((g, mine, v, scores))
        for g, mine, v, scores in work:
            p = jnp.exp2(scores)
            if any(u[2] == g for u in mine):
                parts = [p[:, i * 256 : (i + 1) * 256] for i in range(len(mine))]
                parts = [jnp.where(seen, q, 0.0) if u[2] == g else q for u, q in zip(mine, parts)]
                p = jnp.concatenate(parts, axis=1)
            R.oacc[g] += mm(p.astype(BF), v)

    def tile_pair(fn, empty, at0, at1):
        t0, t1 = at0[0] * 4 + at0[1], at1[0] * 4 + at1[1]
        at0, at1 = (0,) + at0, (1,) + at1

        @pl.when((t0 < j) & (t1 < j))
        def _():
            fn([(at0, (0, 1), None), (at1, (1,), None)])

        @pl.when((t0 < j) & (t1 > j))
        def _():
            fn([(at0, (0, 1), None)])

        @pl.when((t0 > j) & (t1 < j))
        def _():
            fn([(at0, (1,), None), (at1, (1,), None)])

        @pl.when((t0 > j) & (t1 > j))
        def _():
            fn([(at0, (1,), None)])

        if empty is not None:

            @pl.when(t1 > j)
            def _():
                empty(at1)

    own = [((0, y, x), (0, 1), 0), ((1, y, x), (1,), 1)]

    def near(fn, empty=None):
        @pl.loop(1, 4)
        def _(k):
            tile_pair(fn, empty, (y, up(x, k)), (up(y, k), x))

    def side(fn, a, empty=None):
        @pl.loop(0, 4)
        def _(k):
            tile_pair(fn, empty, (up(y, a), k), (k, up(x, a)))

    forward(own)
    ag_kv[1]()
    ag_kv[2]()
    near(forward)
    ag_c[1]()
    ag_kv[3]()
    ag_o[2]()
    ag_kv[4]()

    @pl.loop(0, 3)
    def _(k):
        @pl.when(k == 2)
        def _():
            ag_kv[5]()
            ag_o[3]()
            ag_m[2]()

        side(forward, 1 + 2 * k - 3 * lax.div(k, 2))

    ag_o[4]()
    ag_o[5]()

    for n, k in enumerate(steps):
        gates.got(R.gt.at[up(y, 4 - k)], 6 + n)
    lower = lax.broadcasted_iota(jnp.int32, (16, 128), 1) < 64

    def regroup(u, w):
        return (
            jnp.where(lower, u, pltpu.roll(w, 64, 1)),
            jnp.where(lower, pltpu.roll(u, 64, 1), w),
        )

    for m in range(8):
        u, w = (R.gt[q // 4, q % 4].astype(F32) for q in (2 * m, 2 * m + 1))
        u, w = regroup(u, w)
        R.gtn[:, m * 128 : (m + 1) * 128] = u.astype(BF)
        R.gtn[:, 1024 + m * 128 : 1152 + m * 128] = w.astype(BF)

    @pl.loop(0, 2)
    def _(zi):
        v = mm_tb(R.xn[pl.ds(zi * 2, 2)].reshape(256, WIDTH), R.gtn[...])
        R.gl[pl.ds(zi * 2, 2)] = v.reshape(2, 128, 16)

    lanes = lax.broadcasted_iota(jnp.int32, (128, 128), 1)

    @pl.loop(0, 4)
    def _(i):
        zi, ci = lax.div(i, 2), lax.rem(i, 2)
        for h in (0, 1):
            rows = pl.ds(pl.multiple_of(h * 256 + ci * 128, 128), 128)
            total = R.oacc[zi, rows, 128:256]
            a = R.oacc[zi, rows, 0:128] / total
            R.att[i, :, h * 128 : (h + 1) * 128] = a
            R.qx[zi, h, ci, :, 128:256] = three_parts(-jnp.log2(total), lanes)
            gate = jax.nn.sigmoid(R.gl[i][:, h : h + 1])
            R.gated[i, :, h * 128 : (h + 1) * 128] = (a * gate).astype(BF)

    def spread(n, value):
        cols = pl.ds(pl.multiple_of(n * 256, 256), 256)
        return cols, value.reshape(4, 2, 64, 256).astype(BF)

    rs1 = reduce_rows(R.pb, R.rsib, R.rz)
    ag_n = gather_rows(R.nm)

    def project(cc):
        rows = jnp.concatenate([R.gated[cc], R.gated[2 + cc]], axis=0)

        @pl.loop(0, 8, unroll=4)
        def _(n):
            w = R.wo[lax.div(n, 4), lax.rem(n, 4)].reshape(256, 256)
            cols = pl.ds(pl.multiple_of(n * 256, 256), 256)
            v = mm_tb(rows, w).astype(BF).reshape(2, 2, 64, 256)
            R.pb[cc, :, :, cols] = v[0]
            R.pb[2 + cc, :, :, cols] = v[1]

    project(1 - c)
    rs1.s0()
    project(c)
    rs1.s1()
    rs1.s2()
    ag_m[3]()
    ag_d[2]()
    rs1.s3()

    def owned(t):
        return pl.ds(pl.multiple_of(t * 16, 16), 16)

    @pl.loop(0, 4)
    def _(t):
        rows = owned(t)
        v = R.x[pl.ds(pl.multiple_of(zh * 64 + t * 16, 16), 16), :].astype(F32)
        v = v + rs1.total(rows)
        R.hid[rows] = v
        R.nm[me, zh, rows] = (v * rms_scale(v) * R.fgain[...]).astype(BF)

    rs1.end()
    for g in (ex_a, ex_o, ex_m, ex_d):
        g[2]()
    gates.end()
    ag_n.s0()
    ag_c[2]()
    ag_n.s1()
    ag_m[4]()
    ag_n.s2()
    ag_m[5]()
    ag_d[3]()
    ag_n.s3()

    def weight(k, n):
        at = pl.ds(pl.multiple_of(k * 768 + n * 256, 256), 256)
        return R.wm[:, :, :, :, :, at].reshape(WIDTH, 256)

    @pl.loop(0, 3, unroll=3)
    def _(n):
        cols = pl.ds(pl.multiple_of(n * 256, 256), 256)
        rows = R.nm[...].reshape(512, WIDTH)
        gate = mm(rows, weight(0, n))
        upper = mm(rows, weight(1, n))
        sg = jax.nn.sigmoid(gate)
        silu = gate * sg
        R.act[0, :, cols] = (upper * (sg * (1.0 + gate * (1.0 - sg)))).astype(BF)
        R.act[1, :, cols] = silu.astype(BF)
        R.act[2, :, cols] = (silu * upper).astype(BF)

    def block(n):
        return (lax.div(n, 4), lax.rem(n, 4), ALL, ALL, ALL)

    def turned(ref, n):
        cols = pl.ds(pl.multiple_of(n * 256, 256), 256)
        return ref[:, :, :, cols].reshape(512, 256).T

    big = (R.m_r2, R.m_r1, R.m_q2, R.m_q1)
    rs_d = scatter(R.ga, big, rings[0], slice(0, 768))
    rs_m = scatter(R.wm, big, rings[1], slice(0, 1536), slice(768, 2304))

    @pl.loop(0, 8, unroll=4)
    def _(n):
        g = mm(turned(R.cot, n), R.act[2])
        R.ga[block(n) + (slice(0, 768),)] = g.astype(BF).reshape(4, 2, 32, 768)

    rs_d.start()
    ag_d[4]()
    ag_d[5]()

    @pl.loop(0, 3, unroll=3)
    def _(n):
        cols = pl.ds(pl.multiple_of(n * 256, 256), 256)
        grad = mm(R.cot[...].reshape(512, WIDTH), weight(2, n))
        R.act[0, :, cols] = (grad * R.act[0, :, cols].astype(F32)).astype(BF)
        R.act[1, :, cols] = (grad * R.act[1, :, cols].astype(F32)).astype(BF)

    @pl.loop(0, 8, unroll=4)
    def _(n):
        at = block(n)
        v = mm_tb(R.act[0], R.wm[at + (slice(0, 768),)].reshape(256, 768))
        v = v + mm_tb(R.act[1], R.wm[at + (slice(768, 1536),)].reshape(256, 768))
        cols, v = spread(n, v)
        R.pb[:, :, :, cols] = v

    rs2 = reduce_rows(R.pb, R.rsib, R.rz)
    rs_f = reduce_rows(R.pb2, R.rsib, R.rz)
    rs2.s0()

    def feed_weights(n):
        at = block(n)
        t = turned(R.nm, n)
        R.wm[at + (slice(0, 768),)] = mm(t, R.act[0]).astype(BF).reshape(4, 2, 32, 768)
        R.wm[at + (slice(768, 1536),)] = mm(t, R.act[1]).astype(BF).reshape(4, 2, 32, 768)

    pl.loop(0, 4, unroll=4)(feed_weights)
    rs2.s1()
    rs_d.onward()
    pl.loop(4, 8, unroll=4)(feed_weights)
    rs2.s2()

    def tell(devices, sem):
        for d in devices:
            pl.semaphore_signal(sem, inc=1, device_id=d, device_id_type=MESH)

    group = [sib] + zdev
    ring = xdev[:2] + ydev[:2]
    ag_n.end()
    tell(group, R.free.at[0])
    ag_h = gather_rows(R.nm)
    rs_m.start()

    @pl.loop(0, 8, unroll=4)
    def _(n):
        w = R.wm[block(n) + (slice(1536, 2304),)].reshape(256, 768)
        cols, v = spread(n, mm_tb(R.act[2], w))
        R.pb2[:, :, :, cols] = v

    R.dgs[...] = jnp.zeros((2, WIDTH), F32)
    ag_c[3]()
    rs2.s3()
    pl.semaphore_wait(R.free.at[0], 4)

    @pl.loop(0, 4)
    def _(t):
        rows = owned(t)
        dv, dg = rms_back(R.hid[rows], R.fgain[...], rs2.total(rows))
        dh = dv + R.ct[pl.ds(pl.multiple_of(zh * 64 + t * 16, 16), 16), :].astype(F32)
        R.dgs[1:2, :] += dg
        R.gh[rows] = dh
        R.nm[me, zh, rows] = dh.astype(BF)

    rs2.end()
    ag_h.s0()
    rs_d.t3()
    ag_h.s1()
    rs_m.onward()
    ag_h.s2()
    ag_h.s3()
    rs_f.s0()

    @pl.loop(0, 2)
    def _(zi):
        w = R.wo[...].reshape(WIDTH, 256)
        both = mm(R.nm[pl.ds(zi * 2, 2)].reshape(256, WIDTH), w)
        for ci in (0, 1):
            i, grad = zi * 2 + ci, both[ci * 128 : (ci + 1) * 128]
            logits = jnp.zeros((128, 128), F32)
            for h in (0, 1):
                gate = jax.nn.sigmoid(R.gl[i][:, h : h + 1])
                gr = grad[:, h * 128 : (h + 1) * 128]
                a = R.att[i, :, h * 128 : (h + 1) * 128]
                low = (gr * gate).astype(BF)
                dl = jnp.sum(gr * a, axis=1, keepdims=True) * (gate * (1.0 - gate))
                logits = jnp.where(lanes == h, dl, logits)
                delta = jnp.sum(low.astype(F32) * a, axis=1, keepdims=True)
                R.dox[zi, h, ci, :, 0:128] = low
                R.dox[zi, h, ci, :, 128:256] = three_parts(-delta, lanes)
            R.gsc[i, :, 512:640] = logits.astype(BF)

    rs_f.s1()

    R.oacc[...] = jnp.zeros((2, 512, 256), F32)
    row_t = lax.broadcasted_iota(jnp.int32, (256, 512), 1)
    key_t = lax.broadcasted_iota(jnp.int32, (256, 512), 0)
    seen_t = key_t <= lax.rem(row_t, 256)

    def backward(tiles):
        at = [u[0] for u in tiles]
        k = [keys_of(u) for u in at]
        kx = [jnp.concatenate([u, ones], axis=1) for u in k]
        vx = [values_of(u) for u in at]
        kt = [u.T for u in k]
        q = [R.qx[g].reshape(512, 256) for g in (0, 1)]
        d = [R.dox[g].reshape(512, 256) for g in (0, 1)]
        units = [(i, g, u[2] == g) for i, u in enumerate(tiles) for g in u[1]]
        p = [mm_tb(kx[i], q[g]) for i, g, _ in units]
        dp = [mm_tb(vx[i], d[g]) for i, g, _ in units]
        p = [jnp.exp2(u) for u in p]
        p = [jnp.where(seen_t, u, 0.0) if cut else u for u, (_, _, cut) in zip(p, units)]
        ds = [(u * w).astype(BF) for u, w in zip(p, dp)]
        p = [u.astype(BF) for u in p]
        dv = [mm(u, d[g][:, 0:128]) for u, (_, g, _) in zip(p, units)]
        dk = [mm(u, q[g][:, 0:128]) for u, (_, g, _) in zip(ds, units)]
        dq = [mm(kt[i], u) for u, (i, _, _) in zip(ds, units)]
        for g in (0, 1):
            mine = [u for u, (_, h, _) in zip(dq, units) if h == g]
            if mine:
                total = sum(mine[1:], mine[0])
                R.oacc[g, 0:128] += total[:, 0:256]
                R.oacc[g, 128:256] += total[:, 256:512]
        for i, place in enumerate(at):
            mine = [n for n, u in enumerate(units) if u[0] == i]
            first, rest = mine[0], mine[1:]
            total = sum([dk[n] for n in rest], dk[first])
            R.kv[place + (ALL, ALL, slice(0, 128))] = total.astype(BF).reshape(2, 128, 128)
            total = sum([dv[n] for n in rest], dv[first])
            R.kv[place + (ALL, ALL, slice(128, 256))] = total.astype(BF).reshape(2, 128, 128)

    def nothing(at):
        R.kv[at] = jnp.zeros((2, 128, 256), BF)

    small = (R.k_r2, R.k_r1, R.k_q2, R.k_q1)
    rs_k = scatter(R.kv, small, rings[4], slice(0, 256))

    @pl.loop(0, 3)
    def _(k):
        side(backward, 2 - k + 3 * lax.div(k, 2), nothing)

        @pl.when(k == 0)
        def _():
            rs_k.t0()

        @pl.when(k == 1)
        def _():
            rs_k.t1(0)
            rs_d.t4()

        @pl.when(k == 2)
        def _():
            rs_k.t1(1)

    rs_f.s2()
    rs_k.t2(0)
    rs_k.t2(1)
    rs_m.t3()
    near(backward, nothing)
    backward(own)
    rs_f.s3()
    tw_o = twin(R.ob)

    @pl.loop(0, 4)
    def _(t):
        rows = owned(t)
        R.ob[zh, rows] = (R.hid[rows] + rs_f.total(rows)).astype(BF)

    rs_f.end()
    tell(group, R.free.at[1])
    tw_o[0]()

    rs_d.t5()
    tell(ring, R.free.at[2])
    R.wm[:, y, x, :, :, 1536:2304] = R.ga[:, y, x, :, :, 0:768]
    rs_k.t3()
    rs_m.t4()

    R.dgh[...] = jnp.zeros((8, 128), F32)

    @pl.loop(0, 4)
    def _(i):
        zi, ci = lax.div(i, 2), lax.rem(i, 2)
        for h in (0, 1):
            cols = pl.ds(pl.multiple_of(ci * 128, 128), 128)
            dq = R.oacc[zi, h * 128 : (h + 1) * 128, cols].T * SCALE
            dq = rope_back(dq, R.cos[i], R.sin[i])
            dv, dg = rms_back(R.qraw[i, :, h * 128 : (h + 1) * 128], R.qg[...], dq)
            R.dgh[0:1, :] += dg
            R.gsc[i, :, h * 128 : (h + 1) * 128] = dv.astype(BF)

    rs_k.t4()

    turned_gates = R.gsc[:, :, 512:640].reshape(512, 128).T[0:16]

    @pl.loop(0, 8, unroll=4)
    def _(n):
        at = block(n)
        g = mm(turned(R.nm, n), R.gated[...].reshape(512, 256))
        R.ga[at + (slice(0, 256),)] = g.astype(BF).reshape(4, 2, 32, 256)
        t = turned(R.xn, n)
        g = mm(t, R.gsc[:, :, 0:256].reshape(512, 256))
        R.ga[at + (slice(256, 512),)] = g.astype(BF).reshape(4, 2, 32, 256)
        cols = pl.ds(pl.multiple_of(n * 256, 256), 256)
        R.gtg[:, cols] = mm(turned_gates, R.xn[:, :, :, cols].reshape(512, 256))

    for m in range(8):
        u, w = (R.gtg[:, q + m * 128 : q + (m + 1) * 128] for q in (0, 1024))
        u, w = regroup(u, w)
        R.gg[m // 2, m % 2 * 2] = u.astype(BF)
        R.gg[m // 2, m % 2 * 2 + 1] = w.astype(BF)
    gates = Group(9, gates.base)
    for n, k in enumerate(steps):
        gates.go(R.gg.at[up(y, k)], R.gg_y.at[n], ydev[n], 6 + n)
    rs_e = scatter(R.ga, big, rings[2], slice(0, 512))
    pl.semaphore_wait(R.free.at[2], 4)
    rs_e.start()
    rs_m.t5()
    gb_m = give_back(R.wm, R.wlm, pairs[0])
    gb_m[0]()
    rs_k.t5()

    @pl.loop(0, 4)
    def _(i):
        zi, ci = lax.div(i, 2), lax.rem(i, 2)
        dk = R.kv[zi, y, x, ci, :, 0:128].astype(F32) * LN2
        dk = rope_back(dk, R.cos[i], R.sin[i])
        dv, dg = rms_back(R.kraw[i], R.kg[...], dk)
        R.dgh[1:2, :] += dg
        R.gsc[i, :, 256:384] = dv.astype(BF)
        R.gsc[i, :, 384:512] = R.kv[zi, y, x, ci, :, 128:256]

    @pl.loop(0, 8, unroll=4)
    def _(n):
        g = mm(turned(R.xn, n), R.gsc[:, :, 256:512].reshape(512, 256))
        R.ga[block(n) + (slice(512, 768),)] = g.astype(BF).reshape(4, 2, 32, 256)

    rs_l = scatter(R.ga, small, rings[3], slice(512, 768), slice(0, 256), slice(0, 32))
    rs_l.start()

    @pl.loop(0, 8, unroll=4)
    def _(n):
        at = block(n)
        v = mm_tb(R.gsc[:, :, 0:512].reshape(512, 512), R.wa[at].reshape(256, PROJ))
        cols = pl.ds(pl.multiple_of(n * 256, 256), 256)
        v = v + mm(R.gsc[:, :, 512:528].reshape(512, 16), R.gtn[:, cols])
        dg = jnp.sum(v * R.xn[:, :, :, cols].reshape(512, 256).astype(F32), axis=0, keepdims=True)
        R.dgs[0:1, cols] = dg / R.ag[:, cols]
        cols, v = spread(n, v)
        R.pb[:, :, :, cols] = v

    rs3 = reduce_rows(R.pb, R.rsib, R.rz)
    pl.semaphore_wait(R.free.at[1], 4)
    rs3.s0()

    for r in range(16):
        R.sums[0, r : r + 1, :] = R.dgs[0:1, r * 128 : (r + 1) * 128]
        R.sums[0, 16 + r : 17 + r, :] = R.dgs[1:2, r * 128 : (r + 1) * 128]
    R.sums[0, 32:40, :] = R.dgh[...]

    def add_up(stage, devices):
        g, first = Group(len(devices)), (0, 7, 10)[stage]
        for i, d in enumerate(devices):
            g.go(R.sums.at[stage], R.came.at[first + i], d, i)

        def finish():
            v = R.sums[stage]
            for i in range(len(devices)):
                g.got(R.came.at[first + i], i)
                v = v + R.came[first + i]
            R.sums[stage + 1] = v
            g.end()

        return finish

    fin = add_up(0, group + zsib)
    rs_e.onward()
    for n in range(3):
        gates.got(R.gg_y.at[n], 6 + n)
    v = R.gg[y].astype(F32)
    for n in range(3):
        v = v + R.gg_y[n].astype(F32)
    R.gg[y] = v.astype(BF)
    for n, k in enumerate(steps):
        gates.go(R.gg.at[y, up(x, k)], R.gg_x.at[n], xdev[n], 3 + n)
    rs3.s1()
    rs_l.onward()
    rs3.s2()
    fin()
    fin = add_up(1, xdev)
    rs_e.t3()
    rs_l.t3()
    for n in range(3):
        gates.got(R.gg_x.at[n], 3 + n)
    v = R.gg[y, x].astype(F32)
    for n in range(3):
        v = v + R.gg_x[n].astype(F32)
    R.gt_out[me] = v.astype(BF)
    for n, (_, d) in enumerate(near_group):
        gates.go(R.gt_out.at[me], R.gt_out.at[me], d, n)
    rs_e.t4()
    rs3.s3()
    tw_i = twin(R.ib)

    @pl.loop(0, 4)
    def _(t):
        rows = owned(t)
        v = R.x[pl.ds(pl.multiple_of(zh * 64 + t * 16, 16), 16), :].astype(F32)
        dv, _ = rms_back(v, R.ag[...], rs3.total(rows))
        R.ib[zh, rows] = (R.gh[rows] + dv).astype(BF)

    tw_i[0]()
    rs3.end()
    fin()
    fin = add_up(2, ydev)
    rs_l.t4()
    rs_e.t5()
    rs_l.t5()
    gb_a = give_back(R.ga, R.wl8, pairs[1])
    gb_a[0]()

    def put(i, src, dst):
        cp = pltpu.make_async_copy(src, dst, R.put.at[i])
        cp.start()
        return cp

    gb_m[1]()
    puts = [put(0, R.wlm, R.o_fm)]
    tw_o[1]()
    puts.append(put(1, R.ob, R.o_out))
    fin()
    puts.append(put(2, R.sums.at[3], R.o_gain))
    tw_i[1]()
    puts.append(put(3, R.ib, R.o_in))
    for n, (i, _) in enumerate(near_group):
        gates.got(R.gt_out.at[i], n)
    gates.end()
    puts.append(put(5, R.gt_out, R.o_gt))
    gb_a[1]()
    puts.append(put(4, R.wl8, R.o_fa))
    for cp in puts:
        cp.wait()
    ag_x[3]()
    ag_h.end()
    gb_m[2]()
    gb_a[2]()
    assert count[0] == COPIES, count


INPUTS = [
    *("x", "ct", "ag", "qg", "kg", "fgain"),
    *("qw", "kw", "vw", "gw", "ow", "fg", "fu", "fd"),
    *("cr", "sr", "cb", "sb"),
]
OUTPUTS = [
    ("o_out", (2, 64, WIDTH), BF),
    ("o_in", (2, 64, WIDTH), BF),
    ("o_gain", (40, 128), F32),
    ("o_fm", (4, 32, 2304), BF),
    ("o_fa", (4, 32, ATT), BF),
    ("o_gt", (4, 16, 128), BF),
]
RESULTS = [
    ((128, WIDTH), BF),
    ((128, WIDTH), BF),
    ((1, 32), F32),
    ((32, 1024), F32),
    ((32, 512), F32),
    ((32, 512), F32),
    ((8, 32), F32),
    ((1, 128), F32),
    ((1, 128), F32),
    ((32, 1024), F32),
    ((1, 32), F32),
    ((32, 3072), F32),
    ((32, 3072), F32),
    ((32, 3072), F32),
]
SCRATCH = [
    ("wla", (4, 32, PROJ), BF),
    ("wlo", (4, 32, 256), BF),
    ("wl8", (4, 32, ATT), BF),
    ("wlm", (4, 32, 2304), BF),
    ("wa", (2, 4, 4, 2, 32, PROJ), BF),
    ("wo", (2, 4, 4, 2, 32, 256), BF),
    ("gt_l", (4, 16, 128), BF),
    ("gt_in", (4, 16, 128), BF),
    ("gt", (4, 4, 16, 128), BF),
    ("gtn", (16, WIDTH), BF),
    ("gtg", (16, WIDTH), F32),
    ("gg", (4, 4, 16, 128), BF),
    ("gg_y", (3, 4, 16, 128), BF),
    ("gg_x", (3, 16, 128), BF),
    ("gt_out", (4, 16, 128), BF),
    ("ga", (2, 4, 4, 2, 32, ATT), BF),
    ("wm", (2, 4, 4, 2, 32, 2304), BF),
    ("kv", (2, 4, 4, 2, 128, 256), BF),
    ("xn", (4, 2, 64, WIDTH), BF),
    ("cot", (4, 2, 64, WIDTH), BF),
    ("nm", (4, 2, 64, WIDTH), BF),
    ("cos", (4, 128, 128), F32),
    ("sin", (4, 128, 128), F32),
    ("qraw", (4, 128, 256), F32),
    ("kraw", (4, 128, 128), F32),
    ("gl", (4, 128, 16), F32),
    ("qx", (2, 2, 2, 128, 256), BF),
    ("dox", (2, 2, 2, 128, 256), BF),
    ("oacc", (2, 512, 256), F32),
    ("att", (4, 128, 256), F32),
    ("gated", (4, 128, 256), BF),
    ("gsc", (4, 128, 640), BF),
    ("act", (3, 512, 768), BF),
    ("hid", (64, WIDTH), F32),
    ("gh", (64, WIDTH), F32),
    ("dgs", (2, WIDTH), F32),
    ("dgh", (8, 128), F32),
    ("pb", (4, 2, 64, WIDTH), BF),
    ("pb2", (4, 2, 64, WIDTH), BF),
    ("rsib", (2, 2, 64, WIDTH), BF),
    ("rz", (3, 64, WIDTH), BF),
    ("m_r2", (2, 2, 4, 32, 2304), BF),
    ("m_r1", (2, 2, 4, 2, 32, 2304), BF),
    ("m_q2", (2, 2, 1, 32, 2304), BF),
    ("m_q1", (2, 2, 1, 2, 32, 2304), BF),
    ("k_r2", (2, 2, 4, 128, 256), BF),
    ("k_r1", (2, 2, 4, 2, 128, 256), BF),
    ("k_q2", (2, 2, 1, 128, 256), BF),
    ("k_q1", (2, 2, 1, 2, 128, 256), BF),
    ("ob", (2, 64, WIDTH), BF),
    ("ib", (2, 64, WIDTH), BF),
    ("sums", (4, 40, 128), F32),
    ("came", (13, 40, 128), F32),
]
COPIES = 184


def kernel(*refs):
    names = INPUTS + [o[0] for o in OUTPUTS] + [v[0] for v in SCRATCH] + ["send", "recv", "free", "put"]
    body(SimpleNamespace(**dict(zip(names, refs))))


def finish(out, grad_in, gain, fm, fa, gt, *to):
    to[0][...] = out[...].reshape(128, WIDTH)
    to[1][...] = grad_in[...].reshape(128, WIDTH)
    place = lax.axis_index("seq")
    for at, first in ((2, 0), (10, 16)):
        v = gain[pl.ds(first + lax.div(place, 4), 1), :]
        to[at][...] = pltpu.roll(v, lax.rem(128 - lax.rem(place, 4) * 32, 128), 1)[:, 0:32]
    to[7][...] = gain[32:33, :]
    to[8][...] = gain[33:34, :]
    ours = lax.div(place, 32) * 2 + lax.rem(place, 2)
    for i in range(4):
        wide = slice(i * 256, (i + 1) * 256)
        low = slice(i * 128, (i + 1) * 128)
        to[9][:, wide] = fa[i, :, 0:256].astype(F32)
        to[3][:, wide] = fa[i, :, 256:512].astype(F32)
        to[4][:, low] = fa[i, :, 512:640].astype(F32)
        to[5][:, low] = fa[i, :, 640:768].astype(F32)
        tile = pltpu.roll(gt[i].astype(F32), lax.rem(128 - ours * 32, 128), 1)
        to[6][2 * i : 2 * i + 2, :] = tile[0:2, 0:32]
        for k in range(3):
            cols = slice(k * 768, (k + 1) * 768)
            to[11 + k][:, i * 768 : (i + 1) * 768] = fm[i, :, cols].astype(F32)


def rope_tables():
    inverse = ROPE_BASE ** (-np.arange(HEAD // 2) * 2.0 / HEAD)
    inverse = np.concatenate([inverse, inverse]).astype(np.float32).astype(np.float64)
    rows = np.arange(128)[:, None] * inverse
    blocks = np.arange(64)[:, None] * 128 * inverse
    return [jnp.asarray(f(a), F32) for a in (rows, blocks) for f in (np.cos, np.sin)]


def per_device(
    inputs,
    attention_gain,
    query_weight,
    key_matrix,
    value_matrix,
    gate_weight,
    query_gain,
    key_gain,
    out_weight,
    feed_gain,
    feed_gate,
    feed_up,
    feed_down,
    cotangent,
):
    vmem = pl.BlockSpec(memory_space=pltpu.VMEM)
    out = pl.pallas_call(
        kernel,
        out_shape=[jax.ShapeDtypeStruct(shape, kind) for _, shape, kind in OUTPUTS],
        in_specs=[vmem] * len(INPUTS),
        out_specs=[pl.BlockSpec(memory_space=pl.ANY)] * len(OUTPUTS),
        scratch_shapes=[pltpu.VMEM(shape, kind) for _, shape, kind in SCRATCH]
        + [pltpu.SemaphoreType.DMA((COPIES,)), pltpu.SemaphoreType.DMA((COPIES,))]
        + [pltpu.SemaphoreType.REGULAR((3,)), pltpu.SemaphoreType.DMA((6,))],
        compiler_params=pltpu.CompilerParams(
            collective_id=0, has_side_effects=True, vmem_limit_bytes=63 * 2**20
        ),
        name="block",
    )(
        inputs,
        cotangent,
        attention_gain.reshape(1, WIDTH),
        query_gain.reshape(1, HEAD),
        key_gain.reshape(1, HEAD),
        feed_gain.reshape(1, WIDTH),
        query_weight,
        key_matrix,
        value_matrix,
        gate_weight.T,
        out_weight.T,
        feed_gate,
        feed_up,
        feed_down.T,
        *rope_tables(),
    )
    out = pl.pallas_call(
        finish,
        out_shape=[jax.ShapeDtypeStruct(shape, kind) for shape, kind in RESULTS],
        compiler_params=pltpu.CompilerParams(vmem_limit_bytes=60 * 2**20),
        name="results",
    )(*out)
    out = list(out)
    for i in (2, 7, 8, 10):
        out[i] = out[i].reshape(-1)
    for i in (6, 9, 13):
        out[i] = out[i].T
    return tuple(out)


def solution(mesh):
    seq, both, turned = P("seq", None), P("seq", "grp"), P("grp", "seq")
    in_specs = (seq, P(), both, both, both, both, P(), P(), turned, P(), both, both, turned, seq)
    out_specs = (
        seq, seq, P("seq"), both, both, both, both, P(), P(), turned, P("seq"), both, both, turned,
    )
    return jax.shard_map(
        per_device, mesh=mesh, in_specs=in_specs, out_specs=out_specs, check_vma=False
    )
```

```python
from types import SimpleNamespace

import jax
import jax.numpy as jnp
import numpy as np
from jax import lax
from jax.experimental import pallas as pl
from jax.experimental.pallas import tpu as pltpu
from jax.sharding import PartitionSpec as P

EPSILON = 1e-06
ROPE_BASE = 1000000.0
WIDTH = 2048
HEAD = 128
EIGHTH = 768
ATT = 768
PROJ = 512
SCALE = HEAD**-0.5
LOG2E = 1.4426950408889634
LN2 = 0.6931471805599453
BF, F32 = jnp.bfloat16, jnp.float32
MESH = pl.DeviceIdType.MESH
ALL = slice(None)


def mm(a, b):
    return jnp.dot(a, b, preferred_element_type=F32)


def mm_tb(a, b):
    return lax.dot_general(a, b, (((1,), (1,)), ((), ())), preferred_element_type=F32)


def rms_scale(v):
    return lax.rsqrt(jnp.mean(v * v, axis=-1, keepdims=True) + EPSILON)


def rms_back(v, gain, dy):
    r = rms_scale(v)
    u = gain * dy
    dv = r * (u - v * (r * r * jnp.mean(u * v, axis=-1, keepdims=True)))
    return dv, jnp.sum(dy * v * r, axis=0, keepdims=True)


def rope(v, cos, sin):
    return v * cos + pltpu.roll(v, HEAD // 2, 1) * sin


def rope_back(v, cos, sin):
    return v * cos + pltpu.roll(v * sin, HEAD // 2, 1)


def three_parts(v, lanes):
    hi = v.astype(BF).astype(F32)
    mid = (v - hi).astype(BF).astype(F32)
    low = v - hi - mid
    return jnp.where(
        lanes == 0, hi, jnp.where(lanes == 1, mid, jnp.where(lanes == 2, low, 0.0))
    ).astype(BF)


def select(row_of, shape):
    row = lax.broadcasted_iota(jnp.int32, shape, 0)
    col = lax.broadcasted_iota(jnp.int32, shape, 1)
    return jnp.where(row_of(row, col), 1.0, 0.0).astype(BF)


def body(R):
    s, zh = lax.axis_index("seq"), lax.axis_index("grp")
    c = lax.rem(s, 2)
    x = lax.rem(lax.div(s, 2), 4)
    y = lax.rem(lax.div(s, 8), 4)
    zl = lax.div(s, 32)
    z = zh * 2 + zl
    j = y * 4 + x
    me = zl * 2 + c

    def up(v, k):
        return lax.rem(v + k, 4)

    def dev(zz, yy, xx, cc):
        return (lax.rem(zz, 2) * 32 + yy * 8 + xx * 2 + cc, lax.div(zz, 2))

    sib = dev(z, y, x, 1 - c)
    zs = [up(z, 1), up(z, 3), up(z, 2)]
    zdev = [dev(v, y, x, c) for v in zs]
    part = (zl_dev := (1 - zl) * 32 + y * 8 + x * 2 + c, zh)
    diag = ((1 - zl) * 32 + y * 8 + x * 2 + 1 - c, zh)
    other = (zl_dev, 1 - zh)
    xdev = [dev(z, y, up(x, k), c) for k in (1, 3, 2)]
    ydev = [dev(z, up(y, k), x, c) for k in (1, 3, 2)]

    barrier = pltpu.get_barrier_semaphore()
    zsib = [dev(v, y, x, 1 - c) for v in zs]
    greet = [sib] + zdev + zsib + xdev + ydev
    for d in greet:
        pl.semaphore_signal(barrier, inc=1, device_id=d, device_id_type=MESH)

    count, sends, first_send = [0], [0], {}

    def take(counter, k):
        counter[0] += k
        return counter[0] - k

    def ids(k):
        return take(count, k)

    class Group:
        def __init__(self, k, base=None, whole=None):
            self.base, self.whole, self.sent = ids(k) if base is None else base, whole, []
            if self.base not in first_send:
                first_send[self.base] = take(sends, 1 if whole else k)

        def copy(self, src, dst, d, i):
            out = first_send[self.base] + (0 if self.whole else i)
            return pltpu.make_async_remote_copy(
                src_ref=src, dst_ref=dst, send_sem=R.send.at[out],
                recv_sem=R.recv.at[self.base + i], device_id=d, device_id_type=MESH,
            )

        def run(self, ends, d, i):
            self.copy(*ends(), d, i).start()
            self.sent.append(lambda: self.copy(*ends(), d, i))

        def go(self, src, dst, d, i):
            self.run(lambda: (src, dst), d, i)

        def got(self, ref, i):
            self.copy(ref, ref, sib, i).wait_recv()

        def end(self):
            if self.whole:
                ref = self.whole()
                self.copy(ref, ref, sib, 0).wait_send()
            else:
                for cp in self.sent:
                    cp().wait_send()

    def exchange(buf, wl, base, cs=ALL):
        g = Group(3, base)

        def start():
            buf[zl, y, x, c, :, cs] = wl[me, :, cs]
            dst = buf.at[zl, y, x, c, :, cs]
            g.go(wl.at[zl * 2 + 1 - c, :, cs], dst, sib, 0)
            g.go(wl.at[(1 - zl) * 2 + c, :, cs], dst, part, 1)
            g.go(wl.at[(1 - zl) * 2 + 1 - c, :, cs], dst, diag, 2)

        def wait():
            g.got(buf.at[zl, y, x, 1 - c, :, cs], 0)
            g.got(buf.at[1 - zl, y, x, c, :, cs], 1)
            g.got(buf.at[1 - zl, y, x, 1 - c, :, cs], 2)

        return start, wait, g.end

    def give_back(src, dst, base):
        g = Group(3, base)

        def start():
            dst[me] = src[zl, y, x, c]
            g.go(src.at[zl, y, x, 1 - c], dst.at[me], sib, 0)
            g.go(src.at[1 - zl, y, x, c], dst.at[me], part, 1)
            g.go(src.at[1 - zl, y, x, 1 - c], dst.at[me], diag, 2)

        def wait():
            g.got(dst.at[zl * 2 + 1 - c], 0)
            g.got(dst.at[(1 - zl) * 2 + c], 1)
            g.got(dst.at[(1 - zl) * 2 + 1 - c], 2)

        return start, wait, g.end

    a_y = SimpleNamespace(
        three=(0, slice(0, 3)), half=lambda p, h: (0, p, ALL, h), elem=lambda p, k, h: (0, p, k, h),
        k=4, pos=y, dev=ydev,
    )
    a_x = SimpleNamespace(
        three=(0, y, slice(0, 3)), half=lambda p, h: (0, y, p, h), elem=lambda p, k, h: (0, y, p, h),
        k=1, pos=x, dev=xdev,
    )
    b_x = SimpleNamespace(
        three=(1, ALL, slice(0, 3)), half=lambda p, h: (1, ALL, p, h), elem=lambda p, k, h: (1, k, p, h),
        k=4, pos=x, dev=xdev,
    )
    b_y = SimpleNamespace(
        three=(1, slice(0, 3), x), half=lambda p, h: (1, p, x, h), elem=lambda p, k, h: (1, p, x, h),
        k=1, pos=y, dev=ydev,
    )

    def gather_ring(buf, a, cs, base):
        def cut(at):
            return buf.at[at if cs is None else at + (ALL,) * (5 - len(at)) + (cs,)]

        g, p = Group(6, base, lambda: cut(a.three)), a.pos
        left, right, across = up(p, 3), up(p, 1), up(p, 2)

        def half(q, h):
            return cut(a.half(q, h))

        def s1():
            for i, (h, d) in enumerate(((0, 0), (1, 1), (1, 0), (0, 1))):
                g.run(lambda h=h: (half(p, h), half(p, h)), a.dev[d], i)

        def s2():
            g.got(half(left, 0), 0)
            g.run(lambda: (half(left, 0), half(left, 0)), a.dev[0], 4)
            g.got(half(right, 1), 1)
            g.run(lambda: (half(right, 1), half(right, 1)), a.dev[1], 5)

        def s3():
            g.got(half(left, 1), 2)
            g.got(half(right, 0), 3)

        def s4():
            g.got(half(across, 0), 4)
            g.got(half(across, 1), 5)

        return s1, s2, s3, s4, g.end

    def gather(buf, base, cs=None):
        one = [gather_ring(buf, a_x, cs, base), gather_ring(buf, b_y, cs, base + 6)]
        two = [gather_ring(buf, a_y, cs, base + 12), gather_ring(buf, b_x, cs, base + 18)]

        def t1():
            for r in one:
                r[0]()

        def t2():
            for r in one:
                r[1]()

        def t3():
            for r, q in zip(one, two):
                r[2]()
                r[3]()
                q[0]()

        def t4():
            for r in two:
                r[1]()

        def t5():
            for r in two:
                r[2]()

        def t6():
            for r in two:
                r[3]()
            for r in one + two:
                r[4]()

        return t1, t2, t3, t4, t5, t6

    def reduce_ring(buf, a, r2, r1, cs, bs, rows, base):
        def cut(at):
            return buf.at[at + (ALL,) * (5 - len(at)) + (cs,)]

        g, p, k = Group(6, base, lambda: cut(a.three)), a.pos, a.k
        first = ALL if k == 4 else 0
        across, beside = up(p, 2), (up(p, 1), up(p, 3))

        def half(q, h):
            return cut(a.half(q, h))

        def elem(q, n, h):
            return a.elem(q, n, h) + (ALL, cs)

        def far(i):
            return r2.at[i, first, rows, bs]

        def near(i, h):
            return r1.at[i, first, h, rows, bs]

        def loop(fn):
            if k == 1:
                fn(0)
            else:
                pl.loop(0, k)(fn)

        def s1():
            for i in (0, 1):
                g.run(lambda i=i: (half(across, i), far(i)), a.dev[i], i)

        def direct(i):
            g.run(lambda: (half(beside[i], 1 - i), near(i, 1 - i)), a.dev[i], 2 + i)

        def s2(i):
            g.got(far(i), i)
            to = beside[i]

            def add(n):
                at = elem(to, n, i)
                buf[at] = buf[at] + r2[i, n, rows, bs]

            loop(add)
            g.run(lambda: (half(to, i), near(i, i)), a.dev[i], 4 + i)

        def s3():
            for i in (0, 1):
                g.got(near(i, 1 - i), 2 + i)
                g.got(near(i, i), 4 + i)

            def add(n):
                for h in (0, 1):
                    at = elem(p, n, h)
                    total = (
                        buf[at].astype(F32)
                        + r1[0, n, h, rows, bs].astype(F32)
                        + r1[1, n, h, rows, bs].astype(F32)
                    )
                    buf[at] = total.astype(BF)

            loop(add)

        return s1, direct, s2, s3, g.end

    def scatter(buf, bufs, base, cs, bs=None, rows=ALL):
        bs = cs if bs is None else bs
        one = [
            reduce_ring(buf, a_y, bufs[0].at[0], bufs[1].at[0], cs, bs, rows, base),
            reduce_ring(buf, b_x, bufs[0].at[1], bufs[1].at[1], cs, bs, rows, base + 6),
        ]
        two = [
            reduce_ring(buf, a_x, bufs[2].at[0], bufs[3].at[0], cs, bs, rows, base + 12),
            reduce_ring(buf, b_y, bufs[2].at[1], bufs[3].at[1], cs, bs, rows, base + 18),
        ]

        def t0():
            for r in one:
                r[0]()

        def t1(i):
            for r in one:
                r[1](i)

        def t2(i):
            for r in one:
                r[2](i)

        def t3():
            for r, q in zip(one, two):
                r[3]()
                q[0]()
                q[1](0)
                q[1](1)

        def t4():
            for i in (0, 1):
                for r in two:
                    r[2](i)

        def t5():
            for r in two:
                r[3]()
            for r in one + two:
                r[4]()

        def start():
            t0()
            t1(0)
            t1(1)

        def onward():
            t2(0)
            t2(1)

        return SimpleNamespace(t0=t0, t1=t1, t2=t2, t3=t3, t4=t4, t5=t5, start=start, onward=onward)

    def place(zz, cc):
        return (lax.rem(zz, 2) * 2 + cc, lax.div(zz, 2))

    half_rows = (slice(0, 32), slice(32, 64))

    rows_base = ids(8)

    def reduce_rows(pb, rsib, rz):
        g = Group(8, rows_base)

        def mine(zz, h):
            return pb.at[place(zz, c) + (half_rows[h],)]

        def s0():
            for i, t in enumerate((zl, 1 - zl)):
                g.go(pb.at[t * 2 + 1 - c], rsib.at[t], sib, i)

        def s1():
            def add(zz):
                at = place(zz, c)
                pb[at] = pb[at] + rsib[lax.rem(zz, 2), lax.div(zz, 2)]

            g.got(rsib.at[zl], 0)
            add(zs[2])
            for i in (0, 1):
                g.go(mine(zs[2], i), rz.at[2, half_rows[i]], zdev[i], 2 + i)
            g.got(rsib.at[1 - zl], 1)
            for i in (0, 1):
                add(zs[i])
                g.go(mine(zs[i], 1 - i), rz.at[i, half_rows[1 - i]], zdev[i], 4 + i)
            add(z)

        def s2():
            for i in (0, 1):
                rows = half_rows[i]
                g.got(rz.at[2, rows], 2 + i)
                at = place(zs[i], c) + (rows,)
                pb[at] = pb[at] + rz[2, rows]
                g.go(mine(zs[i], i), rz.at[i, rows], zdev[i], 6 + i)

        def s3():
            for i in (0, 1):
                g.got(rz.at[i, half_rows[1 - i]], 4 + i)
                g.got(rz.at[i, half_rows[i]], 6 + i)

        def total(rows):
            v = pb[me, zh, rows].astype(F32)
            return v + rz[0, rows].astype(F32) + rz[1, rows].astype(F32)

        return SimpleNamespace(s0=s0, s1=s1, s2=s2, s3=s3, end=g.end, total=total)

    spread_base = ids(10)

    def gather_rows(buf):
        g = Group(10, spread_base)

        def at(zz, h):
            return buf.at[place(zz, c) + (half_rows[h],)]

        def s0():
            for i, (h, d) in enumerate(((0, 0), (1, 1), (1, 0), (0, 1))):
                g.go(at(z, h), at(z, h), zdev[d], i)
            own = buf.at[place(z, c)]
            g.go(own, own, sib, 6)

        def s1():
            g.got(at(zs[1], 0), 0)
            g.go(at(zs[1], 0), at(zs[1], 0), zdev[0], 4)
            g.got(at(zs[0], 1), 1)
            g.go(at(zs[0], 1), at(zs[0], 1), zdev[1], 5)

        def s2():
            def hand_on(zz, i):
                whole = buf.at[place(zz, c)]
                g.go(whole, whole, sib, i)

            g.got(at(zs[1], 1), 2)
            hand_on(zs[1], 7)
            g.got(at(zs[0], 0), 3)
            hand_on(zs[0], 8)
            g.got(at(zs[2], 0), 4)
            g.got(at(zs[2], 1), 5)
            hand_on(zs[2], 9)

        def s3():
            for i, zz in ((6, z), (7, zs[1]), (8, zs[0]), (9, zs[2])):
                g.got(buf.at[place(zz, 1 - c)], i)

        return SimpleNamespace(s0=s0, s1=s1, s2=s2, s3=s3, end=g.end)

    def gather_blocks(buf):
        g = Group(5)

        def s0():
            g.go(buf.at[me, 0], buf.at[me, 0], part, 0)
            g.go(buf.at[me, 1], buf.at[me, 1], other, 1)
            g.go(buf.at[me], buf.at[me], sib, 2)

        def s1():
            for h in (0, 1):
                at = buf.at[(1 - zl) * 2 + c, h]
                g.got(at, h)
                g.go(at, at, sib, 3 + h)

        def s2():
            g.got(buf.at[zl * 2 + 1 - c], 2)
            for h in (0, 1):
                g.got(buf.at[(1 - zl) * 2 + 1 - c, h], 3 + h)

        return s0, s1, s2, g.end

    def twin(buf):
        g = Group(1)

        def start():
            g.go(buf.at[zh], buf.at[zh], zdev[2], 0)

        def wait():
            g.got(buf.at[1 - zh], 0)
            g.end()

        return start, wait

    for i in range(4):
        R.wla[i, :, 0:256] = R.qw[:, i * 256 : (i + 1) * 256]
        R.wla[i, :, 256:384] = R.kw[:, i * 128 : (i + 1) * 128]
        R.wla[i, :, 384:512] = R.vw[:, i * 128 : (i + 1) * 128]
    pairs, rings = [ids(3) for _ in range(4)], [ids(24) for _ in range(4)]
    ex_a = exchange(R.wa, R.wla, pairs[0])
    ex_o = exchange(R.wo, R.wlo, pairs[1])
    ex_m = exchange(R.wm, R.wlm, pairs[2], slice(0, 1536))
    ex_d = exchange(R.wm, R.wlm, pairs[3], slice(1536, 2304))
    ag_a, ag_o = gather(R.wa, rings[0]), gather(R.wo, rings[1])
    ag_m = gather(R.wm, rings[2], slice(0, 1536))
    ag_d = gather(R.wm, rings[3], slice(1536, 2304))
    ag_x = gather_blocks(R.xn)
    ag_c = gather_blocks(R.cot)
    ag_kv = gather(R.kv, rings[0])

    pl.semaphore_wait(barrier, len(greet))
    ex_a[0]()
    for i in range(4):
        R.wlo[i] = R.ow[:, i * 256 : (i + 1) * 256]
        R.wlm[i, :, 1536:2304] = R.fd[:, i * 768 : (i + 1) * 768]
    ex_o[0]()

    shift = select(lambda r, q: q == r + me * 32, (32, 128))
    wide = mm(R.gw[...], shift).astype(BF)
    for i in range(4):
        pick = select(lambda r, q, i=i: (q == r + 2 * i) & (r < 2), (16, 8))
        R.gt_l[i] = mm(pick, wide).astype(BF)
    gates = Group(9)
    steps = (1, 3, 2)
    near_group = [(zl * 2 + 1 - c, sib), ((1 - zl) * 2 + c, part), ((1 - zl) * 2 + 1 - c, diag)]
    R.gt_in[me] = R.gt_l[me]
    for n, (i, d) in enumerate(near_group):
        gates.go(R.gt_l.at[i], R.gt_in.at[me], d, n)
    ex_d[0]()

    @pl.loop(0, 4)
    def _(t):
        rows = pl.ds(pl.multiple_of(lax.rem(t, 2) * 32, 32), 32)
        v = R.x[pl.ds(pl.multiple_of(t * 32, 32), 32), :].astype(F32)
        R.xn[me, lax.div(t, 2), rows] = (v * rms_scale(v) * R.ag[...]).astype(BF)

    ag_x[0]()
    for i in range(4):
        R.wlm[i, :, 0:768] = R.fg[:, i * 768 : (i + 1) * 768]
        R.wlm[i, :, 768:1536] = R.fu[:, i * 768 : (i + 1) * 768]
    ex_m[0]()
    first = lax.broadcasted_iota(jnp.int32, (128, 128), 1) < 64
    for i in range(4):
        base = (i // 2) * 32 + j * 2 + i % 2
        cb, sb = R.cb[pl.ds(base, 1), :], R.sb[pl.ds(base, 1), :]
        sin = sb * R.cr[...] + cb * R.sr[...]
        R.cos[i] = cb * R.cr[...] - sb * R.sr[...]
        R.sin[i] = jnp.where(first, -sin, sin)
    R.cot[me] = R.ct[...].reshape(2, 64, WIDTH)
    ex_a[1]()
    ag_a[0]()
    ex_o[1]()
    ag_o[0]()
    for n, (i, _) in enumerate(near_group):
        gates.got(R.gt_in.at[i], n)
    R.gt[y, x] = (R.gt_in[0] + R.gt_in[1]) + (R.gt_in[2] + R.gt_in[3])
    for n in range(3):
        gates.go(R.gt.at[y, x], R.gt.at[y, x], xdev[n], 3 + n)
    ag_a[1]()
    ex_d[1]()
    ag_d[0]()
    ag_o[1]()
    ag_a[2]()
    ag_x[1]()
    ag_d[1]()
    ag_a[3]()
    for n, k in enumerate(steps):
        gates.got(R.gt.at[y, up(x, 4 - k)], 3 + n)
    for n in range(3):
        gates.go(R.gt.at[y], R.gt.at[y], ydev[n], 6 + n)
    ex_m[1]()
    ag_m[0]()
    ag_a[4]()
    ag_x[2]()
    ag_a[5]()

    @pl.loop(0, 2)
    def _(zi):
        w = R.wa[...].reshape(WIDTH, PROJ)
        both = mm(R.xn[pl.ds(zi * 2, 2)].reshape(256, WIDTH), w)
        for ci in (0, 1):
            i, raw = zi * 2 + ci, both[ci * 128 : (ci + 1) * 128]
            cos, sin = R.cos[i], R.sin[i]
            R.qraw[i] = raw[:, 0:256]
            R.kraw[i] = raw[:, 256:384]
            for h in (0, 1):
                v = raw[:, h * 128 : (h + 1) * 128]
                q = rope(v * rms_scale(v) * R.qg[...], cos, sin) * (SCALE * LOG2E)
                R.qx[zi, h, ci, :, 0:128] = q.astype(BF)
            v = raw[:, 256:384]
            k = rope(v * rms_scale(v) * R.kg[...], cos, sin)
            R.kv[zi, y, x, ci, :, 0:128] = k.astype(BF)
            R.kv[zi, y, x, ci, :, 128:256] = raw[:, 384:512].astype(BF)

    ag_kv[0]()
    ag_c[0]()
    ag_m[1]()

    ones = jnp.ones((256, 128), BF)
    key_i = lax.broadcasted_iota(jnp.int32, (512, 256), 1)
    row_i = lax.broadcasted_iota(jnp.int32, (512, 256), 0)
    seen = key_i <= lax.rem(row_i, 256)
    R.oacc[...] = jnp.zeros((2, 512, 256), F32)

    def keys_of(at):
        return R.kv[at + (ALL, ALL, slice(0, 128))].reshape(256, 128)

    def values_of(at):
        v = R.kv[at + (ALL, ALL, slice(128, 256))].reshape(256, 128)
        return jnp.concatenate([v, ones], axis=1)

    def forward(tiles):
        work = []
        for g in (0, 1):
            mine = [u for u in tiles if g in u[1]]
            if mine:
                k = jnp.concatenate([keys_of(u[0]) for u in mine], axis=0)
                v = jnp.concatenate([values_of(u[0]) for u in mine], axis=0)
                scores = mm_tb(R.qx[g, :, :, :, 0:128].reshape(512, 128), k)
                work.append((g, mine, v, scores))
        for g, mine, v, scores in work:
            p = jnp.exp2(scores)
            if any(u[2] == g for u in mine):
                parts = [p[:, i * 256 : (i + 1) * 256] for i in range(len(mine))]
                parts = [jnp.where(seen, q, 0.0) if u[2] == g else q for u, q in zip(mine, parts)]
                p = jnp.concatenate(parts, axis=1)
            R.oacc[g] += mm(p.astype(BF), v)

    def tile_pair(fn, empty, at0, at1):
        t0, t1 = at0[0] * 4 + at0[1], at1[0] * 4 + at1[1]
        at0, at1 = (0,) + at0, (1,) + at1

        @pl.when((t0 < j) & (t1 < j))
        def _():
            fn([(at0, (0, 1), None), (at1, (1,), None)])

        @pl.when((t0 < j) & (t1 > j))
        def _():
            fn([(at0, (0, 1), None)])

        @pl.when((t0 > j) & (t1 < j))
        def _():
            fn([(at0, (1,), None), (at1, (1,), None)])

        @pl.when((t0 > j) & (t1 > j))
        def _():
            fn([(at0, (1,), None)])

        if empty is not None:

            @pl.when(t1 > j)
            def _():
                empty(at1)

    own = [((0, y, x), (0, 1), 0), ((1, y, x), (1,), 1)]

    def near(fn, empty=None):
        @pl.loop(1, 4)
        def _(k):
            tile_pair(fn, empty, (y, up(x, k)), (up(y, k), x))

    def side(fn, a, empty=None):
        @pl.loop(0, 4)
        def _(k):
            tile_pair(fn, empty, (up(y, a), k), (k, up(x, a)))

    forward(own)
    ag_kv[1]()
    ag_kv[2]()
    near(forward)
    ag_c[1]()
    ag_kv[3]()
    ag_o[2]()
    ag_kv[4]()

    @pl.loop(0, 3)
    def _(k):
        @pl.when(k == 2)
        def _():
            ag_kv[5]()
            ag_o[3]()
            ag_m[2]()

        side(forward, 1 + 2 * k - 3 * lax.div(k, 2))

    ag_o[4]()
    ag_o[5]()

    for n, k in enumerate(steps):
        gates.got(R.gt.at[up(y, 4 - k)], 6 + n)
    lower = lax.broadcasted_iota(jnp.int32, (16, 128), 1) < 64

    def regroup(u, w):
        return (
            jnp.where(lower, u, pltpu.roll(w, 64, 1)),
            jnp.where(lower, pltpu.roll(u, 64, 1), w),
        )

    for m in range(8):
        u, w = (R.gt[q // 4, q % 4].astype(F32) for q in (2 * m, 2 * m + 1))
        u, w = regroup(u, w)
        R.gtn[:, m * 128 : (m + 1) * 128] = u.astype(BF)
        R.gtn[:, 1024 + m * 128 : 1152 + m * 128] = w.astype(BF)

    @pl.loop(0, 2)
    def _(zi):
        v = mm_tb(R.xn[pl.ds(zi * 2, 2)].reshape(256, WIDTH), R.gtn[...])
        R.gl[pl.ds(zi * 2, 2)] = v.reshape(2, 128, 16)

    lanes = lax.broadcasted_iota(jnp.int32, (128, 128), 1)

    @pl.loop(0, 4)
    def _(i):
        zi, ci = lax.div(i, 2), lax.rem(i, 2)
        for h in (0, 1):
            rows = pl.ds(pl.multiple_of(h * 256 + ci * 128, 128), 128)
            total = R.oacc[zi, rows, 128:256]
            a = R.oacc[zi, rows, 0:128] / total
            R.att[i, :, h * 128 : (h + 1) * 128] = a
            R.qx[zi, h, ci, :, 128:256] = three_parts(-jnp.log2(total), lanes)
            gate = jax.nn.sigmoid(R.gl[i][:, h : h + 1])
            R.gated[i, :, h * 128 : (h + 1) * 128] = (a * gate).astype(BF)

    def spread(n, value):
        cols = pl.ds(pl.multiple_of(n * 256, 256), 256)
        return cols, value.reshape(4, 2, 64, 256).astype(BF)

    rs1 = reduce_rows(R.pb, R.rsib, R.rz)
    ag_n = gather_rows(R.nm)

    def project(cc):
        rows = jnp.concatenate([R.gated[cc], R.gated[2 + cc]], axis=0)

        @pl.loop(0, 8, unroll=4)
        def _(n):
            w = R.wo[lax.div(n, 4), lax.rem(n, 4)].reshape(256, 256)
            cols = pl.ds(pl.multiple_of(n * 256, 256), 256)
            v = mm_tb(rows, w).astype(BF).reshape(2, 2, 64, 256)
            R.pb[cc, :, :, cols] = v[0]
            R.pb[2 + cc, :, :, cols] = v[1]

    project(1 - c)
    rs1.s0()
    project(c)
    rs1.s1()
    rs1.s2()
    ag_m[3]()
    ag_d[2]()
    rs1.s3()

    def owned(t):
        return pl.ds(pl.multiple_of(t * 16, 16), 16)

    @pl.loop(0, 4)
    def _(t):
        rows = owned(t)
        v = R.x[pl.ds(pl.multiple_of(zh * 64 + t * 16, 16), 16), :].astype(F32)
        v = v + rs1.total(rows)
        R.hid[rows] = v
        R.nm[me, zh, rows] = (v * rms_scale(v) * R.fgain[...]).astype(BF)

    rs1.end()
    for g in (ex_a, ex_o, ex_m, ex_d):
        g[2]()
    gates.end()
    ag_n.s0()
    ag_c[2]()
    ag_n.s1()
    ag_m[4]()
    ag_n.s2()
    ag_m[5]()
    ag_d[3]()
    ag_n.s3()

    def weight(k, n):
        at = pl.ds(pl.multiple_of(k * 768 + n * 256, 256), 256)
        return R.wm[:, :, :, :, :, at].reshape(WIDTH, 256)

    @pl.loop(0, 3, unroll=3)
    def _(n):
        cols = pl.ds(pl.multiple_of(n * 256, 256), 256)
        rows = R.nm[...].reshape(512, WIDTH)
        gate = mm(rows, weight(0, n))
        upper = mm(rows, weight(1, n))
        sg = jax.nn.sigmoid(gate)
        silu = gate * sg
        R.act[0, :, cols] = (upper * (sg * (1.0 + gate * (1.0 - sg)))).astype(BF)
        R.act[1, :, cols] = silu.astype(BF)
        R.act[2, :, cols] = (silu * upper).astype(BF)

    def block(n):
        return (lax.div(n, 4), lax.rem(n, 4), ALL, ALL, ALL)

    def turned(ref, n):
        cols = pl.ds(pl.multiple_of(n * 256, 256), 256)
        return ref[:, :, :, cols].reshape(512, 256).T

    big = (R.m_r2, R.m_r1, R.m_q2, R.m_q1)
    rs_d = scatter(R.ga, big, rings[1], slice(0, 768))
    rs_m = scatter(R.wm, big, rings[2], slice(0, 1536), slice(768, 2304))

    @pl.loop(0, 8, unroll=4)
    def _(n):
        g = mm(turned(R.cot, n), R.act[2])
        R.ga[block(n) + (slice(0, 768),)] = g.astype(BF).reshape(4, 2, 32, 768)

    rs_d.start()
    ag_d[4]()
    ag_d[5]()

    @pl.loop(0, 3, unroll=3)
    def _(n):
        cols = pl.ds(pl.multiple_of(n * 256, 256), 256)
        grad = mm(R.cot[...].reshape(512, WIDTH), weight(2, n))
        R.act[0, :, cols] = (grad * R.act[0, :, cols].astype(F32)).astype(BF)
        R.act[1, :, cols] = (grad * R.act[1, :, cols].astype(F32)).astype(BF)

    @pl.loop(0, 8, unroll=4)
    def _(n):
        at = block(n)
        v = mm_tb(R.act[0], R.wm[at + (slice(0, 768),)].reshape(256, 768))
        v = v + mm_tb(R.act[1], R.wm[at + (slice(768, 1536),)].reshape(256, 768))
        cols, v = spread(n, v)
        R.pb[:, :, :, cols] = v

    rs2 = reduce_rows(R.pb, R.rsib, R.rz)
    rs_f = reduce_rows(R.pb2, R.rsib, R.rz)
    rs2.s0()

    def feed_weights(n):
        at = block(n)
        t = turned(R.nm, n)
        R.wm[at + (slice(0, 768),)] = mm(t, R.act[0]).astype(BF).reshape(4, 2, 32, 768)
        R.wm[at + (slice(768, 1536),)] = mm(t, R.act[1]).astype(BF).reshape(4, 2, 32, 768)

    pl.loop(0, 4, unroll=4)(feed_weights)
    rs2.s1()
    rs_d.onward()
    pl.loop(4, 8, unroll=4)(feed_weights)
    rs_m.start()
    rs2.s2()

    def tell(devices, sem):
        for d in devices:
            pl.semaphore_signal(sem, inc=1, device_id=d, device_id_type=MESH)

    group = [sib] + zdev
    ring = xdev[:2] + ydev[:2]
    ag_n.end()
    tell(group, R.free.at[0])
    ag_h = gather_rows(R.nm)

    @pl.loop(0, 8, unroll=4)
    def _(n):
        w = R.wm[block(n) + (slice(1536, 2304),)].reshape(256, 768)
        cols, v = spread(n, mm_tb(R.act[2], w))
        R.pb2[:, :, :, cols] = v

    R.dgs[...] = jnp.zeros((2, WIDTH), F32)
    ag_c[3]()
    rs2.s3()
    pl.semaphore_wait(R.free.at[0], 4)

    @pl.loop(0, 4)
    def _(t):
        rows = owned(t)
        dv, dg = rms_back(R.hid[rows], R.fgain[...], rs2.total(rows))
        dh = dv + R.ct[pl.ds(pl.multiple_of(zh * 64 + t * 16, 16), 16), :].astype(F32)
        R.dgs[1:2, :] += dg
        R.gh[rows] = dh
        R.nm[me, zh, rows] = dh.astype(BF)

    rs2.end()
    ag_h.s0()
    rs_d.t3()
    ag_h.s1()
    rs_m.onward()
    ag_h.s2()
    ag_h.s3()
    rs_f.s0()

    @pl.loop(0, 2)
    def _(zi):
        w = R.wo[...].reshape(WIDTH, 256)
        both = mm(R.nm[pl.ds(zi * 2, 2)].reshape(256, WIDTH), w)
        for ci in (0, 1):
            i, grad = zi * 2 + ci, both[ci * 128 : (ci + 1) * 128]
            logits = jnp.zeros((128, 128), F32)
            for h in (0, 1):
                gate = jax.nn.sigmoid(R.gl[i][:, h : h + 1])
                gr = grad[:, h * 128 : (h + 1) * 128]
                a = R.att[i, :, h * 128 : (h + 1) * 128]
                low = (gr * gate).astype(BF)
                dl = jnp.sum(gr * a, axis=1, keepdims=True) * (gate * (1.0 - gate))
                logits = jnp.where(lanes == h, dl, logits)
                delta = jnp.sum(low.astype(F32) * a, axis=1, keepdims=True)
                R.dox[zi, h, ci, :, 0:128] = low
                R.dox[zi, h, ci, :, 128:256] = three_parts(-delta, lanes)
            R.gsc[i, :, 512:640] = logits.astype(BF)

    rs_f.s1()

    R.oacc[...] = jnp.zeros((2, 512, 256), F32)
    row_t = lax.broadcasted_iota(jnp.int32, (256, 512), 1)
    key_t = lax.broadcasted_iota(jnp.int32, (256, 512), 0)
    seen_t = key_t <= lax.rem(row_t, 256)

    def backward(tiles):
        at = [u[0] for u in tiles]
        k = [keys_of(u) for u in at]
        kx = [jnp.concatenate([u, ones], axis=1) for u in k]
        vx = [values_of(u) for u in at]
        kt = [u.T for u in k]
        q = [R.qx[g].reshape(512, 256) for g in (0, 1)]
        d = [R.dox[g].reshape(512, 256) for g in (0, 1)]
        units = [(i, g, u[2] == g) for i, u in enumerate(tiles) for g in u[1]]
        p = [mm_tb(kx[i], q[g]) for i, g, _ in units]
        dp = [mm_tb(vx[i], d[g]) for i, g, _ in units]
        p = [jnp.exp2(u) for u in p]
        p = [jnp.where(seen_t, u, 0.0) if cut else u for u, (_, _, cut) in zip(p, units)]
        ds = [(u * w).astype(BF) for u, w in zip(p, dp)]
        p = [u.astype(BF) for u in p]
        dv = [mm(u, d[g][:, 0:128]) for u, (_, g, _) in zip(p, units)]
        dk = [mm(u, q[g][:, 0:128]) for u, (_, g, _) in zip(ds, units)]
        dq = [mm(kt[i], u) for u, (i, _, _) in zip(ds, units)]
        for g in (0, 1):
            mine = [u for u, (_, h, _) in zip(dq, units) if h == g]
            if mine:
                total = sum(mine[1:], mine[0])
                R.oacc[g, 0:128] += total[:, 0:256]
                R.oacc[g, 128:256] += total[:, 256:512]
        for i, place in enumerate(at):
            mine = [n for n, u in enumerate(units) if u[0] == i]
            first, rest = mine[0], mine[1:]
            total = sum([dk[n] for n in rest], dk[first])
            R.kv[place + (ALL, ALL, slice(0, 128))] = total.astype(BF).reshape(2, 128, 128)
            total = sum([dv[n] for n in rest], dv[first])
            R.kv[place + (ALL, ALL, slice(128, 256))] = total.astype(BF).reshape(2, 128, 128)

    def nothing(at):
        R.kv[at] = jnp.zeros((2, 128, 256), BF)

    small = (R.k_r2, R.k_r1, R.k_q2, R.k_q1)
    rs_k = scatter(R.kv, small, rings[0], slice(0, 256))

    @pl.loop(0, 3)
    def _(k):
        side(backward, 2 - k + 3 * lax.div(k, 2), nothing)

        @pl.when(k == 0)
        def _():
            rs_k.t0()

        @pl.when(k == 1)
        def _():
            rs_k.t1(0)
            rs_d.t4()

        @pl.when(k == 2)
        def _():
            rs_k.t1(1)

    rs_f.s2()
    rs_k.t2(0)
    rs_k.t2(1)
    rs_m.t3()
    near(backward, nothing)
    backward(own)
    rs_f.s3()
    tw_o = twin(R.ob)

    @pl.loop(0, 4)
    def _(t):
        rows = owned(t)
        R.ob[zh, rows] = (R.hid[rows] + rs_f.total(rows)).astype(BF)

    rs_f.end()
    tell(group, R.free.at[1])
    tw_o[0]()

    rs_d.t5()
    tell(ring, R.free.at[2])
    R.wm[:, y, x, :, :, 1536:2304] = R.ga[:, y, x, :, :, 0:768]
    rs_k.t3()
    rs_m.t4()

    R.dgh[...] = jnp.zeros((8, 128), F32)

    @pl.loop(0, 4)
    def _(i):
        zi, ci = lax.div(i, 2), lax.rem(i, 2)
        for h in (0, 1):
            cols = pl.ds(pl.multiple_of(ci * 128, 128), 128)
            dq = R.oacc[zi, h * 128 : (h + 1) * 128, cols].T * SCALE
            dq = rope_back(dq, R.cos[i], R.sin[i])
            dv, dg = rms_back(R.qraw[i, :, h * 128 : (h + 1) * 128], R.qg[...], dq)
            R.dgh[0:1, :] += dg
            R.gsc[i, :, h * 128 : (h + 1) * 128] = dv.astype(BF)

    rs_k.t4()

    turned_gates = R.gsc[:, :, 512:640].reshape(512, 128).T[0:16]

    @pl.loop(0, 8, unroll=4)
    def _(n):
        at = block(n)
        g = mm(turned(R.nm, n), R.gated[...].reshape(512, 256))
        R.ga[at + (slice(0, 256),)] = g.astype(BF).reshape(4, 2, 32, 256)
        t = turned(R.xn, n)
        g = mm(t, R.gsc[:, :, 0:256].reshape(512, 256))
        R.ga[at + (slice(256, 512),)] = g.astype(BF).reshape(4, 2, 32, 256)
        cols = pl.ds(pl.multiple_of(n * 256, 256), 256)
        R.gtg[:, cols] = mm(turned_gates, R.xn[:, :, :, cols].reshape(512, 256))

    for m in range(8):
        u, w = (R.gtg[:, q + m * 128 : q + (m + 1) * 128] for q in (0, 1024))
        u, w = regroup(u, w)
        R.gg[m // 2, m % 2 * 2] = u.astype(BF)
        R.gg[m // 2, m % 2 * 2 + 1] = w.astype(BF)
    gates = Group(9, gates.base)
    for n, k in enumerate(steps):
        gates.go(R.gg.at[up(y, k)], R.gg_y.at[n], ydev[n], 6 + n)
    rs_e = scatter(R.ga, big, rings[3], slice(0, 512))
    pl.semaphore_wait(R.free.at[2], 4)
    rs_e.start()
    rs_m.t5()
    gb_m = give_back(R.wm, R.wlm, pairs[0])
    gb_m[0]()
    rs_k.t5()

    @pl.loop(0, 4)
    def _(i):
        zi, ci = lax.div(i, 2), lax.rem(i, 2)
        dk = R.kv[zi, y, x, ci, :, 0:128].astype(F32) * LN2
        dk = rope_back(dk, R.cos[i], R.sin[i])
        dv, dg = rms_back(R.kraw[i], R.kg[...], dk)
        R.dgh[1:2, :] += dg
        R.gsc[i, :, 256:384] = dv.astype(BF)
        R.gsc[i, :, 384:512] = R.kv[zi, y, x, ci, :, 128:256]

    @pl.loop(0, 8, unroll=4)
    def _(n):
        g = mm(turned(R.xn, n), R.gsc[:, :, 256:512].reshape(512, 256))
        R.ga[block(n) + (slice(512, 768),)] = g.astype(BF).reshape(4, 2, 32, 256)

    rs_l = scatter(R.ga, small, rings[1], slice(512, 768), slice(0, 256), slice(0, 32))
    rs_l.start()

    @pl.loop(0, 8, unroll=4)
    def _(n):
        at = block(n)
        v = mm_tb(R.gsc[:, :, 0:512].reshape(512, 512), R.wa[at].reshape(256, PROJ))
        cols = pl.ds(pl.multiple_of(n * 256, 256), 256)
        v = v + mm(R.gsc[:, :, 512:528].reshape(512, 16), R.gtn[:, cols])
        dg = jnp.sum(v * R.xn[:, :, :, cols].reshape(512, 256).astype(F32), axis=0, keepdims=True)
        R.dgs[0:1, cols] = dg / R.ag[:, cols]
        cols, v = spread(n, v)
        R.pb[:, :, :, cols] = v

    rs3 = reduce_rows(R.pb, R.rsib, R.rz)
    pl.semaphore_wait(R.free.at[1], 4)
    rs3.s0()

    for r in range(16):
        R.sums[0, r : r + 1, :] = R.dgs[0:1, r * 128 : (r + 1) * 128]
        R.sums[0, 16 + r : 17 + r, :] = R.dgs[1:2, r * 128 : (r + 1) * 128]
    R.sums[0, 32:40, :] = R.dgh[...]

    def add_up(stage, devices):
        g, first = Group(len(devices)), (0, 7, 10)[stage]
        for i, d in enumerate(devices):
            g.go(R.sums.at[stage], R.came.at[first + i], d, i)

        def finish():
            v = R.sums[stage]
            for i in range(len(devices)):
                g.got(R.came.at[first + i], i)
                v = v + R.came[first + i]
            R.sums[stage + 1] = v
            g.end()

        return finish

    fin = add_up(0, group + zsib)
    rs_e.onward()
    for n in range(3):
        gates.got(R.gg_y.at[n], 6 + n)
    v = R.gg[y].astype(F32)
    for n in range(3):
        v = v + R.gg_y[n].astype(F32)
    R.gg[y] = v.astype(BF)
    for n, k in enumerate(steps):
        gates.go(R.gg.at[y, up(x, k)], R.gg_x.at[n], xdev[n], 3 + n)
    rs3.s1()
    rs_l.onward()
    rs3.s2()
    fin()
    fin = add_up(1, xdev)
    rs_e.t3()
    rs_l.t3()
    for n in range(3):
        gates.got(R.gg_x.at[n], 3 + n)
    v = R.gg[y, x].astype(F32)
    for n in range(3):
        v = v + R.gg_x[n].astype(F32)
    R.gt_out[me] = v.astype(BF)
    for n, (_, d) in enumerate(near_group):
        gates.go(R.gt_out.at[me], R.gt_out.at[me], d, n)
    rs_e.t4()
    rs3.s3()
    tw_i = twin(R.ib)

    @pl.loop(0, 4)
    def _(t):
        rows = owned(t)
        v = R.x[pl.ds(pl.multiple_of(zh * 64 + t * 16, 16), 16), :].astype(F32)
        dv, _ = rms_back(v, R.ag[...], rs3.total(rows))
        R.ib[zh, rows] = (R.gh[rows] + dv).astype(BF)

    tw_i[0]()
    rs3.end()
    fin()
    fin = add_up(2, ydev)
    rs_l.t4()
    rs_e.t5()
    rs_l.t5()
    gb_a = give_back(R.ga, R.wl8, pairs[1])
    gb_a[0]()

    def put(i, src, dst):
        cp = pltpu.make_async_copy(src, dst, R.put.at[i])
        cp.start()
        return cp

    gb_m[1]()
    puts = [put(0, R.wlm, R.o_fm)]
    tw_o[1]()
    puts.append(put(1, R.ob, R.o_out))
    fin()
    puts.append(put(2, R.sums.at[3], R.o_gain))
    tw_i[1]()
    puts.append(put(3, R.ib, R.o_in))
    for n, (i, _) in enumerate(near_group):
        gates.got(R.gt_out.at[i], n)
    gates.end()
    puts.append(put(5, R.gt_out, R.o_gt))
    gb_a[1]()
    puts.append(put(4, R.wl8, R.o_fa))
    for cp in puts:
        cp.wait()
    ag_x[3]()
    ag_h.end()
    gb_m[2]()
    gb_a[2]()
    assert (count[0], sends[0]) == (COPIES, SENDS), (count, sends)


INPUTS = [
    *("x", "ct", "ag", "qg", "kg", "fgain"),
    *("qw", "kw", "vw", "gw", "ow", "fg", "fu", "fd"),
    *("cr", "sr", "cb", "sb"),
]
OUTPUTS = [
    ("o_out", (2, 64, WIDTH), BF),
    ("o_in", (2, 64, WIDTH), BF),
    ("o_gain", (40, 128), F32),
    ("o_fm", (4, 32, 2304), BF),
    ("o_fa", (4, 32, ATT), BF),
    ("o_gt", (4, 16, 128), BF),
]
RESULTS = [
    ((128, WIDTH), BF),
    ((128, WIDTH), BF),
    ((1, 32), F32),
    ((32, 1024), F32),
    ((32, 512), F32),
    ((32, 512), F32),
    ((8, 32), F32),
    ((1, 128), F32),
    ((1, 128), F32),
    ((32, 1024), F32),
    ((1, 32), F32),
    ((32, 3072), F32),
    ((32, 3072), F32),
    ((32, 3072), F32),
]
SCRATCH = [
    ("wla", (4, 32, PROJ), BF),
    ("wlo", (4, 32, 256), BF),
    ("wl8", (4, 32, ATT), BF),
    ("wlm", (4, 32, 2304), BF),
    ("wa", (2, 4, 4, 2, 32, PROJ), BF),
    ("wo", (2, 4, 4, 2, 32, 256), BF),
    ("gt_l", (4, 16, 128), BF),
    ("gt_in", (4, 16, 128), BF),
    ("gt", (4, 4, 16, 128), BF),
    ("gtn", (16, WIDTH), BF),
    ("gtg", (16, WIDTH), F32),
    ("gg", (4, 4, 16, 128), BF),
    ("gg_y", (3, 4, 16, 128), BF),
    ("gg_x", (3, 16, 128), BF),
    ("gt_out", (4, 16, 128), BF),
    ("ga", (2, 4, 4, 2, 32, ATT), BF),
    ("wm", (2, 4, 4, 2, 32, 2304), BF),
    ("kv", (2, 4, 4, 2, 128, 256), BF),
    ("xn", (4, 2, 64, WIDTH), BF),
    ("cot", (4, 2, 64, WIDTH), BF),
    ("nm", (4, 2, 64, WIDTH), BF),
    ("cos", (4, 128, 128), F32),
    ("sin", (4, 128, 128), F32),
    ("qraw", (4, 128, 256), F32),
    ("kraw", (4, 128, 128), F32),
    ("gl", (4, 128, 16), F32),
    ("qx", (2, 2, 2, 128, 256), BF),
    ("dox", (2, 2, 2, 128, 256), BF),
    ("oacc", (2, 512, 256), F32),
    ("att", (4, 128, 256), F32),
    ("gated", (4, 128, 256), BF),
    ("gsc", (4, 128, 640), BF),
    ("act", (3, 512, 768), BF),
    ("hid", (64, WIDTH), F32),
    ("gh", (64, WIDTH), F32),
    ("dgs", (2, WIDTH), F32),
    ("dgh", (8, 128), F32),
    ("pb", (4, 2, 64, WIDTH), BF),
    ("pb2", (4, 2, 64, WIDTH), BF),
    ("rsib", (2, 2, 64, WIDTH), BF),
    ("rz", (3, 64, WIDTH), BF),
    ("m_r2", (2, 2, 4, 32, 2304), BF),
    ("m_r1", (2, 2, 4, 2, 32, 2304), BF),
    ("m_q2", (2, 2, 1, 32, 2304), BF),
    ("m_q1", (2, 2, 1, 2, 32, 2304), BF),
    ("k_r2", (2, 2, 4, 128, 256), BF),
    ("k_r1", (2, 2, 4, 2, 128, 256), BF),
    ("k_q2", (2, 2, 1, 128, 256), BF),
    ("k_q1", (2, 2, 1, 2, 128, 256), BF),
    ("ob", (2, 64, WIDTH), BF),
    ("ib", (2, 64, WIDTH), BF),
    ("sums", (4, 40, 128), F32),
    ("came", (13, 40, 128), F32),
]
COPIES, SENDS = 160, 80


def kernel(*refs):
    names = INPUTS + [o[0] for o in OUTPUTS] + [v[0] for v in SCRATCH] + ["send", "recv", "free", "put"]
    body(SimpleNamespace(**dict(zip(names, refs))))


def finish(out, grad_in, gain, fm, fa, gt, *to):
    to[0][...] = out[...].reshape(128, WIDTH)
    to[1][...] = grad_in[...].reshape(128, WIDTH)
    place = lax.axis_index("seq")
    for at, first in ((2, 0), (10, 16)):
        v = gain[pl.ds(first + lax.div(place, 4), 1), :]
        to[at][...] = pltpu.roll(v, lax.rem(128 - lax.rem(place, 4) * 32, 128), 1)[:, 0:32]
    to[7][...] = gain[32:33, :]
    to[8][...] = gain[33:34, :]
    ours = lax.div(place, 32) * 2 + lax.rem(place, 2)
    for i in range(4):
        wide = slice(i * 256, (i + 1) * 256)
        low = slice(i * 128, (i + 1) * 128)
        to[9][:, wide] = fa[i, :, 0:256].astype(F32)
        to[3][:, wide] = fa[i, :, 256:512].astype(F32)
        to[4][:, low] = fa[i, :, 512:640].astype(F32)
        to[5][:, low] = fa[i, :, 640:768].astype(F32)
        tile = pltpu.roll(gt[i].astype(F32), lax.rem(128 - ours * 32, 128), 1)
        to[6][2 * i : 2 * i + 2, :] = tile[0:2, 0:32]
        for k in range(3):
            cols = slice(k * 768, (k + 1) * 768)
            to[11 + k][:, i * 768 : (i + 1) * 768] = fm[i, :, cols].astype(F32)


def rope_tables():
    inverse = ROPE_BASE ** (-np.arange(HEAD // 2) * 2.0 / HEAD)
    inverse = np.concatenate([inverse, inverse]).astype(np.float32).astype(np.float64)
    rows = np.arange(128)[:, None] * inverse
    blocks = np.arange(64)[:, None] * 128 * inverse
    return [jnp.asarray(f(a), F32) for a in (rows, blocks) for f in (np.cos, np.sin)]


def per_device(
    inputs,
    attention_gain,
    query_weight,
    key_matrix,
    value_matrix,
    gate_weight,
    query_gain,
    key_gain,
    out_weight,
    feed_gain,
    feed_gate,
    feed_up,
    feed_down,
    cotangent,
):
    vmem = pl.BlockSpec(memory_space=pltpu.VMEM)
    out = pl.pallas_call(
        kernel,
        out_shape=[jax.ShapeDtypeStruct(shape, kind) for _, shape, kind in OUTPUTS],
        in_specs=[vmem] * len(INPUTS),
        out_specs=[pl.BlockSpec(memory_space=pl.ANY)] * len(OUTPUTS),
        scratch_shapes=[pltpu.VMEM(shape, kind) for _, shape, kind in SCRATCH]
        + [pltpu.SemaphoreType.DMA((SENDS,)), pltpu.SemaphoreType.DMA((COPIES,))]
        + [pltpu.SemaphoreType.REGULAR((3,)), pltpu.SemaphoreType.DMA((6,))],
        compiler_params=pltpu.CompilerParams(
            collective_id=0, has_side_effects=True, vmem_limit_bytes=63 * 2**20
        ),
        name="block",
    )(
        inputs,
        cotangent,
        attention_gain.reshape(1, WIDTH),
        query_gain.reshape(1, HEAD),
        key_gain.reshape(1, HEAD),
        feed_gain.reshape(1, WIDTH),
        query_weight,
        key_matrix,
        value_matrix,
        gate_weight.T,
        out_weight.T,
        feed_gate,
        feed_up,
        feed_down.T,
        *rope_tables(),
    )
    out = pl.pallas_call(
        finish,
        out_shape=[jax.ShapeDtypeStruct(shape, kind) for shape, kind in RESULTS],
        compiler_params=pltpu.CompilerParams(vmem_limit_bytes=60 * 2**20),
        name="results",
    )(*out)
    out = list(out)
    for i in (2, 7, 8, 10):
        out[i] = out[i].reshape(-1)
    for i in (6, 9, 13):
        out[i] = out[i].T
    return tuple(out)


def solution(mesh):
    seq, both, turned = P("seq", None), P("seq", "grp"), P("grp", "seq")
    in_specs = (seq, P(), both, both, both, both, P(), P(), turned, P(), both, both, turned, seq)
    out_specs = (
        seq, seq, P("seq"), both, both, both, both, P(), P(), turned, P("seq"), both, both, turned,
    )
    return jax.shard_map(
        per_device, mesh=mesh, in_specs=in_specs, out_specs=out_specs, check_vma=False
    )
```

```python
from types import SimpleNamespace

import jax
import jax.numpy as jnp
import numpy as np
from jax import lax
from jax.experimental import pallas as pl
from jax.experimental.pallas import tpu as pltpu
from jax.sharding import PartitionSpec as P

EPSILON = 1e-06
ROPE_BASE = 1000000.0
WIDTH = 2048
HEAD = 128
EIGHTH = 768
ATT = 768
PROJ = 512
SCALE = HEAD**-0.5
LOG2E = 1.4426950408889634
LN2 = 0.6931471805599453
BF, F32 = jnp.bfloat16, jnp.float32
MESH = pl.DeviceIdType.MESH
ALL = slice(None)


def mm(a, b):
    return jnp.dot(a, b, preferred_element_type=F32)


def mm_tb(a, b):
    return lax.dot_general(a, b, (((1,), (1,)), ((), ())), preferred_element_type=F32)


def rms_scale(v):
    return lax.rsqrt(jnp.mean(v * v, axis=-1, keepdims=True) + EPSILON)


def rms_back(v, gain, dy):
    r = rms_scale(v)
    u = gain * dy
    dv = r * (u - v * (r * r * jnp.mean(u * v, axis=-1, keepdims=True)))
    return dv, jnp.sum(dy * v * r, axis=0, keepdims=True)


def rope(v, cos, sin):
    return v * cos + pltpu.roll(v, HEAD // 2, 1) * sin


def rope_back(v, cos, sin):
    return v * cos + pltpu.roll(v * sin, HEAD // 2, 1)


def three_parts(v, lanes):
    hi = v.astype(BF).astype(F32)
    mid = (v - hi).astype(BF).astype(F32)
    low = v - hi - mid
    return jnp.where(
        lanes == 0, hi, jnp.where(lanes == 1, mid, jnp.where(lanes == 2, low, 0.0))
    ).astype(BF)


def select(row_of, shape):
    row = lax.broadcasted_iota(jnp.int32, shape, 0)
    col = lax.broadcasted_iota(jnp.int32, shape, 1)
    return jnp.where(row_of(row, col), 1.0, 0.0).astype(BF)


def body(R):
    s, zh = lax.axis_index("seq"), lax.axis_index("grp")
    c = lax.rem(s, 2)
    x = lax.rem(lax.div(s, 2), 4)
    y = lax.rem(lax.div(s, 8), 4)
    zl = lax.div(s, 32)
    z = zh * 2 + zl
    j = y * 4 + x
    me = zl * 2 + c

    def up(v, k):
        return lax.rem(v + k, 4)

    def dev(zz, yy, xx, cc):
        return (lax.rem(zz, 2) * 32 + yy * 8 + xx * 2 + cc, lax.div(zz, 2))

    sib = dev(z, y, x, 1 - c)
    zs = [up(z, 1), up(z, 3), up(z, 2)]
    zdev = [dev(v, y, x, c) for v in zs]
    part = (zl_dev := (1 - zl) * 32 + y * 8 + x * 2 + c, zh)
    diag = ((1 - zl) * 32 + y * 8 + x * 2 + 1 - c, zh)
    other = (zl_dev, 1 - zh)
    xdev = [dev(z, y, up(x, k), c) for k in (1, 3, 2)]
    ydev = [dev(z, up(y, k), x, c) for k in (1, 3, 2)]

    barrier = pltpu.get_barrier_semaphore()
    zsib = [dev(v, y, x, 1 - c) for v in zs]
    greet = [sib] + zdev + zsib + xdev + ydev
    for d in greet:
        pl.semaphore_signal(barrier, inc=1, device_id=d, device_id_type=MESH)

    count, sends, first_send = [0], [0], {}

    def take(counter, k):
        counter[0] += k
        return counter[0] - k

    def ids(k):
        return take(count, k)

    class Group:
        def __init__(self, k, base=None, whole=None):
            self.base, self.whole, self.sent = ids(k) if base is None else base, whole, []
            if self.base not in first_send:
                first_send[self.base] = take(sends, 1 if whole else k)

        def copy(self, src, dst, d, i):
            out = first_send[self.base] + (0 if self.whole else i)
            return pltpu.make_async_remote_copy(
                src_ref=src, dst_ref=dst, send_sem=R.send.at[out],
                recv_sem=R.recv.at[self.base + i], device_id=d, device_id_type=MESH,
            )

        def run(self, ends, d, i):
            self.copy(*ends(), d, i).start()
            self.sent.append(lambda: self.copy(*ends(), d, i))

        def go(self, src, dst, d, i):
            self.run(lambda: (src, dst), d, i)

        def got(self, ref, i):
            self.copy(ref, ref, sib, i).wait_recv()

        def end(self):
            if self.whole:
                ref = self.whole()
                self.copy(ref, ref, sib, 0).wait_send()
            else:
                for cp in self.sent:
                    cp().wait_send()

    def exchange(buf, wl, base, cs=ALL):
        g = Group(3, base)

        def start():
            buf[zl, y, x, c, :, cs] = wl[me, :, cs]
            dst = buf.at[zl, y, x, c, :, cs]
            g.go(wl.at[zl * 2 + 1 - c, :, cs], dst, sib, 0)
            g.go(wl.at[(1 - zl) * 2 + c, :, cs], dst, part, 1)
            g.go(wl.at[(1 - zl) * 2 + 1 - c, :, cs], dst, diag, 2)

        def wait():
            g.got(buf.at[zl, y, x, 1 - c, :, cs], 0)
            g.got(buf.at[1 - zl, y, x, c, :, cs], 1)
            g.got(buf.at[1 - zl, y, x, 1 - c, :, cs], 2)

        return start, wait, g.end

    def give_back(src, dst, base):
        g = Group(3, base)

        def start():
            dst[me] = src[zl, y, x, c]
            g.go(src.at[zl, y, x, 1 - c], dst.at[me], sib, 0)
            g.go(src.at[1 - zl, y, x, c], dst.at[me], part, 1)
            g.go(src.at[1 - zl, y, x, 1 - c], dst.at[me], diag, 2)

        def wait():
            g.got(dst.at[zl * 2 + 1 - c], 0)
            g.got(dst.at[(1 - zl) * 2 + c], 1)
            g.got(dst.at[(1 - zl) * 2 + 1 - c], 2)

        return start, wait, g.end

    a_y = SimpleNamespace(
        three=(0, slice(0, 3)), half=lambda p, h: (0, p, ALL, h), elem=lambda p, k, h: (0, p, k, h),
        k=4, pos=y, dev=ydev,
    )
    a_x = SimpleNamespace(
        three=(0, y, slice(0, 3)), half=lambda p, h: (0, y, p, h), elem=lambda p, k, h: (0, y, p, h),
        k=1, pos=x, dev=xdev,
    )
    b_x = SimpleNamespace(
        three=(1, ALL, slice(0, 3)), half=lambda p, h: (1, ALL, p, h), elem=lambda p, k, h: (1, k, p, h),
        k=4, pos=x, dev=xdev,
    )
    b_y = SimpleNamespace(
        three=(1, slice(0, 3), x), half=lambda p, h: (1, p, x, h), elem=lambda p, k, h: (1, p, x, h),
        k=1, pos=y, dev=ydev,
    )

    def gather_ring(buf, a, cs, base):
        def cut(at):
            return buf.at[at if cs is None else at + (ALL,) * (5 - len(at)) + (cs,)]

        g, p = Group(6, base, lambda: cut(a.three)), a.pos
        left, right, across = up(p, 3), up(p, 1), up(p, 2)

        def half(q, h):
            return cut(a.half(q, h))

        def s1():
            for i, (h, d) in enumerate(((0, 0), (1, 1), (1, 0), (0, 1))):
                g.run(lambda h=h: (half(p, h), half(p, h)), a.dev[d], i)

        def s2():
            g.got(half(left, 0), 0)
            g.run(lambda: (half(left, 0), half(left, 0)), a.dev[0], 4)
            g.got(half(right, 1), 1)
            g.run(lambda: (half(right, 1), half(right, 1)), a.dev[1], 5)

        def s3():
            g.got(half(left, 1), 2)
            g.got(half(right, 0), 3)

        def s4():
            g.got(half(across, 0), 4)
            g.got(half(across, 1), 5)

        return s1, s2, s3, s4, g.end

    def gather(buf, base, cs=None):
        one = [gather_ring(buf, a_x, cs, base), gather_ring(buf, b_y, cs, base + 6)]
        two = [gather_ring(buf, a_y, cs, base + 12), gather_ring(buf, b_x, cs, base + 18)]

        def t1():
            for r in one:
                r[0]()

        def t2():
            for r in one:
                r[1]()

        def t3():
            for r, q in zip(one, two):
                r[2]()
                r[3]()
                q[0]()

        def t4():
            for r in two:
                r[1]()

        def t5():
            for r in two:
                r[2]()

        def t6():
            for r in two:
                r[3]()
            for r in one + two:
                r[4]()

        return t1, t2, t3, t4, t5, t6

    def reduce_ring(buf, a, r2, r1, cs, bs, rows, base):
        def cut(at):
            return buf.at[at + (ALL,) * (5 - len(at)) + (cs,)]

        g, p, k = Group(6, base, lambda: cut(a.three)), a.pos, a.k
        first = ALL if k == 4 else 0
        across, beside = up(p, 2), (up(p, 1), up(p, 3))

        def half(q, h):
            return cut(a.half(q, h))

        def elem(q, n, h):
            return a.elem(q, n, h) + (ALL, cs)

        def far(i):
            return r2.at[i, first, rows, bs]

        def near(i, h):
            return r1.at[i, first, h, rows, bs]

        def loop(fn):
            if k == 1:
                fn(0)
            else:
                pl.loop(0, k)(fn)

        def s1():
            for i in (0, 1):
                g.run(lambda i=i: (half(across, i), far(i)), a.dev[i], i)

        def direct(i):
            g.run(lambda: (half(beside[i], 1 - i), near(i, 1 - i)), a.dev[i], 2 + i)

        def s2(i):
            g.got(far(i), i)
            to = beside[i]

            def add(n):
                at = elem(to, n, i)
                buf[at] = buf[at] + r2[i, n, rows, bs]

            loop(add)
            g.run(lambda: (half(to, i), near(i, i)), a.dev[i], 4 + i)

        def s3():
            for i in (0, 1):
                g.got(near(i, 1 - i), 2 + i)
                g.got(near(i, i), 4 + i)

            def add(n):
                for h in (0, 1):
                    at = elem(p, n, h)
                    total = (
                        buf[at].astype(F32)
                        + r1[0, n, h, rows, bs].astype(F32)
                        + r1[1, n, h, rows, bs].astype(F32)
                    )
                    buf[at] = total.astype(BF)

            loop(add)

        return s1, direct, s2, s3, g.end

    def scatter(buf, bufs, base, cs, bs=None, rows=ALL):
        bs = cs if bs is None else bs
        one = [
            reduce_ring(buf, a_y, bufs[0].at[0], bufs[1].at[0], cs, bs, rows, base),
            reduce_ring(buf, b_x, bufs[0].at[1], bufs[1].at[1], cs, bs, rows, base + 6),
        ]
        two = [
            reduce_ring(buf, a_x, bufs[2].at[0], bufs[3].at[0], cs, bs, rows, base + 12),
            reduce_ring(buf, b_y, bufs[2].at[1], bufs[3].at[1], cs, bs, rows, base + 18),
        ]

        def t0():
            for r in one:
                r[0]()

        def t1(i):
            for r in one:
                r[1](i)

        def t2(i):
            for r in one:
                r[2](i)

        def t3():
            for r, q in zip(one, two):
                r[3]()
                q[0]()
                q[1](0)
                q[1](1)

        def t4():
            for i in (0, 1):
                for r in two:
                    r[2](i)

        def t5():
            for r in two:
                r[3]()
            for r in one + two:
                r[4]()

        def start():
            t0()
            t1(0)
            t1(1)

        def onward():
            t2(0)
            t2(1)

        return SimpleNamespace(t0=t0, t1=t1, t2=t2, t3=t3, t4=t4, t5=t5, start=start, onward=onward)

    def place(zz, cc):
        return (lax.rem(zz, 2) * 2 + cc, lax.div(zz, 2))

    half_rows = (slice(0, 32), slice(32, 64))

    rows_base = ids(8)

    def reduce_rows(pb, rsib, rz):
        g = Group(8, rows_base)

        def mine(zz, h):
            return pb.at[place(zz, c) + (half_rows[h],)]

        def s0():
            for i, t in enumerate((zl, 1 - zl)):
                g.go(pb.at[t * 2 + 1 - c], rsib.at[t], sib, i)

        def s1():
            def add(zz):
                at = place(zz, c)
                pb[at] = pb[at] + rsib[lax.rem(zz, 2), lax.div(zz, 2)]

            g.got(rsib.at[zl], 0)
            add(zs[2])
            for i in (0, 1):
                g.go(mine(zs[2], i), rz.at[2, half_rows[i]], zdev[i], 2 + i)
            g.got(rsib.at[1 - zl], 1)
            for i in (0, 1):
                add(zs[i])
                g.go(mine(zs[i], 1 - i), rz.at[i, half_rows[1 - i]], zdev[i], 4 + i)
            add(z)

        def s2():
            for i in (0, 1):
                rows = half_rows[i]
                g.got(rz.at[2, rows], 2 + i)
                at = place(zs[i], c) + (rows,)
                pb[at] = pb[at] + rz[2, rows]
                g.go(mine(zs[i], i), rz.at[i, rows], zdev[i], 6 + i)

        def s3():
            for i in (0, 1):
                g.got(rz.at[i, half_rows[1 - i]], 4 + i)
                g.got(rz.at[i, half_rows[i]], 6 + i)

        def total(rows):
            v = pb[me, zh, rows].astype(F32)
            return v + rz[0, rows].astype(F32) + rz[1, rows].astype(F32)

        return SimpleNamespace(s0=s0, s1=s1, s2=s2, s3=s3, end=g.end, total=total)

    spread_base = ids(10)

    def gather_rows(buf):
        g = Group(10, spread_base)

        def at(zz, h):
            return buf.at[place(zz, c) + (half_rows[h],)]

        def s0():
            for i, (h, d) in enumerate(((0, 0), (1, 1), (1, 0), (0, 1))):
                g.go(at(z, h), at(z, h), zdev[d], i)
            own = buf.at[place(z, c)]
            g.go(own, own, sib, 6)

        def s1():
            g.got(at(zs[1], 0), 0)
            g.go(at(zs[1], 0), at(zs[1], 0), zdev[0], 4)
            g.got(at(zs[0], 1), 1)
            g.go(at(zs[0], 1), at(zs[0], 1), zdev[1], 5)

        def s2():
            def hand_on(zz, i):
                whole = buf.at[place(zz, c)]
                g.go(whole, whole, sib, i)

            g.got(at(zs[1], 1), 2)
            hand_on(zs[1], 7)
            g.got(at(zs[0], 0), 3)
            hand_on(zs[0], 8)
            g.got(at(zs[2], 0), 4)
            g.got(at(zs[2], 1), 5)
            hand_on(zs[2], 9)

        def s3():
            for i, zz in ((6, z), (7, zs[1]), (8, zs[0]), (9, zs[2])):
                g.got(buf.at[place(zz, 1 - c)], i)

        return SimpleNamespace(s0=s0, s1=s1, s2=s2, s3=s3, end=g.end)

    def gather_blocks(buf):
        g = Group(5)

        def s0():
            g.go(buf.at[me, 0], buf.at[me, 0], part, 0)
            g.go(buf.at[me, 1], buf.at[me, 1], other, 1)
            g.go(buf.at[me], buf.at[me], sib, 2)

        def s1():
            for h in (0, 1):
                at = buf.at[(1 - zl) * 2 + c, h]
                g.got(at, h)
                g.go(at, at, sib, 3 + h)

        def s2():
            g.got(buf.at[zl * 2 + 1 - c], 2)
            for h in (0, 1):
                g.got(buf.at[(1 - zl) * 2 + 1 - c, h], 3 + h)

        return s0, s1, s2, g.end

    def twin(buf):
        g = Group(1)

        def start():
            g.go(buf.at[zh], buf.at[zh], zdev[2], 0)

        def wait():
            g.got(buf.at[1 - zh], 0)
            g.end()

        return start, wait

    for i in range(4):
        R.wla[i, :, 0:256] = R.qw[:, i * 256 : (i + 1) * 256]
        R.wla[i, :, 256:384] = R.kw[:, i * 128 : (i + 1) * 128]
        R.wla[i, :, 384:512] = R.vw[:, i * 128 : (i + 1) * 128]
    pairs, rings = [ids(3) for _ in range(4)], [ids(24) for _ in range(4)]
    ex_a = exchange(R.wa, R.wla, pairs[0])
    ex_o = exchange(R.wo, R.wlo, pairs[1])
    ex_m = exchange(R.wm, R.wlm, pairs[2], slice(0, 1536))
    ex_d = exchange(R.wm, R.wlm, pairs[3], slice(1536, 2304))
    ag_a, ag_o = gather(R.wa, rings[0]), gather(R.wo, rings[1])
    ag_m = gather(R.wm, rings[2], slice(0, 1536))
    ag_d = gather(R.wm, rings[3], slice(1536, 2304))
    ag_x = gather_blocks(R.xn)
    ag_c = gather_blocks(R.cot)
    ag_kv = gather(R.kv, rings[0])

    pl.semaphore_wait(barrier, len(greet))
    ex_a[0]()
    for i in range(4):
        R.wlo[i] = R.ow[:, i * 256 : (i + 1) * 256]
        R.wlm[i, :, 1536:2304] = R.fd[:, i * 768 : (i + 1) * 768]
    ex_o[0]()

    shift = select(lambda r, q: q == r + me * 32, (32, 128))
    wide = mm(R.gw[...], shift).astype(BF)
    for i in range(4):
        pick = select(lambda r, q, i=i: (q == r + 2 * i) & (r < 2), (16, 8))
        R.gt_l[i] = mm(pick, wide).astype(BF)
    gates = Group(9)
    steps = (1, 3, 2)
    near_group = [(zl * 2 + 1 - c, sib), ((1 - zl) * 2 + c, part), ((1 - zl) * 2 + 1 - c, diag)]
    R.gt_in[me] = R.gt_l[me]
    for n, (i, d) in enumerate(near_group):
        gates.go(R.gt_l.at[i], R.gt_in.at[me], d, n)
    ex_d[0]()

    @pl.loop(0, 4)
    def _(t):
        rows = pl.ds(pl.multiple_of(lax.rem(t, 2) * 32, 32), 32)
        v = R.x[pl.ds(pl.multiple_of(t * 32, 32), 32), :].astype(F32)
        R.xn[me, lax.div(t, 2), rows] = (v * rms_scale(v) * R.ag[...]).astype(BF)

    ag_x[0]()
    for i in range(4):
        R.wlm[i, :, 0:768] = R.fg[:, i * 768 : (i + 1) * 768]
        R.wlm[i, :, 768:1536] = R.fu[:, i * 768 : (i + 1) * 768]
    ex_m[0]()
    first = lax.broadcasted_iota(jnp.int32, (128, 128), 1) < 64
    for i in range(4):
        base = (i // 2) * 32 + j * 2 + i % 2
        cb, sb = R.cb[pl.ds(base, 1), :], R.sb[pl.ds(base, 1), :]
        sin = sb * R.cr[...] + cb * R.sr[...]
        R.cos[i] = cb * R.cr[...] - sb * R.sr[...]
        R.sin[i] = jnp.where(first, -sin, sin)
    R.cot[me] = R.ct[...].reshape(2, 64, WIDTH)
    ex_a[1]()
    ag_a[0]()
    ex_o[1]()
    ag_o[0]()
    for n, (i, _) in enumerate(near_group):
        gates.got(R.gt_in.at[i], n)
    R.gt[y, x] = (R.gt_in[0] + R.gt_in[1]) + (R.gt_in[2] + R.gt_in[3])
    for n in range(3):
        gates.go(R.gt.at[y, x], R.gt.at[y, x], xdev[n], 3 + n)
    ag_a[1]()
    ex_d[1]()
    ag_d[0]()
    ag_o[1]()
    ag_a[2]()
    ag_x[1]()
    ag_d[1]()
    ag_a[3]()
    for n, k in enumerate(steps):
        gates.got(R.gt.at[y, up(x, 4 - k)], 3 + n)
    for n in range(3):
        gates.go(R.gt.at[y], R.gt.at[y], ydev[n], 6 + n)
    ex_m[1]()
    ag_m[0]()
    ag_a[4]()
    ag_x[2]()
    ag_a[5]()

    @pl.loop(0, 2)
    def _(zi):
        w = R.wa[...].reshape(WIDTH, PROJ)
        both = mm(R.xn[pl.ds(zi * 2, 2)].reshape(256, WIDTH), w)
        for ci in (0, 1):
            i, raw = zi * 2 + ci, both[ci * 128 : (ci + 1) * 128]
            cos, sin = R.cos[i], R.sin[i]
            R.qraw[i] = raw[:, 0:256]
            R.kraw[i] = raw[:, 256:384]
            for h in (0, 1):
                v = raw[:, h * 128 : (h + 1) * 128]
                q = rope(v * rms_scale(v) * R.qg[...], cos, sin) * (SCALE * LOG2E)
                R.qx[zi, h, ci, :, 0:128] = q.astype(BF)
            v = raw[:, 256:384]
            k = rope(v * rms_scale(v) * R.kg[...], cos, sin)
            R.kv[zi, y, x, ci, :, 0:128] = k.astype(BF)
            R.kv[zi, y, x, ci, :, 128:256] = raw[:, 384:512].astype(BF)

    ag_kv[0]()
    ag_c[0]()
    ag_m[1]()

    ones = jnp.ones((256, 128), BF)
    key_i = lax.broadcasted_iota(jnp.int32, (512, 256), 1)
    row_i = lax.broadcasted_iota(jnp.int32, (512, 256), 0)
    seen = key_i <= lax.rem(row_i, 256)
    R.oacc[...] = jnp.zeros((2, 512, 256), F32)

    def keys_of(at):
        return R.kv[at + (ALL, ALL, slice(0, 128))].reshape(256, 128)

    def values_of(at):
        v = R.kv[at + (ALL, ALL, slice(128, 256))].reshape(256, 128)
        return jnp.concatenate([v, ones], axis=1)

    def forward(tiles):
        work = []
        for g in (0, 1):
            mine = [u for u in tiles if g in u[1]]
            if mine:
                k = jnp.concatenate([keys_of(u[0]) for u in mine], axis=0)
                v = jnp.concatenate([values_of(u[0]) for u in mine], axis=0)
                scores = mm_tb(R.qx[g, :, :, :, 0:128].reshape(512, 128), k)
                work.append((g, mine, v, scores))
        for g, mine, v, scores in work:
            p = jnp.exp2(scores)
            if any(u[2] == g for u in mine):
                parts = [p[:, i * 256 : (i + 1) * 256] for i in range(len(mine))]
                parts = [jnp.where(seen, q, 0.0) if u[2] == g else q for u, q in zip(mine, parts)]
                p = jnp.concatenate(parts, axis=1)
            R.oacc[g] += mm(p.astype(BF), v)

    def tile_pair(fn, empty, at0, at1):
        t0, t1 = at0[0] * 4 + at0[1], at1[0] * 4 + at1[1]
        at0, at1 = (0,) + at0, (1,) + at1

        @pl.when((t0 < j) & (t1 < j))
        def _():
            fn([(at0, (0, 1), None), (at1, (1,), None)])

        @pl.when((t0 < j) & (t1 > j))
        def _():
            fn([(at0, (0, 1), None)])

        @pl.when((t0 > j) & (t1 < j))
        def _():
            fn([(at0, (1,), None), (at1, (1,), None)])

        @pl.when((t0 > j) & (t1 > j))
        def _():
            fn([(at0, (1,), None)])

        if empty is not None:

            @pl.when(t1 > j)
            def _():
                empty(at1)

    own = [((0, y, x), (0, 1), 0), ((1, y, x), (1,), 1)]

    def near(fn, empty=None):
        @pl.loop(1, 4)
        def _(k):
            tile_pair(fn, empty, (y, up(x, k)), (up(y, k), x))

    def side(fn, a, empty=None):
        @pl.loop(0, 4)
        def _(k):
            tile_pair(fn, empty, (up(y, a), k), (k, up(x, a)))

    forward(own)
    ag_kv[1]()
    ag_kv[2]()
    near(forward)
    ag_c[1]()
    ag_kv[3]()
    ag_o[2]()
    ag_kv[4]()

    @pl.loop(0, 3)
    def _(k):
        @pl.when(k == 2)
        def _():
            ag_kv[5]()
            ag_o[3]()
            ag_m[2]()

        side(forward, 1 + 2 * k - 3 * lax.div(k, 2))

    ag_o[4]()
    ag_o[5]()

    for n, k in enumerate(steps):
        gates.got(R.gt.at[up(y, 4 - k)], 6 + n)
    lower = lax.broadcasted_iota(jnp.int32, (16, 128), 1) < 64

    def regroup(u, w):
        return (
            jnp.where(lower, u, pltpu.roll(w, 64, 1)),
            jnp.where(lower, pltpu.roll(u, 64, 1), w),
        )

    for m in range(8):
        u, w = (R.gt[q // 4, q % 4].astype(F32) for q in (2 * m, 2 * m + 1))
        u, w = regroup(u, w)
        R.gtn[:, m * 128 : (m + 1) * 128] = u.astype(BF)
        R.gtn[:, 1024 + m * 128 : 1152 + m * 128] = w.astype(BF)

    @pl.loop(0, 2)
    def _(zi):
        v = mm_tb(R.xn[pl.ds(zi * 2, 2)].reshape(256, WIDTH), R.gtn[...])
        R.gl[pl.ds(zi * 2, 2)] = v.reshape(2, 128, 16)

    lanes = lax.broadcasted_iota(jnp.int32, (128, 128), 1)

    @pl.loop(0, 4)
    def _(i):
        zi, ci = lax.div(i, 2), lax.rem(i, 2)
        for h in (0, 1):
            rows = pl.ds(pl.multiple_of(h * 256 + ci * 128, 128), 128)
            total = R.oacc[zi, rows, 128:256]
            a = R.oacc[zi, rows, 0:128] / total
            R.att[i, :, h * 128 : (h + 1) * 128] = a
            R.qx[zi, h, ci, :, 128:256] = three_parts(-jnp.log2(total), lanes)
            gate = jax.nn.sigmoid(R.gl[i][:, h : h + 1])
            R.gated[i, :, h * 128 : (h + 1) * 128] = (a * gate).astype(BF)

    def spread(n, value):
        cols = pl.ds(pl.multiple_of(n * 256, 256), 256)
        return cols, value.reshape(4, 2, 64, 256).astype(BF)

    rs1 = reduce_rows(R.pb, R.rsib, R.rz)
    ag_n = gather_rows(R.nm)

    def project(cc):
        rows = jnp.concatenate([R.gated[cc], R.gated[2 + cc]], axis=0)

        @pl.loop(0, 8, unroll=4)
        def _(n):
            w = R.wo[lax.div(n, 4), lax.rem(n, 4)].reshape(256, 256)
            cols = pl.ds(pl.multiple_of(n * 256, 256), 256)
            v = mm_tb(rows, w).astype(BF).reshape(2, 2, 64, 256)
            R.pb[cc, :, :, cols] = v[0]
            R.pb[2 + cc, :, :, cols] = v[1]

    project(1 - c)
    rs1.s0()
    project(c)
    rs1.s1()
    rs1.s2()
    ag_m[3]()
    ag_d[2]()
    rs1.s3()

    def owned(t):
        return pl.ds(pl.multiple_of(t * 16, 16), 16)

    @pl.loop(0, 4)
    def _(t):
        rows = owned(t)
        v = R.x[pl.ds(pl.multiple_of(zh * 64 + t * 16, 16), 16), :].astype(F32)
        v = v + rs1.total(rows)
        R.hid[rows] = v
        R.nm[me, zh, rows] = (v * rms_scale(v) * R.fgain[...]).astype(BF)

    rs1.end()
    for g in (ex_a, ex_o, ex_m, ex_d):
        g[2]()
    gates.end()
    ag_n.s0()
    ag_c[2]()
    ag_n.s1()
    ag_m[4]()
    ag_n.s2()
    ag_m[5]()
    ag_d[3]()
    ag_n.s3()

    def weight(k, n):
        at = pl.ds(pl.multiple_of(k * 768 + n * 256, 256), 256)
        return R.wm[:, :, :, :, :, at].reshape(WIDTH, 256)

    @pl.loop(0, 3, unroll=3)
    def _(n):
        cols = pl.ds(pl.multiple_of(n * 256, 256), 256)
        rows = R.nm[...].reshape(512, WIDTH)
        gate = mm(rows, weight(0, n))
        upper = mm(rows, weight(1, n))
        sg = jax.nn.sigmoid(gate)
        silu = gate * sg
        R.act[0, :, cols] = (upper * (sg * (1.0 + gate * (1.0 - sg)))).astype(BF)
        R.act[1, :, cols] = silu.astype(BF)
        R.act[2, :, cols] = (silu * upper).astype(BF)

    def block(n):
        return (lax.div(n, 4), lax.rem(n, 4), ALL, ALL, ALL)

    def turned(ref, n):
        cols = pl.ds(pl.multiple_of(n * 256, 256), 256)
        return ref[:, :, :, cols].reshape(512, 256).T

    big = (R.m_r2, R.m_r1, R.m_q2, R.m_q1)
    rs_d = scatter(R.ga, big, rings[1], slice(0, 768))
    rs_m = scatter(R.wm, big, rings[2], slice(0, 1536), slice(768, 2304))

    @pl.loop(0, 8, unroll=4)
    def _(n):
        g = mm(turned(R.cot, n), R.act[2])
        R.ga[block(n) + (slice(0, 768),)] = g.astype(BF).reshape(4, 2, 32, 768)

    rs_d.start()
    ag_d[4]()
    ag_d[5]()

    @pl.loop(0, 3, unroll=3)
    def _(n):
        cols = pl.ds(pl.multiple_of(n * 256, 256), 256)
        grad = mm(R.cot[...].reshape(512, WIDTH), weight(2, n))
        R.act[0, :, cols] = (grad * R.act[0, :, cols].astype(F32)).astype(BF)
        R.act[1, :, cols] = (grad * R.act[1, :, cols].astype(F32)).astype(BF)

    @pl.loop(0, 8, unroll=4)
    def _(n):
        at = block(n)
        v = mm_tb(R.act[0], R.wm[at + (slice(0, 768),)].reshape(256, 768))
        v = v + mm_tb(R.act[1], R.wm[at + (slice(768, 1536),)].reshape(256, 768))
        cols, v = spread(n, v)
        R.pb[:, :, :, cols] = v

    rs2 = reduce_rows(R.pb, R.rsib, R.rz)
    rs_f = reduce_rows(R.pb2, R.rsib, R.rz)
    rs2.s0()

    def feed_weights(n):
        at = block(n)
        t = turned(R.nm, n)
        R.wm[at + (slice(0, 768),)] = mm(t, R.act[0]).astype(BF).reshape(4, 2, 32, 768)
        R.wm[at + (slice(768, 1536),)] = mm(t, R.act[1]).astype(BF).reshape(4, 2, 32, 768)

    pl.loop(0, 4, unroll=4)(feed_weights)
    rs2.s1()
    rs_d.onward()
    pl.loop(4, 8, unroll=4)(feed_weights)
    rs_m.start()
    rs2.s2()

    def tell(devices, sem):
        for d in devices:
            pl.semaphore_signal(sem, inc=1, device_id=d, device_id_type=MESH)

    group = [sib] + zdev
    ring = xdev[:2] + ydev[:2]
    ag_n.end()
    tell(group, R.free.at[0])
    ag_h = gather_rows(R.nm)

    @pl.loop(0, 8, unroll=4)
    def _(n):
        w = R.wm[block(n) + (slice(1536, 2304),)].reshape(256, 768)
        cols, v = spread(n, mm_tb(R.act[2], w))
        R.pb2[:, :, :, cols] = v

    R.dgs[...] = jnp.zeros((2, WIDTH), F32)
    ag_c[3]()
    rs2.s3()
    pl.semaphore_wait(R.free.at[0], 4)

    @pl.loop(0, 4)
    def _(t):
        rows = owned(t)
        dv, dg = rms_back(R.hid[rows], R.fgain[...], rs2.total(rows))
        dh = dv + R.ct[pl.ds(pl.multiple_of(zh * 64 + t * 16, 16), 16), :].astype(F32)
        R.dgs[1:2, :] += dg
        R.gh[rows] = dh
        R.nm[me, zh, rows] = dh.astype(BF)

    rs2.end()
    ag_h.s0()
    rs_d.t3()
    ag_h.s1()
    rs_m.onward()
    ag_h.s2()
    ag_h.s3()
    rs_f.s0()

    @pl.loop(0, 2)
    def _(zi):
        w = R.wo[...].reshape(WIDTH, 256)
        both = mm(R.nm[pl.ds(zi * 2, 2)].reshape(256, WIDTH), w)
        for ci in (0, 1):
            i, grad = zi * 2 + ci, both[ci * 128 : (ci + 1) * 128]
            logits = jnp.zeros((128, 128), F32)
            for h in (0, 1):
                gate = jax.nn.sigmoid(R.gl[i][:, h : h + 1])
                gr = grad[:, h * 128 : (h + 1) * 128]
                a = R.att[i, :, h * 128 : (h + 1) * 128]
                low = (gr * gate).astype(BF)
                dl = jnp.sum(gr * a, axis=1, keepdims=True) * (gate * (1.0 - gate))
                logits = jnp.where(lanes == h, dl, logits)
                delta = jnp.sum(low.astype(F32) * a, axis=1, keepdims=True)
                R.dox[zi, h, ci, :, 0:128] = low
                R.dox[zi, h, ci, :, 128:256] = three_parts(-delta, lanes)
            R.gsc[i, :, 512:640] = logits.astype(BF)


    R.oacc[...] = jnp.zeros((2, 512, 256), F32)
    row_t = lax.broadcasted_iota(jnp.int32, (256, 512), 1)
    key_t = lax.broadcasted_iota(jnp.int32, (256, 512), 0)
    seen_t = key_t <= lax.rem(row_t, 256)

    def backward(tiles):
        at = [u[0] for u in tiles]
        k = [keys_of(u) for u in at]
        kx = [jnp.concatenate([u, ones], axis=1) for u in k]
        vx = [values_of(u) for u in at]
        kt = [u.T for u in k]
        q = [R.qx[g].reshape(512, 256) for g in (0, 1)]
        d = [R.dox[g].reshape(512, 256) for g in (0, 1)]
        units = [(i, g, u[2] == g) for i, u in enumerate(tiles) for g in u[1]]
        p = [mm_tb(kx[i], q[g]) for i, g, _ in units]
        dp = [mm_tb(vx[i], d[g]) for i, g, _ in units]
        p = [jnp.exp2(u) for u in p]
        p = [jnp.where(seen_t, u, 0.0) if cut else u for u, (_, _, cut) in zip(p, units)]
        ds = [(u * w).astype(BF) for u, w in zip(p, dp)]
        p = [u.astype(BF) for u in p]
        dv = [mm(u, d[g][:, 0:128]) for u, (_, g, _) in zip(p, units)]
        dk = [mm(u, q[g][:, 0:128]) for u, (_, g, _) in zip(ds, units)]
        dq = [mm(kt[i], u) for u, (i, _, _) in zip(ds, units)]
        for g in (0, 1):
            mine = [u for u, (_, h, _) in zip(dq, units) if h == g]
            if mine:
                total = sum(mine[1:], mine[0])
                R.oacc[g, 0:128] += total[:, 0:256]
                R.oacc[g, 128:256] += total[:, 256:512]
        for i, place in enumerate(at):
            mine = [n for n, u in enumerate(units) if u[0] == i]
            first, rest = mine[0], mine[1:]
            total = sum([dk[n] for n in rest], dk[first])
            R.kv[place + (ALL, ALL, slice(0, 128))] = total.astype(BF).reshape(2, 128, 128)
            total = sum([dv[n] for n in rest], dv[first])
            R.kv[place + (ALL, ALL, slice(128, 256))] = total.astype(BF).reshape(2, 128, 128)

    def nothing(at):
        R.kv[at] = jnp.zeros((2, 128, 256), BF)

    small = (R.k_r2, R.k_r1, R.k_q2, R.k_q1)
    rs_k = scatter(R.kv, small, rings[0], slice(0, 256))

    @pl.loop(0, 3)
    def _(k):
        side(backward, 2 - k + 3 * lax.div(k, 2), nothing)

        @pl.when(k == 0)
        def _():
            rs_k.t0()

        @pl.when(k == 1)
        def _():
            rs_k.t1(0)
            rs_d.t4()

        @pl.when(k == 2)
        def _():
            rs_k.t1(1)

    rs_f.s1()
    rs_k.t2(0)
    rs_k.t2(1)
    rs_m.t3()
    near(backward, nothing)
    backward(own)
    rs_f.s2()
    rs_d.t5()
    rs_f.s3()
    tw_o = twin(R.ob)

    @pl.loop(0, 4)
    def _(t):
        rows = owned(t)
        R.ob[zh, rows] = (R.hid[rows] + rs_f.total(rows)).astype(BF)

    rs_f.end()
    tell(group, R.free.at[1])
    tw_o[0]()

    tell(ring, R.free.at[2])
    R.wm[:, y, x, :, :, 1536:2304] = R.ga[:, y, x, :, :, 0:768]
    rs_k.t3()
    rs_m.t4()

    R.dgh[...] = jnp.zeros((8, 128), F32)

    @pl.loop(0, 4)
    def _(i):
        zi, ci = lax.div(i, 2), lax.rem(i, 2)
        for h in (0, 1):
            cols = pl.ds(pl.multiple_of(ci * 128, 128), 128)
            dq = R.oacc[zi, h * 128 : (h + 1) * 128, cols].T * SCALE
            dq = rope_back(dq, R.cos[i], R.sin[i])
            dv, dg = rms_back(R.qraw[i, :, h * 128 : (h + 1) * 128], R.qg[...], dq)
            R.dgh[0:1, :] += dg
            R.gsc[i, :, h * 128 : (h + 1) * 128] = dv.astype(BF)

    rs_k.t4()

    turned_gates = R.gsc[:, :, 512:640].reshape(512, 128).T[0:16]

    @pl.loop(0, 8, unroll=4)
    def _(n):
        at = block(n)
        g = mm(turned(R.nm, n), R.gated[...].reshape(512, 256))
        R.ga[at + (slice(0, 256),)] = g.astype(BF).reshape(4, 2, 32, 256)
        t = turned(R.xn, n)
        g = mm(t, R.gsc[:, :, 0:256].reshape(512, 256))
        R.ga[at + (slice(256, 512),)] = g.astype(BF).reshape(4, 2, 32, 256)
        cols = pl.ds(pl.multiple_of(n * 256, 256), 256)
        R.gtg[:, cols] = mm(turned_gates, R.xn[:, :, :, cols].reshape(512, 256))

    for m in range(8):
        u, w = (R.gtg[:, q + m * 128 : q + (m + 1) * 128] for q in (0, 1024))
        u, w = regroup(u, w)
        R.gg[m // 2, m % 2 * 2] = u.astype(BF)
        R.gg[m // 2, m % 2 * 2 + 1] = w.astype(BF)
    gates = Group(9, gates.base)
    for n, k in enumerate(steps):
        gates.go(R.gg.at[up(y, k)], R.gg_y.at[n], ydev[n], 6 + n)
    rs_e = scatter(R.ga, big, rings[3], slice(0, 512))
    pl.semaphore_wait(R.free.at[2], 4)
    rs_e.start()
    rs_m.t5()
    gb_m = give_back(R.wm, R.wlm, pairs[0])
    gb_m[0]()
    rs_k.t5()

    @pl.loop(0, 4)
    def _(i):
        zi, ci = lax.div(i, 2), lax.rem(i, 2)
        dk = R.kv[zi, y, x, ci, :, 0:128].astype(F32) * LN2
        dk = rope_back(dk, R.cos[i], R.sin[i])
        dv, dg = rms_back(R.kraw[i], R.kg[...], dk)
        R.dgh[1:2, :] += dg
        R.gsc[i, :, 256:384] = dv.astype(BF)
        R.gsc[i, :, 384:512] = R.kv[zi, y, x, ci, :, 128:256]

    @pl.loop(0, 8, unroll=4)
    def _(n):
        g = mm(turned(R.xn, n), R.gsc[:, :, 256:512].reshape(512, 256))
        R.ga[block(n) + (slice(512, 768),)] = g.astype(BF).reshape(4, 2, 32, 256)

    rs_l = scatter(R.ga, small, rings[1], slice(512, 768), slice(0, 256), slice(0, 32))
    rs_l.start()

    @pl.loop(0, 8, unroll=4)
    def _(n):
        at = block(n)
        v = mm_tb(R.gsc[:, :, 0:512].reshape(512, 512), R.wa[at].reshape(256, PROJ))
        cols = pl.ds(pl.multiple_of(n * 256, 256), 256)
        v = v + mm(R.gsc[:, :, 512:528].reshape(512, 16), R.gtn[:, cols])
        dg = jnp.sum(v * R.xn[:, :, :, cols].reshape(512, 256).astype(F32), axis=0, keepdims=True)
        R.dgs[0:1, cols] = dg / R.ag[:, cols]
        cols, v = spread(n, v)
        R.pb[:, :, :, cols] = v

    rs3 = reduce_rows(R.pb, R.rsib, R.rz)
    pl.semaphore_wait(R.free.at[1], 4)
    rs3.s0()

    for r in range(16):
        R.sums[0, r : r + 1, :] = R.dgs[0:1, r * 128 : (r + 1) * 128]
        R.sums[0, 16 + r : 17 + r, :] = R.dgs[1:2, r * 128 : (r + 1) * 128]
    R.sums[0, 32:40, :] = R.dgh[...]

    def add_up(stage, devices):
        g, first = Group(len(devices)), (0, 7, 10)[stage]
        for i, d in enumerate(devices):
            g.go(R.sums.at[stage], R.came.at[first + i], d, i)

        def finish():
            v = R.sums[stage]
            for i in range(len(devices)):
                g.got(R.came.at[first + i], i)
                v = v + R.came[first + i]
            R.sums[stage + 1] = v
            g.end()

        return finish

    fin = add_up(0, group + zsib)
    rs_e.onward()
    for n in range(3):
        gates.got(R.gg_y.at[n], 6 + n)
    v = R.gg[y].astype(F32)
    for n in range(3):
        v = v + R.gg_y[n].astype(F32)
    R.gg[y] = v.astype(BF)
    for n, k in enumerate(steps):
        gates.go(R.gg.at[y, up(x, k)], R.gg_x.at[n], xdev[n], 3 + n)
    rs3.s1()
    rs_l.onward()
    rs3.s2()
    fin()
    fin = add_up(1, xdev)
    rs_e.t3()
    rs_l.t3()
    for n in range(3):
        gates.got(R.gg_x.at[n], 3 + n)
    v = R.gg[y, x].astype(F32)
    for n in range(3):
        v = v + R.gg_x[n].astype(F32)
    R.gt_out[me] = v.astype(BF)
    for n, (_, d) in enumerate(near_group):
        gates.go(R.gt_out.at[me], R.gt_out.at[me], d, n)
    rs_e.t4()
    rs3.s3()
    tw_i = twin(R.ib)

    @pl.loop(0, 4)
    def _(t):
        rows = owned(t)
        v = R.x[pl.ds(pl.multiple_of(zh * 64 + t * 16, 16), 16), :].astype(F32)
        dv, _ = rms_back(v, R.ag[...], rs3.total(rows))
        R.ib[zh, rows] = (R.gh[rows] + dv).astype(BF)

    tw_i[0]()
    rs3.end()
    fin()
    fin = add_up(2, ydev)
    rs_l.t4()
    rs_e.t5()
    rs_l.t5()
    gb_a = give_back(R.ga, R.wl8, pairs[1])
    gb_a[0]()

    def put(i, src, dst):
        cp = pltpu.make_async_copy(src, dst, R.put.at[i])
        cp.start()
        return cp

    gb_m[1]()
    puts = [put(0, R.wlm, R.o_fm)]
    tw_o[1]()
    puts.append(put(1, R.ob, R.o_out))
    fin()
    puts.append(put(2, R.sums.at[3], R.o_gain))
    tw_i[1]()
    puts.append(put(3, R.ib, R.o_in))
    for n, (i, _) in enumerate(near_group):
        gates.got(R.gt_out.at[i], n)
    gates.end()
    puts.append(put(5, R.gt_out, R.o_gt))
    gb_a[1]()
    puts.append(put(4, R.wl8, R.o_fa))
    for cp in puts:
        cp.wait()
    ag_x[3]()
    ag_h.end()
    gb_m[2]()
    gb_a[2]()
    assert (count[0], sends[0]) == (COPIES, SENDS), (count, sends)


INPUTS = [
    *("x", "ct", "ag", "qg", "kg", "fgain"),
    *("qw", "kw", "vw", "gw", "ow", "fg", "fu", "fd"),
    *("cr", "sr", "cb", "sb"),
]
OUTPUTS = [
    ("o_out", (2, 64, WIDTH), BF),
    ("o_in", (2, 64, WIDTH), BF),
    ("o_gain", (40, 128), F32),
    ("o_fm", (4, 32, 2304), BF),
    ("o_fa", (4, 32, ATT), BF),
    ("o_gt", (4, 16, 128), BF),
]
RESULTS = [
    ((128, WIDTH), BF),
    ((128, WIDTH), BF),
    ((1, 32), F32),
    ((32, 1024), F32),
    ((32, 512), F32),
    ((32, 512), F32),
    ((8, 32), F32),
    ((1, 128), F32),
    ((1, 128), F32),
    ((32, 1024), F32),
    ((1, 32), F32),
    ((32, 3072), F32),
    ((32, 3072), F32),
    ((32, 3072), F32),
]
SCRATCH = [
    ("wla", (4, 32, PROJ), BF),
    ("wlo", (4, 32, 256), BF),
    ("wl8", (4, 32, ATT), BF),
    ("wlm", (4, 32, 2304), BF),
    ("wa", (2, 4, 4, 2, 32, PROJ), BF),
    ("wo", (2, 4, 4, 2, 32, 256), BF),
    ("gt_l", (4, 16, 128), BF),
    ("gt_in", (4, 16, 128), BF),
    ("gt", (4, 4, 16, 128), BF),
    ("gtn", (16, WIDTH), BF),
    ("gtg", (16, WIDTH), F32),
    ("gg", (4, 4, 16, 128), BF),
    ("gg_y", (3, 4, 16, 128), BF),
    ("gg_x", (3, 16, 128), BF),
    ("gt_out", (4, 16, 128), BF),
    ("ga", (2, 4, 4, 2, 32, ATT), BF),
    ("wm", (2, 4, 4, 2, 32, 2304), BF),
    ("kv", (2, 4, 4, 2, 128, 256), BF),
    ("xn", (4, 2, 64, WIDTH), BF),
    ("cot", (4, 2, 64, WIDTH), BF),
    ("nm", (4, 2, 64, WIDTH), BF),
    ("cos", (4, 128, 128), F32),
    ("sin", (4, 128, 128), F32),
    ("qraw", (4, 128, 256), F32),
    ("kraw", (4, 128, 128), F32),
    ("gl", (4, 128, 16), F32),
    ("qx", (2, 2, 2, 128, 256), BF),
    ("dox", (2, 2, 2, 128, 256), BF),
    ("oacc", (2, 512, 256), F32),
    ("att", (4, 128, 256), F32),
    ("gated", (4, 128, 256), BF),
    ("gsc", (4, 128, 640), BF),
    ("act", (3, 512, 768), BF),
    ("hid", (64, WIDTH), F32),
    ("gh", (64, WIDTH), F32),
    ("dgs", (2, WIDTH), F32),
    ("dgh", (8, 128), F32),
    ("pb", (4, 2, 64, WIDTH), BF),
    ("pb2", (4, 2, 64, WIDTH), BF),
    ("rsib", (2, 2, 64, WIDTH), BF),
    ("rz", (3, 64, WIDTH), BF),
    ("m_r2", (2, 2, 4, 32, 2304), BF),
    ("m_r1", (2, 2, 4, 2, 32, 2304), BF),
    ("m_q2", (2, 2, 1, 32, 2304), BF),
    ("m_q1", (2, 2, 1, 2, 32, 2304), BF),
    ("k_r2", (2, 2, 4, 128, 256), BF),
    ("k_r1", (2, 2, 4, 2, 128, 256), BF),
    ("k_q2", (2, 2, 1, 128, 256), BF),
    ("k_q1", (2, 2, 1, 2, 128, 256), BF),
    ("ob", (2, 64, WIDTH), BF),
    ("ib", (2, 64, WIDTH), BF),
    ("sums", (4, 40, 128), F32),
    ("came", (13, 40, 128), F32),
]
COPIES, SENDS = 160, 80


def kernel(*refs):
    names = INPUTS + [o[0] for o in OUTPUTS] + [v[0] for v in SCRATCH] + ["send", "recv", "free", "put"]
    body(SimpleNamespace(**dict(zip(names, refs))))


def finish(out, grad_in, gain, fm, fa, gt, *to):
    to[0][...] = out[...].reshape(128, WIDTH)
    to[1][...] = grad_in[...].reshape(128, WIDTH)
    place = lax.axis_index("seq")
    for at, first in ((2, 0), (10, 16)):
        v = gain[pl.ds(first + lax.div(place, 4), 1), :]
        to[at][...] = pltpu.roll(v, lax.rem(128 - lax.rem(place, 4) * 32, 128), 1)[:, 0:32]
    to[7][...] = gain[32:33, :]
    to[8][...] = gain[33:34, :]
    ours = lax.div(place, 32) * 2 + lax.rem(place, 2)
    for i in range(4):
        wide = slice(i * 256, (i + 1) * 256)
        low = slice(i * 128, (i + 1) * 128)
        to[9][:, wide] = fa[i, :, 0:256].astype(F32)
        to[3][:, wide] = fa[i, :, 256:512].astype(F32)
        to[4][:, low] = fa[i, :, 512:640].astype(F32)
        to[5][:, low] = fa[i, :, 640:768].astype(F32)
        tile = pltpu.roll(gt[i].astype(F32), lax.rem(128 - ours * 32, 128), 1)
        to[6][2 * i : 2 * i + 2, :] = tile[0:2, 0:32]
        for k in range(3):
            cols = slice(k * 768, (k + 1) * 768)
            to[11 + k][:, i * 768 : (i + 1) * 768] = fm[i, :, cols].astype(F32)


def rope_tables():
    inverse = ROPE_BASE ** (-np.arange(HEAD // 2) * 2.0 / HEAD)
    inverse = np.concatenate([inverse, inverse]).astype(np.float32).astype(np.float64)
    rows = np.arange(128)[:, None] * inverse
    blocks = np.arange(64)[:, None] * 128 * inverse
    return [jnp.asarray(f(a), F32) for a in (rows, blocks) for f in (np.cos, np.sin)]


def per_device(
    inputs,
    attention_gain,
    query_weight,
    key_matrix,
    value_matrix,
    gate_weight,
    query_gain,
    key_gain,
    out_weight,
    feed_gain,
    feed_gate,
    feed_up,
    feed_down,
    cotangent,
):
    vmem = pl.BlockSpec(memory_space=pltpu.VMEM)
    out = pl.pallas_call(
        kernel,
        out_shape=[jax.ShapeDtypeStruct(shape, kind) for _, shape, kind in OUTPUTS],
        in_specs=[vmem] * len(INPUTS),
        out_specs=[pl.BlockSpec(memory_space=pl.ANY)] * len(OUTPUTS),
        scratch_shapes=[pltpu.VMEM(shape, kind) for _, shape, kind in SCRATCH]
        + [pltpu.SemaphoreType.DMA((SENDS,)), pltpu.SemaphoreType.DMA((COPIES,))]
        + [pltpu.SemaphoreType.REGULAR((3,)), pltpu.SemaphoreType.DMA((6,))],
        compiler_params=pltpu.CompilerParams(
            collective_id=0, has_side_effects=True, vmem_limit_bytes=63 * 2**20
        ),
        name="block",
    )(
        inputs,
        cotangent,
        attention_gain.reshape(1, WIDTH),
        query_gain.reshape(1, HEAD),
        key_gain.reshape(1, HEAD),
        feed_gain.reshape(1, WIDTH),
        query_weight,
        key_matrix,
        value_matrix,
        gate_weight.T,
        out_weight.T,
        feed_gate,
        feed_up,
        feed_down.T,
        *rope_tables(),
    )
    out = pl.pallas_call(
        finish,
        out_shape=[jax.ShapeDtypeStruct(shape, kind) for shape, kind in RESULTS],
        compiler_params=pltpu.CompilerParams(vmem_limit_bytes=60 * 2**20),
        name="results",
    )(*out)
    out = list(out)
    for i in (2, 7, 8, 10):
        out[i] = out[i].reshape(-1)
    for i in (6, 9, 13):
        out[i] = out[i].T
    return tuple(out)


def solution(mesh):
    seq, both, turned = P("seq", None), P("seq", "grp"), P("grp", "seq")
    in_specs = (seq, P(), both, both, both, both, P(), P(), turned, P(), both, both, turned, seq)
    out_specs = (
        seq, seq, P("seq"), both, both, both, both, P(), P(), turned, P("seq"), both, both, turned,
    )
    return jax.shard_map(
        per_device, mesh=mesh, in_specs=in_specs, out_specs=out_specs, check_vma=False
    )
```
